32 devices in a mesh: clip: 8 (over z, x), frame: 4 (over y, core).
Axes of the slice: x: 2, y: 2, z: 4, core: 2. Of those that a mesh axis runs over, the one named last changes fastest.
Arguments:
- tokens: bfloat16 [2, 8, 1024, 768], P(None, 'clip', 'frame'), may hold values from -30 to 30
- counts: int32 [2, 8, 16], P(None, 'clip', 'frame'), may hold values from 16 to 64, as said below
- first_gain: bfloat16 [768], replicated, may hold values from 0.5 to 1.5
- first_bias: bfloat16 [768], replicated, may hold values from -3 to 3
- input_weight: bfloat16 [768, 2304], replicated, may hold values from -0.21875 to 0.21875
- input_bias: bfloat16 [2, 768], replicated, may hold values from -3 to 3
- output_weight: bfloat16 [768, 768], replicated, may hold values from -6 to 6
- output_bias: bfloat16 [768], replicated, may hold values from -3 to 3
- second_gain: bfloat16 [768], replicated, may hold values from 0.5 to 1.5
- second_bias: bfloat16 [768], replicated, may hold values from -3 to 3
- expand_weight: bfloat16 [768, 3072], replicated, may hold values from -0.21875 to 0.21875
- expand_bias: bfloat16 [3072], replicated, may hold values from -3 to 3
- reduce_weight: bfloat16 [3072, 768], replicated, may hold values from -0.109375 to 0.109375
- reduce_bias: bfloat16 [768], replicated, may hold values from -3 to 3
- cotangent: bfloat16 [2, 8, 1024, 768], P(None, 'clip', 'frame'), may hold values from -6 to 6
Outputs:
- layer_out: bfloat16 [2, 8, 1024, 768], P(None, 'clip', 'frame')
- grad_tokens: float32 [2, 8, 1024, 768], P(None, 'clip', 'frame')
- grad_first_gain: float32 [768], P('frame')
- grad_first_bias: float32 [768], P('frame')
- grad_input_weight: float32 [768, 2304], P('frame')
- grad_input_bias: float32 [2, 768], P(None, 'frame')
- grad_output_weight: float32 [768, 768], P('frame')
- grad_output_bias: float32 [768], P('frame')
- grad_second_gain: float32 [768], P('frame')
- grad_second_bias: float32 [768], P('frame')
- grad_expand_weight: float32 [768, 3072], P('frame')
- grad_expand_bias: float32 [3072], P('frame')
- grad_reduce_weight: float32 [3072, 768], P('frame')
- grad_reduce_bias: float32 [768], P('frame')
The draws below stay inside these ranges and needn't reach their ends.
Inputs may be any that keep to these rules, and one draw needn't show every extreme that they name: `counts`: slot s of a frame holds a kept patch when s < that frame's count; the later slots are padding.
All inputs are finite; a program needn't handle non-finite values.
Results may differ from the reference program's by a relative error of at most 0.02.
Values may be sent and summed in bfloat16 or wider, within the bound.
A program may use at most 128 MiB of HBM per device.

```python
import math
import jax
import jax.numpy as jnp
from jax import lax

D = 768
H = 12
HD = 64
FF = 3072
MICRO = 2
SLOTS = 64
SEQ = 1024
FRAMES = 16
GROUPS = 8


def draw_tokens(key, part):
    key = jax.random.fold_in(key, 11)
    base_key, scale_key = jax.random.split(key, 2)
    shape = (MICRO, GROUPS, SEQ, D)
    base = jnp.clip(jax.random.normal(base_key, shape, jnp.float32), -6.0, 6.0)
    scale = jnp.exp(jax.random.uniform(scale_key, (MICRO, GROUPS, SEQ, 1), jnp.float32, math.log(0.5), math.log(5.0)))
    return (base * scale).astype(jnp.bfloat16)


def draw_counts(key, part):
    key = jax.random.fold_in(key, 23)
    base_key, high_key, offset_key = jax.random.split(key, 3)
    least = max(1, SLOTS // 4)
    base = jax.random.randint(base_key, (MICRO, GROUPS, FRAMES), least, SLOTS + 1)
    high_pick = jax.random.randint(high_key, (MICRO, GROUPS, 1), 0, FRAMES)
    offset = jax.random.randint(offset_key, (MICRO, GROUPS, 1), 1, FRAMES)
    low_pick = (high_pick + offset) % FRAMES
    index = jnp.arange(FRAMES, dtype=jnp.int32)[None, None, :]
    base = jnp.where(index == high_pick, SLOTS, base)
    base = jnp.where(index == low_pick, least, base)
    return base.astype(jnp.int32)


def level_of(stream_key, dims, pieces, smallest, high):
    def one(axis_at, shards_of):
        heights = jax.random.uniform(jax.random.fold_in(jax.random.fold_in(stream_key, 6), axis_at), (shards_of,), jnp.float32, smallest / len(pieces), high / len(pieces))
        return jnp.repeat(jnp.exp(heights), dims[axis_at] // shards_of).reshape((-1,) + (1,) * (len(dims) - axis_at - 1))

    level = one(*pieces[0])
    for cut in pieces[1:]:
        level = level * one(*cut)
    return level


def scatter_about(key, dims, scale, most, cuts=(), kind=jnp.bfloat16):
    entries = scale * jax.random.normal(key, dims, jnp.float32)
    if cuts:
        entries = entries * level_of(key, dims, cuts, -0.22, 0.18)
    return jnp.clip(entries, -most, most).astype(kind)


def setup_inputs(seed: int = 0) -> dict:
    streams_of = jax.random.split(jax.random.key(seed), 16)
    tokens = draw_tokens(jax.random.fold_in(streams_of[15], 71), 0)
    counts = draw_counts(jax.random.fold_in(streams_of[15], 71), 0)
    first_gain = jnp.clip(1.0 + 0.1 * jax.random.normal(streams_of[2], (D,), jnp.float32), 0.5, 1.5).astype(jnp.bfloat16)
    first_bias = scatter_about(streams_of[3], (D,), 0.3, 3.0)
    input_weight = scatter_about(streams_of[4], (D, 3 * D), D ** -0.5, 0.21875)
    input_bias = scatter_about(streams_of[5], (2, D), 0.3, 3.0)
    output_weight = scatter_about(streams_of[6], (D, D), 1.0, 6.0)
    output_bias = scatter_about(streams_of[7], (D,), 0.3, 3.0)
    second_gain = jnp.clip(1.0 + 0.1 * jax.random.normal(streams_of[8], (D,), jnp.float32), 0.5, 1.5).astype(jnp.bfloat16)
    second_bias = scatter_about(streams_of[9], (D,), 0.3, 3.0)
    expand_weight = scatter_about(streams_of[10], (D, FF), D ** -0.5, 0.21875)
    expand_bias = scatter_about(streams_of[11], (FF,), 0.3, 3.0)
    reduce_weight = scatter_about(streams_of[12], (FF, D), FF ** -0.5, 0.109375)
    reduce_bias = scatter_about(streams_of[13], (D,), 0.3, 3.0)
    cotangent = scatter_about(streams_of[14], (MICRO, GROUPS, SEQ, D), 1.0, 6.0, ((1, 8), (2, 4)))
    return dict(tokens=tokens, counts=counts, first_gain=first_gain, first_bias=first_bias, input_weight=input_weight, input_bias=input_bias, output_weight=output_weight, output_bias=output_bias, second_gain=second_gain, second_bias=second_bias, expand_weight=expand_weight, expand_bias=expand_bias, reduce_weight=reduce_weight, reduce_bias=reduce_bias, cotangent=cotangent)


@jax.custom_vjp
def low(v):
    return lax.optimization_barrier(v.astype(jnp.bfloat16)).astype(jnp.float32)

@jax.custom_vjp
def low_back(v):
    return v

def low_keep(v):
    return (low(v), None)

def low_pass(kept, grad):
    return (grad,)

def back_keep(v):
    return (v, None)

def back_low(kept, grad):
    return (low(grad),)
low.defvjp(low_keep, low_pass)
low_back.defvjp(back_keep, back_low)
epsilon = 1e-06

def product(left, right):
    return jnp.dot(left, right, precision=lax.Precision.HIGHEST, preferred_element_type=jnp.float32)

def norm_rows(values, gain, shift):
    mean = lax.optimization_barrier(jnp.mean(values, axis=-1, keepdims=True))
    centred = values - mean
    spread = lax.optimization_barrier(jnp.mean(centred * centred, axis=-1, keepdims=True))
    return centred * lax.rsqrt(spread + epsilon) * gain + shift

def attend_block(query, keys, values, valid):
    query_heads = query.reshape(-1, H, HD)
    key_heads = keys.reshape(-1, H, HD)
    value_heads = values.reshape(-1, H, HD)
    scores = jnp.einsum('qhd,khd->hqk', query_heads, key_heads, precision=lax.Precision.HIGHEST)
    scores = low_back(scores)
    scores = jnp.where(valid[None, None, :], scores, -1e+30)
    top = lax.optimization_barrier(jnp.max(scores, axis=-1, keepdims=True))
    lifted = jnp.exp(scores - top)
    total = lax.optimization_barrier(jnp.sum(lifted, axis=-1, keepdims=True))
    summed = jnp.einsum('hqk,khd->hqd', low(lifted), value_heads, precision=lax.Precision.HIGHEST)
    return jnp.transpose(summed / total, (1, 0, 2)).reshape(-1, D)

def layer(seq_in, valid, params):
    first_gain, first_bias, input_weight, input_bias, output_weight, output_bias, second_gain, second_bias, expand_weight, expand_bias, reduce_weight, reduce_bias = params
    first_low = low(norm_rows(seq_in, first_gain, first_bias))
    projected = product(first_low, input_weight)
    query = low_back(low((projected[:, :D] + input_bias[0]) * 0.125))
    keys = low_back(low(projected[:, D:2 * D]))
    values = low_back(low(projected[:, 2 * D:] + input_bias[1]))
    span = min(512, SEQ)
    blocks = query.reshape(SEQ // span, span, D)
    attended = lax.map(jax.checkpoint(lambda piece: attend_block(piece, keys, values, valid)), blocks)
    attended = low_back(low(attended.reshape(SEQ, D)))
    middle = seq_in + low_back(product(attended, output_weight) + output_bias)
    second_low = low(norm_rows(middle, second_gain, second_bias))
    before = low_back(product(second_low, expand_weight) + expand_bias)
    active = low(jax.nn.gelu(before, approximate=False))
    return middle + low_back(product(active, reduce_weight) + reduce_bias)

def reference(tokens, counts, first_gain, first_bias, input_weight, input_bias, output_weight, output_bias, second_gain, second_bias, expand_weight, expand_bias, reduce_weight, reduce_bias, cotangent):
    sequences = tokens.reshape(MICRO * GROUPS, SEQ, D).astype(jnp.float32)
    upstream = cotangent.reshape(MICRO * GROUPS, SEQ, D).astype(jnp.float32)
    positions = jnp.arange(SEQ, dtype=jnp.int32)
    slot_of = positions % SLOTS
    frame_of = positions // SLOTS
    per_frame = counts.reshape(MICRO * GROUPS, FRAMES)
    valid = slot_of[None, :] < per_frame[:, frame_of]
    params = tuple((item.astype(jnp.float32) for item in (first_gain, first_bias, input_weight, input_bias, output_weight, output_bias, second_gain, second_bias, expand_weight, expand_bias, reduce_weight, reduce_bias)))

    def run_all(seqs, weights):

        def one_clip(carry, item):
            return (carry, layer(item[0], item[1], weights))
        return lax.scan(one_clip, None, (seqs, valid))[1]
    result, pullback = jax.vjp(run_all, sequences, params)
    grad_seq, grads = pullback(upstream)
    layer_out = result.reshape(MICRO, GROUPS, SEQ, D).astype(jnp.bfloat16)
    grad_tokens = grad_seq.reshape(MICRO, GROUPS, SEQ, D)
    return (layer_out, grad_tokens, grads[0], grads[1], grads[2], grads[3], grads[4], grads[5], grads[6], grads[7], grads[8], grads[9], grads[10], grads[11])
```

```python
import functools
import jax
import jax.numpy as jnp
from jax import lax
from jax.experimental import pallas as pl
from jax.experimental.pallas import tpu as pltpu
from jax.sharding import PartitionSpec as P

D = 768
H = 12
HD = 64
MICRO = 2
FRAME_DEV = 4
SLOTS = 64
BLOCK = 256


epsilon = 1e-06


def from_behind(block, axis, distance):
    devices = range(lax.axis_size(axis))
    route = [((i - distance) % len(devices), i) for i in devices]
    return lax.ppermute(block, axis, route)


def norm_rows(values, gain, shift):
    mean = jnp.mean(values, axis=-1, keepdims=True)
    centred = values - mean
    spread = jnp.mean(centred * centred, axis=-1, keepdims=True)
    return centred * lax.rsqrt(spread + epsilon) * gain + shift


def gelu_exact(values):
    return jax.nn.gelu(values, approximate=False)


def key_valid(every_count, source):
    frame_counts = lax.dynamic_slice_in_dim(every_count, source * FRAME_DEV, FRAME_DEV, 1)
    slot_index = jnp.arange(SLOTS, dtype=jnp.int32)
    return (slot_index[None, None, :] < frame_counts[:, :, None]).reshape(MICRO, BLOCK)


def scores_of(query, keys, valid):
    key_heads = keys.reshape(MICRO, BLOCK, H, HD)
    scores = jnp.einsum("mqhd,mkhd->mhqk", query, key_heads, preferred_element_type=jnp.float32)
    return jnp.where(valid[:, None, None, :], scores, -1e30)


def absorb(state, query, keys, values, valid):
    top, total, summed = state
    scores = scores_of(query, keys, valid)
    new_top = jnp.maximum(top, jnp.max(scores, axis=-1, keepdims=True))
    factor = jnp.exp(top - new_top)
    lifted = jnp.exp(scores - new_top)
    total = total * factor + jnp.sum(lifted, axis=-1, keepdims=True)
    value_heads = values.reshape(MICRO, BLOCK, H, HD)
    summed = summed * factor + jnp.einsum(
        "mhqk,mkhd->mhqd",
        lifted.astype(jnp.bfloat16),
        value_heads,
        preferred_element_type=jnp.float32,
    )
    return (new_top, total, summed)


def block_back(query, keys, values, valid, log_total, delta, grad_heads):
    scores = scores_of(query, keys, valid)
    weights = jnp.exp(scores - log_total)
    key_heads = keys.reshape(MICRO, BLOCK, H, HD)
    value_heads = values.reshape(MICRO, BLOCK, H, HD)
    grad_weights = jnp.einsum(
        "mqhd,mkhd->mhqk", grad_heads, value_heads, preferred_element_type=jnp.float32
    )
    grad_scores = (weights * (grad_weights - delta)).astype(jnp.bfloat16)
    grad_query = jnp.einsum(
        "mhqk,mkhd->mqhd", grad_scores, key_heads, preferred_element_type=jnp.float32
    )
    grad_keys = jnp.einsum(
        "mhqk,mqhd->mkhd", grad_scores, query, preferred_element_type=jnp.float32
    )
    grad_values = jnp.einsum(
        "mhqk,mqhd->mkhd",
        weights.astype(jnp.bfloat16),
        grad_heads,
        preferred_element_type=jnp.float32,
    )
    return (grad_query, grad_keys.reshape(MICRO, BLOCK, D), grad_values.reshape(MICRO, BLOCK, D))


MESH = pl.DeviceIdType.MESH
K = 36
QR = 384
HR = 192


class Place:
    def __init__(self):
        self.clip = lax.axis_index("clip")
        self.frame = lax.axis_index("frame")
        self.x = lax.rem(self.clip, 2)
        self.z = self.clip // 2
        self.core = lax.rem(self.frame, 2)
        self.y = self.frame // 2
        self.outer = jnp.logical_or(self.z == 0, self.z == 3)
        self.inner = jnp.logical_not(self.outer)
        self.to_core = (self.clip, self.y * 2 + (1 - self.core))
        self.to_y = (self.clip, (1 - self.y) * 2 + self.core)
        self.to_x = (self.z * 2 + (1 - self.x), self.frame)
        mate = self.z + 1 - 2 * lax.rem(self.z, 2)
        self.to_mate = (mate * 2 + self.x, self.frame)
        self.to_inner = ((3 - self.z) * 2 + self.x, self.frame)


def enter(place):
    barrier = pltpu.get_barrier_semaphore()
    for peer in (place.to_core, place.to_y, place.to_x, place.to_mate):
        pl.semaphore_signal(barrier, inc=1, device_id=peer, device_id_type=MESH)

    @pl.when(place.inner)
    def _():
        pl.semaphore_signal(barrier, inc=1, device_id=place.to_inner, device_id_type=MESH)

    pl.semaphore_wait(barrier, jnp.where(place.inner, 5, 4))


class Reduce:
    def __init__(self, place, bufs, send, recv):
        self.p = place
        self.own, self.nbr, self.rc, self.ry, self.rx, self.r1, self.r2, self.ra = bufs
        self.send, self.recv = send, recv

    def copy(self, src, dst, stage, k, peer):
        return pltpu.make_async_remote_copy(
            src_ref=src,
            dst_ref=dst,
            send_sem=self.send.at[stage, k],
            recv_sem=self.recv.at[stage, k],
            device_id=peer,
            device_id_type=MESH,
        )

    def half(self, k):
        return self.own.at[k, self.p.y, pl.ds(pl.multiple_of(self.p.x * HR, HR), HR)]

    def far_half(self, k):
        start = pl.multiple_of((1 - self.p.x) * HR, HR)
        return self.own.at[k, self.p.y, pl.ds(start, HR)]

    def c_core(self, k):
        return self.copy(self.nbr.at[k], self.rc.at[k], 0, k, self.p.to_core)

    def c_y(self, k):
        return self.copy(self.own.at[k, 1 - self.p.y], self.ry.at[k], 1, k, self.p.to_y)

    def c_x(self, k):
        return self.copy(self.far_half(k), self.rx.at[k], 2, k, self.p.to_x)

    def c_in(self, k):
        return self.copy(self.half(k), self.r1.at[k], 3, k, self.p.to_mate)

    def c_mid(self, k):
        return self.copy(self.half(k), self.r2.at[k], 4, k, self.p.to_inner)

    def c_out(self, k):
        return self.copy(self.r2.at[k], self.r1.at[k], 3, k, self.p.to_mate)

    def c_gather(self, k, inner):
        src = self.r2 if inner else self.r1
        return self.copy(src.at[k], self.ra.at[k], 5, k, self.p.to_x)

    def begin(self, k):
        self.c_core(k).start()

    def stage_core(self, k):
        self.c_core(k).wait_recv()
        self.own[k] = self.own[k] + self.rc[k]
        self.c_y(k).start()

    def stage_y(self, k):
        self.c_y(k).wait_recv()
        self.own[k, self.p.y] = self.own[k, self.p.y] + self.ry[k]
        self.c_x(k).start()

    def stage_x(self, k):
        self.c_x(k).wait_recv()
        half = self.half(k)
        half[...] = half[...] + self.rx[k]

        @pl.when(self.p.outer)
        def _():
            self.c_in(k).start()

    def stage_in(self, k):
        @pl.when(self.p.inner)
        def _():
            self.c_in(k).wait_recv()
            half = self.half(k)
            half[...] = half[...] + self.r1[k]
            self.c_mid(k).start()

    def stage_mid(self, k):
        @pl.when(self.p.inner)
        def _():
            self.c_mid(k).wait_recv()
            self.r2[k] = self.r2[k] + self.half(k)[...]
            self.c_out(k).start()
            self.c_gather(k, True).start()

    def stage_out(self, k):
        @pl.when(self.p.outer)
        def _():
            self.c_in(k).wait_recv()
            self.c_gather(k, False).start()

    def stage_done(self, k):
        self.c_gather(k, True).wait_recv()
        self.c_core(k).wait_send()
        self.c_y(k).wait_send()
        self.c_x(k).wait_send()
        self.c_in(k).wait_send()
        self.c_gather(k, True).wait_send()

        @pl.when(self.p.inner)
        def _():
            self.c_mid(k).wait_send()

        mine = jnp.where(self.p.outer, self.r1[k], self.r2[k]).astype(jnp.float32)
        theirs = self.ra[k].astype(jnp.float32)
        first = self.p.x == 0
        return jnp.where(first, mine, theirs), jnp.where(first, theirs, mine)


LAGS = (0, 2, 4, 5, 6, 7, 9)


def reduce_kernel(own_ref, nbr_ref, out_ref, own, nbr, rc, ry, rx, r1, r2, ra, stage, send, recv, lsem, osem):
    place = Place()
    enter(place)
    red = Reduce(place, (own, nbr, rc, ry, rx, r1, r2, ra), send, recv)

    def load(k):
        return (
            pltpu.make_async_copy(own_ref.at[k], own.at[k], lsem.at[0, k]),
            pltpu.make_async_copy(nbr_ref.at[k], nbr.at[k], lsem.at[1, k]),
        )

    def kick(k, _):
        for one in load(k):
            one.start()
        return 0

    lax.fori_loop(0, K, kick, 0)

    def begin(k, _):
        for one in load(k):
            one.wait()
        red.begin(k)
        return 0

    lax.fori_loop(0, K, begin, 0)

    def store(k):
        slot = lax.rem(k, 2)
        return pltpu.make_async_copy(stage.at[slot], out_ref.at[k], osem.at[slot])

    def finish(k):
        @pl.when(k >= 2)
        def _():
            store(k - 2).wait()

        one, two = red.stage_done(k)
        slot = lax.rem(k, 2)
        stage[slot, pl.ds(0, HR)] = one
        stage[slot, pl.ds(HR, HR)] = two
        store(k).start()

    steps = (red.stage_core, red.stage_y, red.stage_x, red.stage_in, red.stage_mid, red.stage_out, finish)

    def tick(t, _):
        for lag, step in zip(LAGS, steps):
            k = t - lag

            @pl.when(jnp.logical_and(k >= 0, k < K))
            def _():
                step(k)

        return 0

    lax.fori_loop(0, K + LAGS[-1], tick, 0)
    store(K - 2).wait()
    store(K - 1).wait()


def reduce_all(own, nbr):
    bf = jnp.bfloat16
    return pl.pallas_call(
        reduce_kernel,
        out_shape=jax.ShapeDtypeStruct((K, QR, 128), jnp.float32),
        in_specs=[pl.BlockSpec(memory_space=pl.ANY)] * 2,
        out_specs=pl.BlockSpec(memory_space=pl.ANY),
        scratch_shapes=[
            pltpu.VMEM((K, 2, QR, 128), bf),
            pltpu.VMEM((K, 2, QR, 128), bf),
            pltpu.VMEM((K, 2, QR, 128), bf),
            pltpu.VMEM((K, QR, 128), bf),
            pltpu.VMEM((K, HR, 128), bf),
            pltpu.VMEM((K, HR, 128), bf),
            pltpu.VMEM((K, HR, 128), bf),
            pltpu.VMEM((K, HR, 128), bf),
            pltpu.VMEM((2, QR, 128), jnp.float32),
            pltpu.SemaphoreType.DMA((6, K)),
            pltpu.SemaphoreType.DMA((6, K)),
            pltpu.SemaphoreType.DMA((2, K)),
            pltpu.SemaphoreType.DMA((2,)),
        ],
        compiler_params=pltpu.CompilerParams(
            collective_id=0, has_side_effects=True, vmem_limit_bytes=60 << 20
        ),
    )(own, nbr)


def pack_wide(grad):
    n = grad.shape[1] // 256
    parts = grad.reshape(4, 192, n, 2, 128)
    return jnp.transpose(parts, (2, 0, 3, 1, 4)).reshape(n, 4, QR, 128)


def unpack_wide(parts):
    n = parts.shape[0]
    return jnp.transpose(parts.reshape(n, 2, 192, 128), (2, 0, 1, 3)).reshape(192, n * 256)


def pack_tall(grad):
    parts = grad.reshape(4, 6, 128, 2, 3, 128)
    return jnp.transpose(parts, (1, 3, 0, 4, 2, 5)).reshape(12, 4, QR, 128)


def unpack_tall(parts):
    parts = parts.reshape(6, 2, 3, 128, 128)
    return jnp.transpose(parts, (0, 3, 1, 2, 4)).reshape(768, 768)


def reduce_weights(in_w, out_w, exp_w, red_w):
    packed = jnp.concatenate(
        [
            pack_tall(red_w.astype(jnp.bfloat16)),
            pack_wide(exp_w.astype(jnp.bfloat16)),
            pack_wide(out_w.astype(jnp.bfloat16)),
            pack_wide(in_w.astype(jnp.bfloat16)),
        ]
    ).reshape(K, 2, 2, QR, 128)
    core = lax.axis_index("frame") % 2
    own = lax.dynamic_index_in_dim(packed, core, 2, keepdims=False)
    nbr = lax.dynamic_index_in_dim(packed, 1 - core, 2, keepdims=False)
    done = reduce_all(own, nbr)
    return (
        unpack_wide(done[27:36]),
        unpack_wide(done[24:27]),
        unpack_wide(done[12:24]),
        unpack_tall(done[0:12]),
    )


def local(
    tokens,
    counts,
    first_gain,
    first_bias,
    input_weight,
    input_bias,
    output_weight,
    output_bias,
    second_gain,
    second_bias,
    expand_weight,
    expand_bias,
    reduce_weight,
    reduce_bias,
    cotangent,
):
    members = lax.axis_size("frame")
    myself = lax.axis_index("frame")
    total_rows = MICRO * BLOCK
    seq_in = tokens.reshape(total_rows, D).astype(jnp.float32)
    every_count = lax.all_gather(counts.reshape(MICRO, FRAME_DEV), "frame", axis=1, tiled=True)
    gain_one = first_gain.astype(jnp.float32)
    shift_one = first_bias.astype(jnp.float32)
    gain_two = second_gain.astype(jnp.float32)
    shift_two = second_bias.astype(jnp.float32)
    qv_bias = input_bias.astype(jnp.float32)
    first_low = norm_rows(seq_in, gain_one, shift_one).astype(jnp.bfloat16)
    projected = jnp.dot(first_low, input_weight, preferred_element_type=jnp.float32)
    query = (
        ((projected[:, :D] + qv_bias[0]) * 0.125).astype(jnp.bfloat16).reshape(MICRO, BLOCK, H, HD)
    )
    keys = projected[:, D : 2 * D].astype(jnp.bfloat16).reshape(MICRO, BLOCK, D)
    values = (projected[:, 2 * D :] + qv_bias[1]).astype(jnp.bfloat16).reshape(MICRO, BLOCK, D)
    start = (
        jnp.full((MICRO, H, BLOCK, 1), -1e30, jnp.float32),
        jnp.zeros((MICRO, H, BLOCK, 1), jnp.float32),
        jnp.zeros((MICRO, H, BLOCK, HD), jnp.float32),
    )
    state = absorb(start, query, keys, values, key_valid(every_count, myself))
    stored = ()

    def forward_hop(step, carry):
        state_now, moving, kept = carry
        moving = from_behind((moving[0], moving[1]), "frame", 1)
        source = (myself - step) % members
        state_now = absorb(state_now, query, moving[0], moving[1], key_valid(every_count, source))
        return (state_now, moving, kept)

    state, _, stored = lax.fori_loop(1, members, forward_hop, (state, (keys, values), stored))
    top, total, summed = state
    log_total = top + jnp.log(total)
    attend_full = jnp.transpose(summed / total, (0, 2, 1, 3))
    attend_low = attend_full.reshape(total_rows, D).astype(jnp.bfloat16)
    middle = (
        seq_in
        + jnp.dot(attend_low, output_weight, preferred_element_type=jnp.float32)
        + output_bias.astype(jnp.float32)
    )
    second_low = norm_rows(middle, gain_two, shift_two).astype(jnp.bfloat16)
    before = jnp.dot(
        second_low, expand_weight, preferred_element_type=jnp.float32
    ) + expand_bias.astype(jnp.float32)
    active_low = gelu_exact(before).astype(jnp.bfloat16)
    result = (
        middle
        + jnp.dot(active_low, reduce_weight, preferred_element_type=jnp.float32)
        + reduce_bias.astype(jnp.float32)
    )
    layer_out = result.astype(jnp.bfloat16).reshape(MICRO, 1, BLOCK, D)
    upstream_low = cotangent.reshape(total_rows, D)
    upstream = upstream_low.astype(jnp.float32)
    grad_reduce_weight = jnp.dot(active_low.T, upstream_low, preferred_element_type=jnp.float32)
    grad_reduce_bias = jnp.sum(upstream, axis=0)
    grad_active = jnp.dot(upstream_low, reduce_weight.T, preferred_element_type=jnp.float32)
    _, gelu_back = jax.vjp(gelu_exact, before)
    grad_before = gelu_back(grad_active)[0].astype(jnp.bfloat16)
    grad_expand_weight = jnp.dot(second_low.T, grad_before, preferred_element_type=jnp.float32)
    grad_expand_bias = jnp.sum(grad_before.astype(jnp.float32), axis=0)
    grad_second = jnp.dot(grad_before, expand_weight.T, preferred_element_type=jnp.float32)
    _, second_back = jax.vjp(norm_rows, middle, gain_two, shift_two)
    middle_part, grad_second_gain, grad_second_bias = second_back(grad_second)
    grad_middle = upstream + middle_part
    grad_branch = grad_middle.astype(jnp.bfloat16)
    grad_output_weight = jnp.dot(attend_low.T, grad_branch, preferred_element_type=jnp.float32)
    grad_output_bias = jnp.sum(grad_branch.astype(jnp.float32), axis=0)
    grad_attend = jnp.dot(grad_branch, output_weight.T, preferred_element_type=jnp.float32).astype(
        jnp.bfloat16
    )
    grad_heads = grad_attend.reshape(MICRO, BLOCK, H, HD)
    delta = jnp.transpose(
        jnp.sum(grad_heads.astype(jnp.float32) * attend_full, axis=-1), (0, 2, 1)
    )[..., None]
    first_terms = block_back(
        query, keys, values, key_valid(every_count, myself), log_total, delta, grad_heads
    )

    def backward_hop(step, carry):
        grad_query, running, moving = carry
        running = (
            from_behind(running[0].astype(jnp.bfloat16), "frame", 1).astype(jnp.float32),
            from_behind(running[1].astype(jnp.bfloat16), "frame", 1).astype(jnp.float32),
        )
        current = from_behind((moving[0], moving[1]), "frame", 1)
        source = (myself - step) % members
        add_query, add_keys, add_values = block_back(
            query,
            current[0],
            current[1],
            key_valid(every_count, source),
            log_total,
            delta,
            grad_heads,
        )
        return (grad_query + add_query, (running[0] + add_keys, running[1] + add_values), current)

    grad_query, running, _ = lax.fori_loop(
        1, members, backward_hop, (first_terms[0], (first_terms[1], first_terms[2]), (keys, values))
    )
    finished = (
        from_behind(running[0].astype(jnp.bfloat16), "frame", 1).astype(jnp.float32),
        from_behind(running[1].astype(jnp.bfloat16), "frame", 1).astype(jnp.float32),
    )
    query_low = grad_query.astype(jnp.bfloat16).reshape(total_rows, D) * 0.125
    keys_low = finished[0].astype(jnp.bfloat16).reshape(total_rows, D)
    values_low = finished[1].astype(jnp.bfloat16).reshape(total_rows, D)
    grad_projected = jnp.concatenate([query_low, keys_low, values_low], axis=1)
    grad_input_weight = jnp.dot(first_low.T, grad_projected, preferred_element_type=jnp.float32)
    grad_input_bias = jnp.stack(
        [
            jnp.sum(query_low.astype(jnp.float32), axis=0),
            jnp.sum(values_low.astype(jnp.float32), axis=0),
        ]
    )
    grad_first = jnp.dot(grad_projected, input_weight.T, preferred_element_type=jnp.float32)
    _, first_back = jax.vjp(norm_rows, seq_in, gain_one, shift_one)
    input_part, grad_first_gain, grad_first_bias = first_back(grad_first)
    grad_tokens = (grad_middle + input_part).reshape(MICRO, 1, BLOCK, D)
    shares = (
        lax.psum_scatter(
            grad_first_gain.astype(jnp.bfloat16), "frame", scatter_dimension=0, tiled=True
        ).astype(jnp.float32),
        lax.psum_scatter(
            grad_first_bias.astype(jnp.bfloat16), "frame", scatter_dimension=0, tiled=True
        ).astype(jnp.float32),
        lax.psum_scatter(
            grad_input_weight.astype(jnp.bfloat16), "frame", scatter_dimension=0, tiled=True
        ).astype(jnp.float32),
        lax.psum_scatter(
            grad_input_bias.astype(jnp.bfloat16), "frame", scatter_dimension=1, tiled=True
        ).astype(jnp.float32),
        lax.psum_scatter(
            grad_output_weight.astype(jnp.bfloat16), "frame", scatter_dimension=0, tiled=True
        ).astype(jnp.float32),
        lax.psum_scatter(
            grad_output_bias.astype(jnp.bfloat16), "frame", scatter_dimension=0, tiled=True
        ).astype(jnp.float32),
        lax.psum_scatter(
            grad_second_gain.astype(jnp.bfloat16), "frame", scatter_dimension=0, tiled=True
        ).astype(jnp.float32),
        lax.psum_scatter(
            grad_second_bias.astype(jnp.bfloat16), "frame", scatter_dimension=0, tiled=True
        ).astype(jnp.float32),
        lax.psum_scatter(
            grad_expand_weight.astype(jnp.bfloat16), "frame", scatter_dimension=0, tiled=True
        ).astype(jnp.float32),
        lax.psum_scatter(
            grad_expand_bias.astype(jnp.bfloat16), "frame", scatter_dimension=0, tiled=True
        ).astype(jnp.float32),
        lax.psum_scatter(
            grad_reduce_weight.astype(jnp.bfloat16), "frame", scatter_dimension=0, tiled=True
        ).astype(jnp.float32),
        lax.psum_scatter(
            grad_reduce_bias.astype(jnp.bfloat16), "frame", scatter_dimension=0, tiled=True
        ).astype(jnp.float32),
    )
    totals = (
        lax.psum(shares[0].astype(jnp.bfloat16), "clip").astype(jnp.float32),
        lax.psum(shares[1].astype(jnp.bfloat16), "clip").astype(jnp.float32),
        lax.psum(shares[2].astype(jnp.bfloat16), "clip").astype(jnp.float32),
        lax.psum(shares[3].astype(jnp.bfloat16), "clip").astype(jnp.float32),
        lax.psum(shares[4].astype(jnp.bfloat16), "clip").astype(jnp.float32),
        lax.psum(shares[5].astype(jnp.bfloat16), "clip").astype(jnp.float32),
        lax.psum(shares[6].astype(jnp.bfloat16), "clip").astype(jnp.float32),
        lax.psum(shares[7].astype(jnp.bfloat16), "clip").astype(jnp.float32),
        lax.psum(shares[8].astype(jnp.bfloat16), "clip").astype(jnp.float32),
        lax.psum(shares[9].astype(jnp.bfloat16), "clip").astype(jnp.float32),
        lax.psum(shares[10].astype(jnp.bfloat16), "clip").astype(jnp.float32),
        lax.psum(shares[11].astype(jnp.bfloat16), "clip").astype(jnp.float32),
    )
    return (
        layer_out,
        grad_tokens,
        totals[0],
        totals[1],
        totals[2],
        totals[3],
        totals[4],
        totals[5],
        totals[6],
        totals[7],
        totals[8],
        totals[9],
        totals[10],
        totals[11],
    )


def local_slice(
    tokens,
    counts,
    first_gain,
    first_bias,
    input_weight,
    input_bias,
    output_weight,
    output_bias,
    second_gain,
    second_bias,
    expand_weight,
    expand_bias,
    reduce_weight,
    reduce_bias,
    cotangent,
):
    members = lax.axis_size("frame")
    myself = lax.axis_index("frame")
    total_rows = MICRO * BLOCK
    seq_in = tokens.reshape(total_rows, D).astype(jnp.float32)
    every_count = lax.all_gather(counts.reshape(MICRO, FRAME_DEV), "frame", axis=1, tiled=True)
    gain_one = first_gain.astype(jnp.float32)
    shift_one = first_bias.astype(jnp.float32)
    gain_two = second_gain.astype(jnp.float32)
    shift_two = second_bias.astype(jnp.float32)
    qv_bias = input_bias.astype(jnp.float32)
    first_low = norm_rows(seq_in, gain_one, shift_one).astype(jnp.bfloat16)
    projected = jnp.dot(first_low, input_weight, preferred_element_type=jnp.float32)
    query = (
        ((projected[:, :D] + qv_bias[0]) * 0.125).astype(jnp.bfloat16).reshape(MICRO, BLOCK, H, HD)
    )
    keys = projected[:, D : 2 * D].astype(jnp.bfloat16).reshape(MICRO, BLOCK, D)
    values = (projected[:, 2 * D :] + qv_bias[1]).astype(jnp.bfloat16).reshape(MICRO, BLOCK, D)
    start = (
        jnp.full((MICRO, H, BLOCK, 1), -1e30, jnp.float32),
        jnp.zeros((MICRO, H, BLOCK, 1), jnp.float32),
        jnp.zeros((MICRO, H, BLOCK, HD), jnp.float32),
    )
    state = absorb(start, query, keys, values, key_valid(every_count, myself))
    stored = ()

    def forward_hop(step, carry):
        state_now, moving, kept = carry
        moving = from_behind((moving[0], moving[1]), "frame", 1)
        source = (myself - step) % members
        state_now = absorb(state_now, query, moving[0], moving[1], key_valid(every_count, source))
        return (state_now, moving, kept)

    state, _, stored = lax.fori_loop(1, members, forward_hop, (state, (keys, values), stored))
    top, total, summed = state
    log_total = top + jnp.log(total)
    attend_full = jnp.transpose(summed / total, (0, 2, 1, 3))
    attend_low = attend_full.reshape(total_rows, D).astype(jnp.bfloat16)
    middle = (
        seq_in
        + jnp.dot(attend_low, output_weight, preferred_element_type=jnp.float32)
        + output_bias.astype(jnp.float32)
    )
    second_low = norm_rows(middle, gain_two, shift_two).astype(jnp.bfloat16)
    before = jnp.dot(
        second_low, expand_weight, preferred_element_type=jnp.float32
    ) + expand_bias.astype(jnp.float32)
    active_low = gelu_exact(before).astype(jnp.bfloat16)
    result = (
        middle
        + jnp.dot(active_low, reduce_weight, preferred_element_type=jnp.float32)
        + reduce_bias.astype(jnp.float32)
    )
    layer_out = result.astype(jnp.bfloat16).reshape(MICRO, 1, BLOCK, D)
    upstream_low = cotangent.reshape(total_rows, D)
    upstream = upstream_low.astype(jnp.float32)
    grad_reduce_weight = jnp.dot(active_low.T, upstream_low, preferred_element_type=jnp.float32)
    grad_reduce_bias = jnp.sum(upstream, axis=0)
    grad_active = jnp.dot(upstream_low, reduce_weight.T, preferred_element_type=jnp.float32)
    _, gelu_back = jax.vjp(gelu_exact, before)
    grad_before = gelu_back(grad_active)[0].astype(jnp.bfloat16)
    grad_expand_weight = jnp.dot(second_low.T, grad_before, preferred_element_type=jnp.float32)
    grad_expand_bias = jnp.sum(grad_before.astype(jnp.float32), axis=0)
    grad_second = jnp.dot(grad_before, expand_weight.T, preferred_element_type=jnp.float32)
    _, second_back = jax.vjp(norm_rows, middle, gain_two, shift_two)
    middle_part, grad_second_gain, grad_second_bias = second_back(grad_second)
    grad_middle = upstream + middle_part
    grad_branch = grad_middle.astype(jnp.bfloat16)
    grad_output_weight = jnp.dot(attend_low.T, grad_branch, preferred_element_type=jnp.float32)
    grad_output_bias = jnp.sum(grad_branch.astype(jnp.float32), axis=0)
    grad_attend = jnp.dot(grad_branch, output_weight.T, preferred_element_type=jnp.float32).astype(
        jnp.bfloat16
    )
    grad_heads = grad_attend.reshape(MICRO, BLOCK, H, HD)
    delta = jnp.transpose(
        jnp.sum(grad_heads.astype(jnp.float32) * attend_full, axis=-1), (0, 2, 1)
    )[..., None]
    first_terms = block_back(
        query, keys, values, key_valid(every_count, myself), log_total, delta, grad_heads
    )

    def backward_hop(step, carry):
        grad_query, running, moving = carry
        running = (
            from_behind(running[0].astype(jnp.bfloat16), "frame", 1).astype(jnp.float32),
            from_behind(running[1].astype(jnp.bfloat16), "frame", 1).astype(jnp.float32),
        )
        current = from_behind((moving[0], moving[1]), "frame", 1)
        source = (myself - step) % members
        add_query, add_keys, add_values = block_back(
            query,
            current[0],
            current[1],
            key_valid(every_count, source),
            log_total,
            delta,
            grad_heads,
        )
        return (grad_query + add_query, (running[0] + add_keys, running[1] + add_values), current)

    grad_query, running, _ = lax.fori_loop(
        1, members, backward_hop, (first_terms[0], (first_terms[1], first_terms[2]), (keys, values))
    )
    finished = (
        from_behind(running[0].astype(jnp.bfloat16), "frame", 1).astype(jnp.float32),
        from_behind(running[1].astype(jnp.bfloat16), "frame", 1).astype(jnp.float32),
    )
    query_low = grad_query.astype(jnp.bfloat16).reshape(total_rows, D) * 0.125
    keys_low = finished[0].astype(jnp.bfloat16).reshape(total_rows, D)
    values_low = finished[1].astype(jnp.bfloat16).reshape(total_rows, D)
    grad_projected = jnp.concatenate([query_low, keys_low, values_low], axis=1)
    grad_input_weight = jnp.dot(first_low.T, grad_projected, preferred_element_type=jnp.float32)
    grad_input_bias = jnp.stack(
        [
            jnp.sum(query_low.astype(jnp.float32), axis=0),
            jnp.sum(values_low.astype(jnp.float32), axis=0),
        ]
    )
    grad_first = jnp.dot(grad_projected, input_weight.T, preferred_element_type=jnp.float32)
    _, first_back = jax.vjp(norm_rows, seq_in, gain_one, shift_one)
    input_part, grad_first_gain, grad_first_bias = first_back(grad_first)
    grad_tokens = (grad_middle + input_part).reshape(MICRO, 1, BLOCK, D)
    shares = (
        lax.psum_scatter(
            grad_first_gain.astype(jnp.bfloat16), "frame", scatter_dimension=0, tiled=True
        ).astype(jnp.float32),
        lax.psum_scatter(
            grad_first_bias.astype(jnp.bfloat16), "frame", scatter_dimension=0, tiled=True
        ).astype(jnp.float32),
        None,
        lax.psum_scatter(
            grad_input_bias.astype(jnp.bfloat16), "frame", scatter_dimension=1, tiled=True
        ).astype(jnp.float32),
        None,
        lax.psum_scatter(
            grad_output_bias.astype(jnp.bfloat16), "frame", scatter_dimension=0, tiled=True
        ).astype(jnp.float32),
        lax.psum_scatter(
            grad_second_gain.astype(jnp.bfloat16), "frame", scatter_dimension=0, tiled=True
        ).astype(jnp.float32),
        lax.psum_scatter(
            grad_second_bias.astype(jnp.bfloat16), "frame", scatter_dimension=0, tiled=True
        ).astype(jnp.float32),
        None,
        lax.psum_scatter(
            grad_expand_bias.astype(jnp.bfloat16), "frame", scatter_dimension=0, tiled=True
        ).astype(jnp.float32),
        None,
        lax.psum_scatter(
            grad_reduce_bias.astype(jnp.bfloat16), "frame", scatter_dimension=0, tiled=True
        ).astype(jnp.float32),
    )
    big = reduce_weights(grad_input_weight, grad_output_weight, grad_expand_weight, grad_reduce_weight)
    totals = (
        lax.psum(shares[0].astype(jnp.bfloat16), "clip").astype(jnp.float32),
        lax.psum(shares[1].astype(jnp.bfloat16), "clip").astype(jnp.float32),
        big[0],
        lax.psum(shares[3].astype(jnp.bfloat16), "clip").astype(jnp.float32),
        big[1],
        lax.psum(shares[5].astype(jnp.bfloat16), "clip").astype(jnp.float32),
        lax.psum(shares[6].astype(jnp.bfloat16), "clip").astype(jnp.float32),
        lax.psum(shares[7].astype(jnp.bfloat16), "clip").astype(jnp.float32),
        big[2],
        lax.psum(shares[9].astype(jnp.bfloat16), "clip").astype(jnp.float32),
        big[3],
        lax.psum(shares[11].astype(jnp.bfloat16), "clip").astype(jnp.float32),
    )
    return (
        layer_out,
        grad_tokens,
        totals[0],
        totals[1],
        totals[2],
        totals[3],
        totals[4],
        totals[5],
        totals[6],
        totals[7],
        totals[8],
        totals[9],
        totals[10],
        totals[11],
    )


def solution(mesh):
    fits = mesh.shape["clip"] == 8 and mesh.shape["frame"] == 4
    return jax.shard_map(
        local_slice if fits else local,
        mesh=mesh,
        in_specs=(
            P(None, "clip", "frame", None),
            P(None, "clip", "frame"),
            P(),
            P(),
            P(),
            P(),
            P(),
            P(),
            P(),
            P(),
            P(),
            P(),
            P(),
            P(),
            P(None, "clip", "frame", None),
        ),
        out_specs=(
            P(None, "clip", "frame", None),
            P(None, "clip", "frame", None),
            P("frame"),
            P("frame"),
            P("frame", None),
            P(None, "frame"),
            P("frame", None),
            P("frame"),
            P("frame"),
            P("frame"),
            P("frame", None),
            P("frame"),
            P("frame", None),
            P("frame"),
        ),
        check_vma=False,
    )
```

```python
import jax
import jax.numpy as jnp
from jax import lax
from jax.experimental import pallas as pl
from jax.experimental.pallas import tpu as pltpu
from jax.sharding import PartitionSpec as P

D = 768
H = 12
HD = 64
MICRO = 2
FRAME_DEV = 4
SLOTS = 64
BLOCK = 256


epsilon = 1e-06


def from_behind(block, axis, distance):
    devices = range(lax.axis_size(axis))
    route = [((i - distance) % len(devices), i) for i in devices]
    return lax.ppermute(block, axis, route)


def norm_rows(values, gain, shift):
    mean = jnp.mean(values, axis=-1, keepdims=True)
    centred = values - mean
    spread = jnp.mean(centred * centred, axis=-1, keepdims=True)
    return centred * lax.rsqrt(spread + epsilon) * gain + shift


def gelu_exact(values):
    return jax.nn.gelu(values, approximate=False)


def key_valid(every_count, source):
    frame_counts = lax.dynamic_slice_in_dim(every_count, source * FRAME_DEV, FRAME_DEV, 1)
    slot_index = jnp.arange(SLOTS, dtype=jnp.int32)
    return (slot_index[None, None, :] < frame_counts[:, :, None]).reshape(MICRO, BLOCK)


def scores_of(query, keys, valid):
    key_heads = keys.reshape(MICRO, BLOCK, H, HD)
    scores = jnp.einsum("mqhd,mkhd->mhqk", query, key_heads, preferred_element_type=jnp.float32)
    return jnp.where(valid[:, None, None, :], scores, -1e30)


def absorb(state, query, keys, values, valid):
    top, total, summed = state
    scores = scores_of(query, keys, valid)
    new_top = jnp.maximum(top, jnp.max(scores, axis=-1, keepdims=True))
    factor = jnp.exp(top - new_top)
    lifted = jnp.exp(scores - new_top)
    total = total * factor + jnp.sum(lifted, axis=-1, keepdims=True)
    value_heads = values.reshape(MICRO, BLOCK, H, HD)
    summed = summed * factor + jnp.einsum(
        "mhqk,mkhd->mhqd",
        lifted.astype(jnp.bfloat16),
        value_heads,
        preferred_element_type=jnp.float32,
    )
    return (new_top, total, summed)


def block_back(query, keys, values, valid, log_total, delta, grad_heads):
    scores = scores_of(query, keys, valid)
    weights = jnp.exp(scores - log_total)
    key_heads = keys.reshape(MICRO, BLOCK, H, HD)
    value_heads = values.reshape(MICRO, BLOCK, H, HD)
    grad_weights = jnp.einsum(
        "mqhd,mkhd->mhqk", grad_heads, value_heads, preferred_element_type=jnp.float32
    )
    grad_scores = (weights * (grad_weights - delta)).astype(jnp.bfloat16)
    grad_query = jnp.einsum(
        "mhqk,mkhd->mqhd", grad_scores, key_heads, preferred_element_type=jnp.float32
    )
    grad_keys = jnp.einsum(
        "mhqk,mqhd->mkhd", grad_scores, query, preferred_element_type=jnp.float32
    )
    grad_values = jnp.einsum(
        "mhqk,mqhd->mkhd",
        weights.astype(jnp.bfloat16),
        grad_heads,
        preferred_element_type=jnp.float32,
    )
    return (grad_query, grad_keys.reshape(MICRO, BLOCK, D), grad_values.reshape(MICRO, BLOCK, D))


def local(
    tokens,
    counts,
    first_gain,
    first_bias,
    input_weight,
    input_bias,
    output_weight,
    output_bias,
    second_gain,
    second_bias,
    expand_weight,
    expand_bias,
    reduce_weight,
    reduce_bias,
    cotangent,
):
    members = lax.axis_size("frame")
    myself = lax.axis_index("frame")
    total_rows = MICRO * BLOCK
    seq_in = tokens.reshape(total_rows, D).astype(jnp.float32)
    every_count = lax.all_gather(counts.reshape(MICRO, FRAME_DEV), "frame", axis=1, tiled=True)
    gain_one = first_gain.astype(jnp.float32)
    shift_one = first_bias.astype(jnp.float32)
    gain_two = second_gain.astype(jnp.float32)
    shift_two = second_bias.astype(jnp.float32)
    qv_bias = input_bias.astype(jnp.float32)
    first_low = norm_rows(seq_in, gain_one, shift_one).astype(jnp.bfloat16)
    projected = jnp.dot(first_low, input_weight, preferred_element_type=jnp.float32)
    query = (
        ((projected[:, :D] + qv_bias[0]) * 0.125).astype(jnp.bfloat16).reshape(MICRO, BLOCK, H, HD)
    )
    keys = projected[:, D : 2 * D].astype(jnp.bfloat16).reshape(MICRO, BLOCK, D)
    values = (projected[:, 2 * D :] + qv_bias[1]).astype(jnp.bfloat16).reshape(MICRO, BLOCK, D)
    start = (
        jnp.full((MICRO, H, BLOCK, 1), -1e30, jnp.float32),
        jnp.zeros((MICRO, H, BLOCK, 1), jnp.float32),
        jnp.zeros((MICRO, H, BLOCK, HD), jnp.float32),
    )
    state = absorb(start, query, keys, values, key_valid(every_count, myself))
    stored = ()

    def forward_hop(step, carry):
        state_now, moving, kept = carry
        moving = from_behind((moving[0], moving[1]), "frame", 1)
        source = (myself - step) % members
        state_now = absorb(state_now, query, moving[0], moving[1], key_valid(every_count, source))
        return (state_now, moving, kept)

    state, _, stored = lax.fori_loop(1, members, forward_hop, (state, (keys, values), stored))
    top, total, summed = state
    log_total = top + jnp.log(total)
    attend_full = jnp.transpose(summed / total, (0, 2, 1, 3))
    attend_low = attend_full.reshape(total_rows, D).astype(jnp.bfloat16)
    middle = (
        seq_in
        + jnp.dot(attend_low, output_weight, preferred_element_type=jnp.float32)
        + output_bias.astype(jnp.float32)
    )
    second_low = norm_rows(middle, gain_two, shift_two).astype(jnp.bfloat16)
    before = jnp.dot(
        second_low, expand_weight, preferred_element_type=jnp.float32
    ) + expand_bias.astype(jnp.float32)
    active_low = gelu_exact(before).astype(jnp.bfloat16)
    result = (
        middle
        + jnp.dot(active_low, reduce_weight, preferred_element_type=jnp.float32)
        + reduce_bias.astype(jnp.float32)
    )
    layer_out = result.astype(jnp.bfloat16).reshape(MICRO, 1, BLOCK, D)
    upstream_low = cotangent.reshape(total_rows, D)
    upstream = upstream_low.astype(jnp.float32)
    grad_reduce_weight = jnp.dot(active_low.T, upstream_low, preferred_element_type=jnp.float32)
    grad_reduce_bias = jnp.sum(upstream, axis=0)
    grad_active = jnp.dot(upstream_low, reduce_weight.T, preferred_element_type=jnp.float32)
    _, gelu_back = jax.vjp(gelu_exact, before)
    grad_before = gelu_back(grad_active)[0].astype(jnp.bfloat16)
    grad_expand_weight = jnp.dot(second_low.T, grad_before, preferred_element_type=jnp.float32)
    grad_expand_bias = jnp.sum(grad_before.astype(jnp.float32), axis=0)
    grad_second = jnp.dot(grad_before, expand_weight.T, preferred_element_type=jnp.float32)
    _, second_back = jax.vjp(norm_rows, middle, gain_two, shift_two)
    middle_part, grad_second_gain, grad_second_bias = second_back(grad_second)
    grad_middle = upstream + middle_part
    grad_branch = grad_middle.astype(jnp.bfloat16)
    grad_output_weight = jnp.dot(attend_low.T, grad_branch, preferred_element_type=jnp.float32)
    grad_output_bias = jnp.sum(grad_branch.astype(jnp.float32), axis=0)
    grad_attend = jnp.dot(grad_branch, output_weight.T, preferred_element_type=jnp.float32).astype(
        jnp.bfloat16
    )
    grad_heads = grad_attend.reshape(MICRO, BLOCK, H, HD)
    delta = jnp.transpose(
        jnp.sum(grad_heads.astype(jnp.float32) * attend_full, axis=-1), (0, 2, 1)
    )[..., None]
    first_terms = block_back(
        query, keys, values, key_valid(every_count, myself), log_total, delta, grad_heads
    )

    def backward_hop(step, carry):
        grad_query, running, moving = carry
        running = (
            from_behind(running[0].astype(jnp.bfloat16), "frame", 1).astype(jnp.float32),
            from_behind(running[1].astype(jnp.bfloat16), "frame", 1).astype(jnp.float32),
        )
        current = from_behind((moving[0], moving[1]), "frame", 1)
        source = (myself - step) % members
        add_query, add_keys, add_values = block_back(
            query,
            current[0],
            current[1],
            key_valid(every_count, source),
            log_total,
            delta,
            grad_heads,
        )
        return (grad_query + add_query, (running[0] + add_keys, running[1] + add_values), current)

    grad_query, running, _ = lax.fori_loop(
        1, members, backward_hop, (first_terms[0], (first_terms[1], first_terms[2]), (keys, values))
    )
    finished = (
        from_behind(running[0].astype(jnp.bfloat16), "frame", 1).astype(jnp.float32),
        from_behind(running[1].astype(jnp.bfloat16), "frame", 1).astype(jnp.float32),
    )
    query_low = grad_query.astype(jnp.bfloat16).reshape(total_rows, D) * 0.125
    keys_low = finished[0].astype(jnp.bfloat16).reshape(total_rows, D)
    values_low = finished[1].astype(jnp.bfloat16).reshape(total_rows, D)
    grad_projected = jnp.concatenate([query_low, keys_low, values_low], axis=1)
    grad_input_weight = jnp.dot(first_low.T, grad_projected, preferred_element_type=jnp.float32)
    grad_input_bias = jnp.stack(
        [
            jnp.sum(query_low.astype(jnp.float32), axis=0),
            jnp.sum(values_low.astype(jnp.float32), axis=0),
        ]
    )
    grad_first = jnp.dot(grad_projected, input_weight.T, preferred_element_type=jnp.float32)
    _, first_back = jax.vjp(norm_rows, seq_in, gain_one, shift_one)
    input_part, grad_first_gain, grad_first_bias = first_back(grad_first)
    grad_tokens = (grad_middle + input_part).reshape(MICRO, 1, BLOCK, D)
    shares = (
        lax.psum_scatter(
            grad_first_gain.astype(jnp.bfloat16), "frame", scatter_dimension=0, tiled=True
        ).astype(jnp.float32),
        lax.psum_scatter(
            grad_first_bias.astype(jnp.bfloat16), "frame", scatter_dimension=0, tiled=True
        ).astype(jnp.float32),
        lax.psum_scatter(
            grad_input_weight.astype(jnp.bfloat16), "frame", scatter_dimension=0, tiled=True
        ).astype(jnp.float32),
        lax.psum_scatter(
            grad_input_bias.astype(jnp.bfloat16), "frame", scatter_dimension=1, tiled=True
        ).astype(jnp.float32),
        lax.psum_scatter(
            grad_output_weight.astype(jnp.bfloat16), "frame", scatter_dimension=0, tiled=True
        ).astype(jnp.float32),
        lax.psum_scatter(
            grad_output_bias.astype(jnp.bfloat16), "frame", scatter_dimension=0, tiled=True
        ).astype(jnp.float32),
        lax.psum_scatter(
            grad_second_gain.astype(jnp.bfloat16), "frame", scatter_dimension=0, tiled=True
        ).astype(jnp.float32),
        lax.psum_scatter(
            grad_second_bias.astype(jnp.bfloat16), "frame", scatter_dimension=0, tiled=True
        ).astype(jnp.float32),
        lax.psum_scatter(
            grad_expand_weight.astype(jnp.bfloat16), "frame", scatter_dimension=0, tiled=True
        ).astype(jnp.float32),
        lax.psum_scatter(
            grad_expand_bias.astype(jnp.bfloat16), "frame", scatter_dimension=0, tiled=True
        ).astype(jnp.float32),
        lax.psum_scatter(
            grad_reduce_weight.astype(jnp.bfloat16), "frame", scatter_dimension=0, tiled=True
        ).astype(jnp.float32),
        lax.psum_scatter(
            grad_reduce_bias.astype(jnp.bfloat16), "frame", scatter_dimension=0, tiled=True
        ).astype(jnp.float32),
    )
    totals = (
        lax.psum(shares[0].astype(jnp.bfloat16), "clip").astype(jnp.float32),
        lax.psum(shares[1].astype(jnp.bfloat16), "clip").astype(jnp.float32),
        lax.psum(shares[2].astype(jnp.bfloat16), "clip").astype(jnp.float32),
        lax.psum(shares[3].astype(jnp.bfloat16), "clip").astype(jnp.float32),
        lax.psum(shares[4].astype(jnp.bfloat16), "clip").astype(jnp.float32),
        lax.psum(shares[5].astype(jnp.bfloat16), "clip").astype(jnp.float32),
        lax.psum(shares[6].astype(jnp.bfloat16), "clip").astype(jnp.float32),
        lax.psum(shares[7].astype(jnp.bfloat16), "clip").astype(jnp.float32),
        lax.psum(shares[8].astype(jnp.bfloat16), "clip").astype(jnp.float32),
        lax.psum(shares[9].astype(jnp.bfloat16), "clip").astype(jnp.float32),
        lax.psum(shares[10].astype(jnp.bfloat16), "clip").astype(jnp.float32),
        lax.psum(shares[11].astype(jnp.bfloat16), "clip").astype(jnp.float32),
    )
    return (
        layer_out,
        grad_tokens,
        totals[0],
        totals[1],
        totals[2],
        totals[3],
        totals[4],
        totals[5],
        totals[6],
        totals[7],
        totals[8],
        totals[9],
        totals[10],
        totals[11],
    )


MESH = pl.DeviceIdType.MESH
BF = jnp.bfloat16
F32 = jnp.float32
K = 36
QR = 384
HR = 192
SLOT_COUNT = 8
ROWS = 512
PART = 256
FF = 3072
LOW = -1e30
LAGS = (0, 2, 4, 5, 6, 7, 9)


def dot_nn(a, b):
    return lax.dot_general(a, b, (((1,), (0,)), ((), ())), preferred_element_type=F32)


def dot_nt(a, b):
    return lax.dot_general(a, b, (((1,), (1,)), ((), ())), preferred_element_type=F32)


def dot_tn(a, b):
    return lax.dot_general(a, b, (((0,), (0,)), ((), ())), preferred_element_type=F32)


def at128(index):
    return pl.ds(pl.multiple_of(index, 128), 128)


def at256(index):
    return pl.ds(pl.multiple_of(index, 256), 256)


def loop(low, high, body):
    def step(i, carry):
        body(i)
        return carry

    lax.fori_loop(low, high, step, 0)


class Place:
    def __init__(self):
        self.clip = lax.axis_index("clip")
        self.frame = lax.axis_index("frame")
        self.x = lax.rem(self.clip, 2)
        self.z = self.clip // 2
        self.core = lax.rem(self.frame, 2)
        self.y = self.frame // 2
        self.outer = jnp.logical_or(self.z == 0, self.z == 3)
        self.inner = jnp.logical_not(self.outer)
        self.to_core = (self.clip, self.y * 2 + (1 - self.core))
        self.to_y = (self.clip, (1 - self.y) * 2 + self.core)
        self.to_x = (self.z * 2 + (1 - self.x), self.frame)
        mate = self.z + 1 - 2 * lax.rem(self.z, 2)
        self.to_mate = (mate * 2 + self.x, self.frame)
        self.to_inner = ((3 - self.z) * 2 + self.x, self.frame)

    def seat(self, quarter):
        yy, cc = quarter // 2, quarter % 2
        return yy + 2 * (self.core if cc == 0 else 1 - self.core)


def enter(place):
    barrier = pltpu.get_barrier_semaphore()
    for peer in (place.to_core, place.to_y, place.to_x, place.to_mate):
        pl.semaphore_signal(barrier, inc=1, device_id=peer, device_id_type=MESH)

    @pl.when(place.inner)
    def _():
        pl.semaphore_signal(barrier, inc=1, device_id=place.to_inner, device_id_type=MESH)

    pl.semaphore_wait(barrier, jnp.where(place.inner, 5, 4))


def remote(src, dst, send, recv, peer):
    return pltpu.make_async_remote_copy(
        src_ref=src, dst_ref=dst, send_sem=send, recv_sem=recv, device_id=peer, device_id_type=MESH
    )


class Reduce:
    def __init__(self, place, bufs, tot, send, recv, tsem):
        self.p = place
        self.own, self.nbr, self.rc, self.ry, self.rx, self.r1, self.r2 = bufs
        self.tot, self.send, self.recv, self.tsem = tot, send, recv, tsem

    def copy(self, src, dst, stage, k, peer):
        return remote(src, dst, self.send.at[stage, k], self.recv.at[stage, k], peer)

    def my_half(self):
        return pl.ds(pl.multiple_of(self.p.x * HR, HR), HR)

    def half(self, k):
        return self.own.at[k, self.p.y, self.my_half()]

    def c_core(self, k):
        return self.copy(self.nbr.at[lax.rem(k, SLOT_COUNT)], self.rc.at[k], 0, k, self.p.to_core)

    def c_y(self, k):
        return self.copy(self.own.at[k, 1 - self.p.y], self.ry.at[k], 1, k, self.p.to_y)

    def c_x(self, k):
        start = pl.multiple_of((1 - self.p.x) * HR, HR)
        far = self.own.at[k, self.p.y, pl.ds(start, HR)]
        return self.copy(far, self.rx.at[k], 2, k, self.p.to_x)

    def c_in(self, k):
        return self.copy(self.half(k), self.r1.at[k], 3, k, self.p.to_mate)

    def c_mid(self, k):
        return self.copy(self.half(k), self.r2.at[k], 4, k, self.p.to_inner)

    def c_out(self, k):
        return self.copy(self.r2.at[k], self.r1.at[k], 3, k, self.p.to_mate)

    def c_gather(self, k, inner):
        src = self.r2 if inner else self.r1
        return self.copy(src.at[k], self.tot.at[k, self.my_half()], 5, k, self.p.to_x)

    def c_keep(self, k, inner):
        src = self.r2 if inner else self.r1
        return pltpu.make_async_copy(src.at[k], self.tot.at[k, self.my_half()], self.tsem.at[k])

    def slot(self, k):
        @pl.when(k >= SLOT_COUNT)
        def _():
            self.c_core(k - SLOT_COUNT).wait_send()

        return lax.rem(k, SLOT_COUNT)

    def emit_wide(self, k, grad):
        slot = self.slot(k)
        for yy in range(2):
            for side in range(2):
                rows = slice(side * HR, (side + 1) * HR)
                cols = slice(side * 128, (side + 1) * 128)
                self.own[k, yy, rows] = grad[yy * HR : (yy + 1) * HR, cols]
                self.nbr[slot, yy, rows] = grad[QR + yy * HR : QR + (yy + 1) * HR, cols]
        self.c_core(k).start()

    def emit_tall(self, k, grad, first):
        slot = self.slot(k)
        for yy in range(2):
            for i in range(3):
                rows = slice(i * 128, (i + 1) * 128)
                cols = slice(first + i * 128, first + (i + 1) * 128)
                self.own[k, yy, rows] = grad[yy * 128 : (yy + 1) * 128, cols]
                self.nbr[slot, yy, rows] = grad[256 + yy * 128 : 256 + (yy + 1) * 128, cols]
        self.c_core(k).start()

    def stage_core(self, k):
        self.c_core(k).wait_recv()
        self.own[k] = self.own[k] + self.rc[k]
        self.c_y(k).start()

    def stage_y(self, k):
        self.c_y(k).wait_recv()
        self.own[k, self.p.y] = self.own[k, self.p.y] + self.ry[k]
        self.c_x(k).start()

    def stage_x(self, k):
        self.c_x(k).wait_recv()
        half = self.half(k)
        half[...] = half[...] + self.rx[k]

        @pl.when(self.p.outer)
        def _():
            self.c_in(k).start()

    def stage_in(self, k):
        @pl.when(self.p.inner)
        def _():
            self.c_in(k).wait_recv()
            half = self.half(k)
            half[...] = half[...] + self.r1[k]
            self.c_mid(k).start()

    def stage_mid(self, k):
        @pl.when(self.p.inner)
        def _():
            self.c_mid(k).wait_recv()
            self.r2[k] = self.r2[k] + self.half(k)[...]
            self.c_out(k).start()
            self.c_gather(k, True).start()
            self.c_keep(k, True).start()

    def stage_out(self, k):
        @pl.when(self.p.outer)
        def _():
            self.c_in(k).wait_recv()
            self.c_gather(k, False).start()
            self.c_keep(k, False).start()

    def stage_done(self, k):
        self.c_gather(k, True).wait_recv()
        self.c_y(k).wait_send()
        self.c_x(k).wait_send()
        self.c_in(k).wait_send()
        self.c_gather(k, True).wait_send()
        self.c_keep(k, True).wait()

        @pl.when(k >= K - SLOT_COUNT)
        def _():
            self.c_core(k).wait_send()

        @pl.when(self.p.inner)
        def _():
            self.c_mid(k).wait_send()

    def tick(self, t):
        stages = (
            self.stage_core,
            self.stage_y,
            self.stage_x,
            self.stage_in,
            self.stage_mid,
            self.stage_out,
            self.stage_done,
        )
        for lag, stage in zip(LAGS, stages):
            k = t - lag
            if isinstance(k, int):
                if 0 <= k < K:
                    stage(k)
            else:

                @pl.when(jnp.logical_and(k >= 0, k < K))
                def _(stage=stage, k=k):
                    stage(k)


def norm_parts(values):
    mean = jnp.mean(values, axis=-1, keepdims=True)
    centred = values - mean
    spread = jnp.mean(centred * centred, axis=-1, keepdims=True)
    scale = lax.rsqrt(spread + epsilon)
    return centred * scale, scale


def norm_back(hat, scale, gain, grad):
    lifted = grad * gain
    level = jnp.mean(lifted, axis=-1, keepdims=True)
    slope = jnp.mean(lifted * hat, axis=-1, keepdims=True)
    return scale * (lifted - level - hat * slope)


def three_parts(values):
    high = values.astype(BF).astype(F32)
    rest = values - high
    middle = rest.astype(BF).astype(F32)
    return high, middle, rest - middle


def layer_kernel(
    tok_ref, cot_ref, cnt_ref, vec, wi_ref, wo_ref, we_ref, wr_ref,
    tot_ref, vs, lo_ref, gto_ref, gtr_ref,
    own, nbr, rc, ry, rx, r1, r2,
    tokx, dyx, w1, wo, wr, qkv, kvr, rowb, kaug, qaug, att, mid, low2, turned, g_t, du_t, y_sum, h_sum,
    d_out, dp, dkv_own, dkv_send, dkv_recv, lo, gts, vr,
    send, recv, tsem, lsem, xsend, xrecv, ksend, krecv, vsend, vrecv,
):
    p = Place()
    loads = [
        pltpu.make_async_copy(tok_ref.at[p.y, 0], tokx.at[pl.ds(0, PART)], lsem.at[0]),
        pltpu.make_async_copy(wi_ref, w1.at[:, pl.ds(0, 2304)], lsem.at[1]),
        pltpu.make_async_copy(cot_ref.at[p.y, 0], dyx.at[pl.ds(0, PART)], lsem.at[2]),
        pltpu.make_async_copy(wo_ref, wo, lsem.at[3]),
        pltpu.make_async_copy(wr_ref, wr, lsem.at[4]),
    ]
    for one in loads:
        one.start()
    enter(p)
    red = Reduce(p, (own, nbr, rc, ry, rx, r1, r2), tot_ref, send, recv, tsem)

    def swap(index, src, dst, peer):
        return remote(src, dst, xsend.at[index], xrecv.at[index], peer)

    c_tok = swap(0, tok_ref.at[1 - p.y, 0], tokx.at[pl.ds(PART, PART)], p.to_y)
    c_cot = swap(1, cot_ref.at[1 - p.y, 0], dyx.at[pl.ds(PART, PART)], p.to_y)
    c_row = swap(2, rowb.at[2], rowb.at[1], p.to_y)
    c_aug = swap(3, kaug.at[pl.ds(0, ROWS)], kaug.at[pl.ds(ROWS, ROWS)], p.to_core)
    c_kv = [
        swap(4 + r, qkv.at[pl.ds(r * PART, PART), pl.ds(768, 1536)], kvr.at[pl.ds(r * PART, PART)], p.to_core)
        for r in range(2)
    ]
    c_tok.start()

    lane = lax.broadcasted_iota(jnp.int32, (16, PART), 1)

    def bias_row(m):
        frame = lane // SLOTS
        kept = jnp.zeros_like(lane)
        for j in range(FRAME_DEV):
            kept = jnp.where(frame == j, cnt_ref[m, 0, j], kept)
        return jnp.where(lane - frame * SLOTS < kept, 0.0, LOW).astype(BF)

    rowb[0] = bias_row(p.y)
    rowb[2] = bias_row(1 - p.y)
    c_row.start()
    pick = jnp.where(
        jnp.logical_and(
            lax.broadcasted_iota(jnp.int32, (16, 128), 0) == 0,
            lax.broadcasted_iota(jnp.int32, (16, 128), 1) == 0,
        ),
        1.0,
        0.0,
    ).astype(BF)
    kaug[pl.ds(0, PART)] = dot_tn(rowb[0], pick).astype(BF)
    lane_q = lax.broadcasted_iota(jnp.int32, (PART, 128), 1)
    lane_row = lax.broadcasted_iota(jnp.int32, (1, 128), 1)
    head_mask = [
        jnp.where((lane_row < 64) == (h == 0), 1.0, 0.0).astype(BF) for h in range(2)
    ]
    qaug[...] = jnp.where(lax.broadcasted_iota(jnp.int32, (ROWS, 128), 1) == 0, 1.0, 0.0)
    vs[...] = jnp.zeros_like(vs)

    def project(r):
        rows = pl.ds(r * PART, PART)
        hat, _ = norm_parts(tokx[rows].astype(F32))
        low2[rows] = (hat * vec[0:1] + vec[1:2]).astype(BF)

        def column(j):
            col = pl.multiple_of(j * 256, 256)
            part = lax.rem(j, 3) * 256
            shift = jnp.where(
                j < 3, vec[2:3, at256(part)], jnp.where(j >= 6, vec[3:4, at256(part)], 0.0)
            )
            value = dot_nn(low2[rows], w1[:, pl.ds(col, 256)]) + shift
            qkv[rows, pl.ds(col, 256)] = (value * jnp.where(j < 3, 0.125, 1.0)).astype(BF)

        loop(3, 9, column)
        c_kv[r].start()
        loop(0, 3, column)

    loads[0].wait()
    loads[1].wait()
    project(0)
    c_tok.wait_recv()
    c_row.wait_recv()
    c_cot.start()
    kaug[pl.ds(PART, PART)] = dot_tn(rowb[1], pick).astype(BF)
    c_aug.start()
    project(1)
    load_we = pltpu.make_async_copy(we_ref, w1, lsem.at[5])
    load_we.start()
    c_kv[0].wait_recv()
    c_kv[1].wait_recv()
    c_aug.wait_recv()

    def attend(pair):
        col = pl.multiple_of(pair * 128, 128)
        ones = jnp.ones((ROWS, 128), BF)
        first = jnp.where(lane_q == 0, 1.0, 0.0).astype(BF)
        k_here = jnp.concatenate([qkv[:, at128(768 + col)], kaug[pl.ds(0, ROWS)]], axis=1)
        k_there = jnp.concatenate([kvr[:, at128(col)], kaug[pl.ds(ROWS, ROWS)]], axis=1)
        v_here = jnp.concatenate([qkv[:, at128(1536 + col)], ones], axis=1)
        v_there = jnp.concatenate([kvr[:, at128(768 + col)], ones], axis=1)
        for block in range(2):
            rows = pl.ds(block * PART, PART)
            query = qkv[rows, at128(col)]
            extra = qaug[rows]
            outs = []
            for h in range(2):
                lifted = jnp.concatenate([query * head_mask[h], first], axis=1)
                s_here = dot_nt(lifted, k_here)
                s_there = dot_nt(lifted, k_there)
                top = jnp.maximum(
                    jnp.max(s_here, axis=-1, keepdims=True), jnp.max(s_there, axis=-1, keepdims=True)
                )
                e_here = jnp.exp(s_here - top).astype(BF)
                e_there = jnp.exp(s_there - top).astype(BF)
                both = dot_nn(e_here, v_here) + dot_nn(e_there, v_there)
                total = both[:, 128:]
                outs.append(both[:, :128] / total)
                parts = three_parts(top + jnp.log(total))
                base = 1 + 3 * (2 * pair + h)
                for i in range(3):
                    extra = jnp.where(lane_q == base + i, -parts[i], extra)
            qaug[rows] = extra
            att[rows, at128(col)] = jnp.where(lane_q < 64, outs[0], outs[1]).astype(BF)

    loop(0, 6, attend)

    def turn(rows, block):
        flipped = block.T
        for quarter in range(4):
            seat = pl.multiple_of(p.seat(quarter) * HR, HR)
            turned[pl.ds(seat, HR), rows] = flipped[quarter * HR : (quarter + 1) * HR]

    loads[3].wait()

    def middle(i):
        rows = at256(i * PART)
        value = tokx[rows].astype(F32) + dot_nn(att[rows], wo[...]) + vec[4:5]
        mid[rows] = value
        hat, _ = norm_parts(value)
        block = (hat * vec[5:6] + vec[6:7]).astype(BF)
        low2[rows] = block
        turn(rows, block)

    loop(0, 2, middle)
    loads[2].wait()
    loads[4].wait()
    load_we.wait()
    c_cot.wait_recv()
    y_sum[...] = jnp.zeros_like(y_sum)
    h_sum[...] = jnp.zeros_like(h_sum)

    def feed(t):
        starts = []
        for side in range(2):
            cc = p.core if side == 0 else 1 - p.core
            for yy in range(2):
                starts.append((yy * 2 + cc) * 768 + t * 128)
        w_up = jnp.concatenate([w1[:, at128(s)] for s in starts], axis=1)
        shifts = vec[8:12, at128(t * 128)]
        zeroth = p.core == 0
        shift = jnp.concatenate(
            [
                jnp.where(zeroth, shifts[yy * 2 + s : yy * 2 + s + 1], shifts[yy * 2 + 1 - s : yy * 2 + 2 - s])
                for s in range(2)
                for yy in range(2)
            ],
            axis=1,
        )
        before = dot_nn(low2[...], w_up) + shift
        half = 0.5 + 0.5 * lax.erf(before * 0.7071067811865476)
        active = (before * half).astype(BF)
        slope = half + before * (jnp.exp(before * before * -0.5) * 0.3989422804014327)
        g_t[...] = active
        w_down = jnp.concatenate([wr[at128(s), :] for s in starts], axis=0)
        du_t[...] = (dot_nt(dyx[...], w_down) * slope).astype(BF)
        tall = dot_nn(g_t[...].T, dyx[...]).astype(BF)
        red.emit_tall(4 * t, tall, 0)
        red.emit_tall(4 * t + 1, tall, QR)
        for e in range(2):
            seats = [e + 2 * (p.core if cc == 0 else 1 - p.core) for cc in range(2)]
            right = jnp.concatenate([du_t[:, at128(s * 128)] for s in seats], axis=1)
            red.emit_wide(4 * t + 2 + e, dot_nn(turned[...], right).astype(BF))
        sums = jnp.sum(du_t[...].astype(F32), axis=0, keepdims=True)
        seat = [sums[:, i * 128 : (i + 1) * 128] for i in range(4)]
        vs[8:12, at128(t * 128)] = jnp.concatenate(
            [
                jnp.where(zeroth, seat[yy + 2 * cc], seat[yy + 2 - 2 * cc])
                for yy in range(2)
                for cc in range(2)
            ],
            axis=0,
        )
        red.tick(2 * t)
        y_sum[...] += dot_nn(g_t[...], w_down)
        h_sum[...] += dot_nt(du_t[...], w_up)
        red.tick(2 * t + 1)

    loop(0, 6, feed)
    reload_wi = pltpu.make_async_copy(wi_ref, w1.at[:, pl.ds(0, 2304)], lsem.at[6])
    reload_wi.start()

    def second(i):
        rows = at256(i * PART)
        value = mid[rows]
        lo[rows] = (value + y_sum[rows] + vec[7:8]).astype(BF)
        hat, scale = norm_parts(value)
        grad = h_sum[rows]
        upstream = dyx[rows].astype(F32)
        vs[5:6] += jnp.sum(grad * hat, axis=0, keepdims=True)
        vs[6:7] += jnp.sum(grad, axis=0, keepdims=True)
        vs[7:8] += jnp.sum(upstream, axis=0, keepdims=True)
        total = upstream + norm_back(hat, scale, vec[5:6], grad)
        mid[rows] = total
        block = total.astype(BF)
        low2[rows] = block
        vs[4:5] += jnp.sum(block.astype(F32), axis=0, keepdims=True)
        d_out[rows] = dot_nt(block, wo[...]).astype(BF)
        turn(rows, att[rows])

    loop(0, 2, second)
    red.tick(12)

    def out_grad(n):
        red.emit_wide(24 + n, dot_nn(turned[...], low2[:, at256(n * 256)]).astype(BF))

    loop(0, 3, out_grad)
    red.tick(13)

    def c_dkv(pair):
        return remote(
            dkv_send.at[lax.rem(pair, 2)], dkv_recv.at[pair], ksend.at[pair], krecv.at[pair], p.to_core
        )

    def settle(pair):
        c_dkv(pair).wait_recv()
        slot = lax.rem(pair, 2)
        for i in range(2):
            total = dkv_own[slot, i] + dkv_recv[pair, i].astype(F32)
            dp[:, at128(768 * (i + 1) + pair * 128)] = total.astype(BF)

    lane_k = lax.broadcasted_iota(jnp.int32, (ROWS, 128), 1)

    def attend_back(pair):
        col = pl.multiple_of(pair * 128, 128)
        slot = lax.rem(pair, 2)
        query = qkv[:, at128(col)]
        extra_q = qaug[...].astype(BF)
        grads = d_out[:, at128(col)]
        outs = att[:, at128(col)].astype(F32)
        three = jnp.where(lane_k < 3, 1.0, 0.0).astype(BF)
        dq = jnp.zeros((128, ROWS), F32)
        dk = [jnp.zeros((ROWS, 128), F32)] * 2
        dv = [jnp.zeros((ROWS, 128), F32)] * 2
        for h in range(2):
            q_h = query * head_mask[h]
            g_h = grads * head_mask[h]
            parts = three_parts(jnp.sum(g_h.astype(F32) * outs, axis=-1, keepdims=True))
            extra_g = jnp.zeros((ROWS, 128), F32)
            for i in range(3):
                extra_g = jnp.where(lane_k == i, -parts[i], extra_g)
            q_wide = jnp.concatenate([q_h, extra_q], axis=1)
            g_wide = jnp.concatenate([g_h, extra_g.astype(BF)], axis=1)
            base = 1 + 3 * (2 * pair + h)
            mark = jnp.where(
                jnp.logical_and(lane_k >= base, lane_k < base + 3), 1.0, 0.0
            ).astype(BF)
            for side in range(2):
                if side == 0:
                    key, value = qkv[:, at128(768 + col)], qkv[:, at128(1536 + col)]
                else:
                    key, value = kvr[:, at128(col)], kvr[:, at128(768 + col)]
                k_wide = jnp.concatenate([key, kaug[pl.ds(side * ROWS, ROWS)] + mark], axis=1)
                v_wide = jnp.concatenate([value, three], axis=1)
                weight = jnp.exp(dot_nt(k_wide, q_wide))
                slope = (weight * dot_nt(v_wide, g_wide)).astype(BF)
                dv[side] = dv[side] + dot_nn(weight.astype(BF), g_h)
                dk[side] = dk[side] + dot_nn(slope, q_h)
                dq = dq + dot_nn((key * head_mask[h]).T, slope)
        dp[:, at128(col)] = (dq.T.astype(BF).astype(F32) * 0.125).astype(BF)

        @pl.when(pair >= 1)
        def _():
            settle(pair - 1)

        @pl.when(pair >= 2)
        def _():
            c_dkv(pair - 2).wait_send()

        dkv_own[slot, 0] = dk[0]
        dkv_own[slot, 1] = dv[0]
        dkv_send[slot, 0] = dk[1].astype(BF)
        dkv_send[slot, 1] = dv[1].astype(BF)
        c_dkv(pair).start()
        red.tick(14 + 2 * pair)
        red.tick(15 + 2 * pair)

    loop(0, 6, attend_back)
    settle(5)
    c_dkv(4).wait_send()
    c_dkv(5).wait_send()

    def turn_first(i):
        rows = at256(i * PART)
        hat, _ = norm_parts(tokx[rows].astype(F32))
        turn(rows, (hat * vec[0:1] + vec[1:2]).astype(BF))

    loop(0, 2, turn_first)

    def in_grad(n):
        red.emit_wide(27 + n, dot_nn(turned[...], dp[:, at256(n * 256)]).astype(BF))
        red.tick(26 + n)

    loop(0, 9, in_grad)
    vs[2:3] = jnp.sum(dp[:, 0:768].astype(F32), axis=0, keepdims=True)
    vs[3:4] = jnp.sum(dp[:, 1536:2304].astype(F32), axis=0, keepdims=True)
    reload_wi.wait()
    c_lo = swap(6, lo.at[pl.ds(PART, PART)], lo_ref.at[p.y], p.to_y)
    keep_lo = pltpu.make_async_copy(lo.at[pl.ds(0, PART)], lo_ref.at[p.y], lsem.at[7])
    c_lo.start()
    keep_lo.start()

    def first_back(i):
        rows = at256(i * PART)
        grad = dot_nt(dp[rows], w1[:, pl.ds(0, 2304)])
        hat, scale = norm_parts(tokx[rows].astype(F32))
        vs[0:1] += jnp.sum(grad * hat, axis=0, keepdims=True)
        vs[1:2] += jnp.sum(grad, axis=0, keepdims=True)
        y_sum[rows] = mid[rows] + norm_back(hat, scale, vec[0:1], grad)

    loop(0, 2, first_back)
    gts[...] = y_sum[pl.ds(PART, PART)].astype(BF)
    c_gt = swap(7, gts, gtr_ref, p.to_y)
    keep_gt = pltpu.make_async_copy(y_sum.at[pl.ds(0, PART)], gto_ref, lsem.at[8])
    c_gt.start()
    keep_gt.start()

    def c_vec(stage, peer):
        return remote(vr.at[2 * stage], vr.at[2 * stage + 1], vsend.at[stage], vrecv.at[stage], peer)

    def vec_pair(stage, peer):
        vr[2 * stage] = vs[...]
        c_vec(stage, peer).start()

    def vec_take(stage, peer):
        c_vec(stage, peer).wait()
        vs[...] += vr[2 * stage + 1]

    vec_pair(0, p.to_core)
    red.tick(35)
    vec_take(0, p.to_core)
    vec_pair(1, p.to_y)
    red.tick(36)
    vec_take(1, p.to_y)
    vec_pair(2, p.to_x)
    red.tick(37)
    vec_take(2, p.to_x)

    @pl.when(p.outer)
    def _():
        vec_pair(3, p.to_mate)

    red.tick(38)

    @pl.when(p.inner)
    def _():
        c_vec(3, p.to_mate).wait_recv()
        vs[...] += vr[7]
        vec_pair(4, p.to_inner)

    red.tick(39)

    @pl.when(p.inner)
    def _():
        vec_take(4, p.to_inner)
        vec_pair(3, p.to_mate)

    red.tick(40)

    @pl.when(p.outer)
    def _():
        c_vec(3, p.to_mate).wait_recv()
        vs[...] = vr[7]

    c_vec(3, p.to_mate).wait_send()

    def drain(t):
        red.tick(t)

    loop(41, K + LAGS[-1], drain)
    c_tok.wait_send()
    c_row.wait_send()
    c_cot.wait_send()
    c_aug.wait_send()
    c_kv[0].wait_send()
    c_kv[1].wait_send()
    c_lo.wait()
    c_gt.wait()
    keep_lo.wait()
    keep_gt.wait()


def finish_kernel(tot, vs, lo_in, gto, gtr, lo_out, gt, g0, g1, wi, g2, wo, g4, g5, g6, we, g8, wr, g7):
    y = lax.axis_index("frame") // 2
    frame = lax.axis_index("frame")
    lo_out[...] = lo_in[...].reshape(2, 1, PART, D)
    gt[y, 0] = gto[...]
    gt[1 - y, 0] = gtr[...].astype(F32)
    for t in range(6):
        for hh in range(2):
            for i in range(3):
                col = (3 * hh + i) * 128
                wr[t * 128 : (t + 1) * 128, col : col + 128] = tot[4 * t + hh, i * 128 : (i + 1) * 128].astype(F32)
        for j in range(4):
            col = j * 768 + t * 128
            side = j % 2
            we[:, col : col + 128] = tot[4 * t + 2 + j // 2, side * HR : (side + 1) * HR].astype(F32)
    for out, base, count in ((wo, 24, 3), (wi, 27, 9)):
        for n in range(count):
            for side in range(2):
                col = n * 256 + side * 128
                out[:, col : col + 128] = tot[base + n, side * HR : (side + 1) * HR].astype(F32)
    own = [jnp.zeros((16, HR), F32)]
    for f in range(4):
        own.append(jnp.where(frame == f, vs[:, f * HR : (f + 1) * HR], own[-1]))
    mine = own[-1]
    g0[...] = mine[0]
    g1[...] = mine[1]
    g2[...] = mine[2:4]
    g4[...] = mine[4]
    g5[...] = mine[5]
    g6[...] = mine[6]
    g7[...] = mine[7]
    row = vs[8:9]
    for f in range(1, 4):
        row = jnp.where(frame == f, vs[8 + f : 9 + f], row)
    g8[...] = row[0]


def local_slice(
    tokens,
    counts,
    first_gain,
    first_bias,
    input_weight,
    input_bias,
    output_weight,
    output_bias,
    second_gain,
    second_bias,
    expand_weight,
    expand_bias,
    reduce_weight,
    reduce_bias,
    cotangent,
):
    rows = [first_gain, first_bias, input_bias[0], input_bias[1], output_bias, second_gain, second_bias, reduce_bias]
    vec = jnp.concatenate([jnp.stack(rows), expand_bias.reshape(4, D), jnp.zeros((4, D), BF)]).astype(F32)
    anywhere = pl.BlockSpec(memory_space=pl.ANY)
    vmem = pl.BlockSpec(memory_space=pltpu.VMEM)
    smem = pl.BlockSpec(memory_space=pltpu.SMEM)
    shape = jax.ShapeDtypeStruct
    dma = pltpu.SemaphoreType.DMA
    tot, vs, lo, gto, gtr = pl.pallas_call(
        layer_kernel,
        out_shape=(
            shape((K, QR, 128), BF),
            shape((16, D), F32),
            shape((2, PART, D), BF),
            shape((PART, D), F32),
            shape((PART, D), BF),
        ),
        in_specs=[anywhere, anywhere, smem, vmem] + [anywhere] * 4,
        out_specs=(anywhere, vmem, anywhere, anywhere, anywhere),
        scratch_shapes=[
            pltpu.VMEM((K, 2, QR, 128), BF),
            pltpu.VMEM((SLOT_COUNT, 2, QR, 128), BF),
            pltpu.VMEM((K, 2, QR, 128), BF),
            pltpu.VMEM((K, QR, 128), BF),
            pltpu.VMEM((K, HR, 128), BF),
            pltpu.VMEM((K, HR, 128), BF),
            pltpu.VMEM((K, HR, 128), BF),
            pltpu.VMEM((ROWS, D), BF),
            pltpu.VMEM((ROWS, D), BF),
            pltpu.VMEM((D, FF), BF),
            pltpu.VMEM((D, D), BF),
            pltpu.VMEM((FF, D), BF),
            pltpu.VMEM((ROWS, 3 * D), BF),
            pltpu.VMEM((ROWS, 2 * D), BF),
            pltpu.VMEM((3, 16, PART), BF),
            pltpu.VMEM((2 * ROWS, 128), BF),
            pltpu.VMEM((ROWS, 128), F32),
            pltpu.VMEM((ROWS, D), BF),
            pltpu.VMEM((ROWS, D), F32),
            pltpu.VMEM((ROWS, D), BF),
            pltpu.VMEM((D, ROWS), BF),
            pltpu.VMEM((ROWS, ROWS), BF),
            pltpu.VMEM((ROWS, ROWS), BF),
            pltpu.VMEM((ROWS, D), F32),
            pltpu.VMEM((ROWS, D), F32),
            pltpu.VMEM((ROWS, D), BF),
            pltpu.VMEM((ROWS, 3 * D), BF),
            pltpu.VMEM((2, 2, ROWS, 128), F32),
            pltpu.VMEM((2, 2, ROWS, 128), BF),
            pltpu.VMEM((6, 2, ROWS, 128), BF),
            pltpu.VMEM((ROWS, D), BF),
            pltpu.VMEM((PART, D), BF),
            pltpu.VMEM((10, 16, D), F32),
            dma((6, K)),
            dma((6, K)),
            dma((K,)),
            dma((9,)),
            dma((8,)),
            dma((8,)),
            dma((6,)),
            dma((6,)),
            dma((5,)),
            dma((5,)),
        ],
        compiler_params=pltpu.CompilerParams(
            collective_id=0, has_side_effects=True, vmem_limit_bytes=62 << 20
        ),
    )(tokens, cotangent, counts, vec, input_weight, output_weight, expand_weight, reduce_weight)
    return pl.pallas_call(
        finish_kernel,
        out_shape=(
            shape((MICRO, 1, PART, D), BF),
            shape((MICRO, 1, PART, D), F32),
            shape((HR,), F32),
            shape((HR,), F32),
            shape((HR, 3 * D), F32),
            shape((2, HR), F32),
            shape((HR, D), F32),
            shape((HR,), F32),
            shape((HR,), F32),
            shape((HR,), F32),
            shape((HR, FF), F32),
            shape((D,), F32),
            shape((D, D), F32),
            shape((HR,), F32),
        ),
        in_specs=[vmem] * 5,
        out_specs=(vmem,) * 14,
        compiler_params=pltpu.CompilerParams(vmem_limit_bytes=40 << 20),
    )(tot, vs, lo, gto, gtr)


def solution(mesh):
    fits = mesh.shape["clip"] == 8 and mesh.shape["frame"] == 4
    return jax.shard_map(
        local_slice if fits else local,
        mesh=mesh,
        in_specs=(
            P(None, "clip", "frame", None),
            P(None, "clip", "frame"),
            P(),
            P(),
            P(),
            P(),
            P(),
            P(),
            P(),
            P(),
            P(),
            P(),
            P(),
            P(),
            P(None, "clip", "frame", None),
        ),
        out_specs=(
            P(None, "clip", "frame", None),
            P(None, "clip", "frame", None),
            P("frame"),
            P("frame"),
            P("frame", None),
            P(None, "frame"),
            P("frame", None),
            P("frame"),
            P("frame"),
            P("frame"),
            P("frame", None),
            P("frame"),
            P("frame", None),
            P("frame"),
        ),
        check_vma=False,
    )
```

```python
import jax
import jax.numpy as jnp
from jax import lax
from jax.experimental import pallas as pl
from jax.experimental.pallas import tpu as pltpu
from jax.sharding import PartitionSpec as P

D = 768
H = 12
HD = 64
MICRO = 2
FRAME_DEV = 4
SLOTS = 64
BLOCK = 256


epsilon = 1e-06


def from_behind(block, axis, distance):
    devices = range(lax.axis_size(axis))
    route = [((i - distance) % len(devices), i) for i in devices]
    return lax.ppermute(block, axis, route)


def norm_rows(values, gain, shift):
    mean = jnp.mean(values, axis=-1, keepdims=True)
    centred = values - mean
    spread = jnp.mean(centred * centred, axis=-1, keepdims=True)
    return centred * lax.rsqrt(spread + epsilon) * gain + shift


def gelu_exact(values):
    return jax.nn.gelu(values, approximate=False)


def key_valid(every_count, source):
    frame_counts = lax.dynamic_slice_in_dim(every_count, source * FRAME_DEV, FRAME_DEV, 1)
    slot_index = jnp.arange(SLOTS, dtype=jnp.int32)
    return (slot_index[None, None, :] < frame_counts[:, :, None]).reshape(MICRO, BLOCK)


def scores_of(query, keys, valid):
    key_heads = keys.reshape(MICRO, BLOCK, H, HD)
    scores = jnp.einsum("mqhd,mkhd->mhqk", query, key_heads, preferred_element_type=jnp.float32)
    return jnp.where(valid[:, None, None, :], scores, -1e30)


def absorb(state, query, keys, values, valid):
    top, total, summed = state
    scores = scores_of(query, keys, valid)
    new_top = jnp.maximum(top, jnp.max(scores, axis=-1, keepdims=True))
    factor = jnp.exp(top - new_top)
    lifted = jnp.exp(scores - new_top)
    total = total * factor + jnp.sum(lifted, axis=-1, keepdims=True)
    value_heads = values.reshape(MICRO, BLOCK, H, HD)
    summed = summed * factor + jnp.einsum(
        "mhqk,mkhd->mhqd",
        lifted.astype(jnp.bfloat16),
        value_heads,
        preferred_element_type=jnp.float32,
    )
    return (new_top, total, summed)


def block_back(query, keys, values, valid, log_total, delta, grad_heads):
    scores = scores_of(query, keys, valid)
    weights = jnp.exp(scores - log_total)
    key_heads = keys.reshape(MICRO, BLOCK, H, HD)
    value_heads = values.reshape(MICRO, BLOCK, H, HD)
    grad_weights = jnp.einsum(
        "mqhd,mkhd->mhqk", grad_heads, value_heads, preferred_element_type=jnp.float32
    )
    grad_scores = (weights * (grad_weights - delta)).astype(jnp.bfloat16)
    grad_query = jnp.einsum(
        "mhqk,mkhd->mqhd", grad_scores, key_heads, preferred_element_type=jnp.float32
    )
    grad_keys = jnp.einsum(
        "mhqk,mqhd->mkhd", grad_scores, query, preferred_element_type=jnp.float32
    )
    grad_values = jnp.einsum(
        "mhqk,mqhd->mkhd",
        weights.astype(jnp.bfloat16),
        grad_heads,
        preferred_element_type=jnp.float32,
    )
    return (grad_query, grad_keys.reshape(MICRO, BLOCK, D), grad_values.reshape(MICRO, BLOCK, D))


def local(
    tokens,
    counts,
    first_gain,
    first_bias,
    input_weight,
    input_bias,
    output_weight,
    output_bias,
    second_gain,
    second_bias,
    expand_weight,
    expand_bias,
    reduce_weight,
    reduce_bias,
    cotangent,
):
    members = lax.axis_size("frame")
    myself = lax.axis_index("frame")
    total_rows = MICRO * BLOCK
    seq_in = tokens.reshape(total_rows, D).astype(jnp.float32)
    every_count = lax.all_gather(counts.reshape(MICRO, FRAME_DEV), "frame", axis=1, tiled=True)
    gain_one = first_gain.astype(jnp.float32)
    shift_one = first_bias.astype(jnp.float32)
    gain_two = second_gain.astype(jnp.float32)
    shift_two = second_bias.astype(jnp.float32)
    qv_bias = input_bias.astype(jnp.float32)
    first_low = norm_rows(seq_in, gain_one, shift_one).astype(jnp.bfloat16)
    projected = jnp.dot(first_low, input_weight, preferred_element_type=jnp.float32)
    query = (
        ((projected[:, :D] + qv_bias[0]) * 0.125).astype(jnp.bfloat16).reshape(MICRO, BLOCK, H, HD)
    )
    keys = projected[:, D : 2 * D].astype(jnp.bfloat16).reshape(MICRO, BLOCK, D)
    values = (projected[:, 2 * D :] + qv_bias[1]).astype(jnp.bfloat16).reshape(MICRO, BLOCK, D)
    start = (
        jnp.full((MICRO, H, BLOCK, 1), -1e30, jnp.float32),
        jnp.zeros((MICRO, H, BLOCK, 1), jnp.float32),
        jnp.zeros((MICRO, H, BLOCK, HD), jnp.float32),
    )
    state = absorb(start, query, keys, values, key_valid(every_count, myself))
    stored = ()

    def forward_hop(step, carry):
        state_now, moving, kept = carry
        moving = from_behind((moving[0], moving[1]), "frame", 1)
        source = (myself - step) % members
        state_now = absorb(state_now, query, moving[0], moving[1], key_valid(every_count, source))
        return (state_now, moving, kept)

    state, _, stored = lax.fori_loop(1, members, forward_hop, (state, (keys, values), stored))
    top, total, summed = state
    log_total = top + jnp.log(total)
    attend_full = jnp.transpose(summed / total, (0, 2, 1, 3))
    attend_low = attend_full.reshape(total_rows, D).astype(jnp.bfloat16)
    middle = (
        seq_in
        + jnp.dot(attend_low, output_weight, preferred_element_type=jnp.float32)
        + output_bias.astype(jnp.float32)
    )
    second_low = norm_rows(middle, gain_two, shift_two).astype(jnp.bfloat16)
    before = jnp.dot(
        second_low, expand_weight, preferred_element_type=jnp.float32
    ) + expand_bias.astype(jnp.float32)
    active_low = gelu_exact(before).astype(jnp.bfloat16)
    result = (
        middle
        + jnp.dot(active_low, reduce_weight, preferred_element_type=jnp.float32)
        + reduce_bias.astype(jnp.float32)
    )
    layer_out = result.astype(jnp.bfloat16).reshape(MICRO, 1, BLOCK, D)
    upstream_low = cotangent.reshape(total_rows, D)
    upstream = upstream_low.astype(jnp.float32)
    grad_reduce_weight = jnp.dot(active_low.T, upstream_low, preferred_element_type=jnp.float32)
    grad_reduce_bias = jnp.sum(upstream, axis=0)
    grad_active = jnp.dot(upstream_low, reduce_weight.T, preferred_element_type=jnp.float32)
    _, gelu_back = jax.vjp(gelu_exact, before)
    grad_before = gelu_back(grad_active)[0].astype(jnp.bfloat16)
    grad_expand_weight = jnp.dot(second_low.T, grad_before, preferred_element_type=jnp.float32)
    grad_expand_bias = jnp.sum(grad_before.astype(jnp.float32), axis=0)
    grad_second = jnp.dot(grad_before, expand_weight.T, preferred_element_type=jnp.float32)
    _, second_back = jax.vjp(norm_rows, middle, gain_two, shift_two)
    middle_part, grad_second_gain, grad_second_bias = second_back(grad_second)
    grad_middle = upstream + middle_part
    grad_branch = grad_middle.astype(jnp.bfloat16)
    grad_output_weight = jnp.dot(attend_low.T, grad_branch, preferred_element_type=jnp.float32)
    grad_output_bias = jnp.sum(grad_branch.astype(jnp.float32), axis=0)
    grad_attend = jnp.dot(grad_branch, output_weight.T, preferred_element_type=jnp.float32).astype(
        jnp.bfloat16
    )
    grad_heads = grad_attend.reshape(MICRO, BLOCK, H, HD)
    delta = jnp.transpose(
        jnp.sum(grad_heads.astype(jnp.float32) * attend_full, axis=-1), (0, 2, 1)
    )[..., None]
    first_terms = block_back(
        query, keys, values, key_valid(every_count, myself), log_total, delta, grad_heads
    )

    def backward_hop(step, carry):
        grad_query, running, moving = carry
        running = (
            from_behind(running[0].astype(jnp.bfloat16), "frame", 1).astype(jnp.float32),
            from_behind(running[1].astype(jnp.bfloat16), "frame", 1).astype(jnp.float32),
        )
        current = from_behind((moving[0], moving[1]), "frame", 1)
        source = (myself - step) % members
        add_query, add_keys, add_values = block_back(
            query,
            current[0],
            current[1],
            key_valid(every_count, source),
            log_total,
            delta,
            grad_heads,
        )
        return (grad_query + add_query, (running[0] + add_keys, running[1] + add_values), current)

    grad_query, running, _ = lax.fori_loop(
        1, members, backward_hop, (first_terms[0], (first_terms[1], first_terms[2]), (keys, values))
    )
    finished = (
        from_behind(running[0].astype(jnp.bfloat16), "frame", 1).astype(jnp.float32),
        from_behind(running[1].astype(jnp.bfloat16), "frame", 1).astype(jnp.float32),
    )
    query_low = grad_query.astype(jnp.bfloat16).reshape(total_rows, D) * 0.125
    keys_low = finished[0].astype(jnp.bfloat16).reshape(total_rows, D)
    values_low = finished[1].astype(jnp.bfloat16).reshape(total_rows, D)
    grad_projected = jnp.concatenate([query_low, keys_low, values_low], axis=1)
    grad_input_weight = jnp.dot(first_low.T, grad_projected, preferred_element_type=jnp.float32)
    grad_input_bias = jnp.stack(
        [
            jnp.sum(query_low.astype(jnp.float32), axis=0),
            jnp.sum(values_low.astype(jnp.float32), axis=0),
        ]
    )
    grad_first = jnp.dot(grad_projected, input_weight.T, preferred_element_type=jnp.float32)
    _, first_back = jax.vjp(norm_rows, seq_in, gain_one, shift_one)
    input_part, grad_first_gain, grad_first_bias = first_back(grad_first)
    grad_tokens = (grad_middle + input_part).reshape(MICRO, 1, BLOCK, D)
    shares = (
        lax.psum_scatter(
            grad_first_gain.astype(jnp.bfloat16), "frame", scatter_dimension=0, tiled=True
        ).astype(jnp.float32),
        lax.psum_scatter(
            grad_first_bias.astype(jnp.bfloat16), "frame", scatter_dimension=0, tiled=True
        ).astype(jnp.float32),
        lax.psum_scatter(
            grad_input_weight.astype(jnp.bfloat16), "frame", scatter_dimension=0, tiled=True
        ).astype(jnp.float32),
        lax.psum_scatter(
            grad_input_bias.astype(jnp.bfloat16), "frame", scatter_dimension=1, tiled=True
        ).astype(jnp.float32),
        lax.psum_scatter(
            grad_output_weight.astype(jnp.bfloat16), "frame", scatter_dimension=0, tiled=True
        ).astype(jnp.float32),
        lax.psum_scatter(
            grad_output_bias.astype(jnp.bfloat16), "frame", scatter_dimension=0, tiled=True
        ).astype(jnp.float32),
        lax.psum_scatter(
            grad_second_gain.astype(jnp.bfloat16), "frame", scatter_dimension=0, tiled=True
        ).astype(jnp.float32),
        lax.psum_scatter(
            grad_second_bias.astype(jnp.bfloat16), "frame", scatter_dimension=0, tiled=True
        ).astype(jnp.float32),
        lax.psum_scatter(
            grad_expand_weight.astype(jnp.bfloat16), "frame", scatter_dimension=0, tiled=True
        ).astype(jnp.float32),
        lax.psum_scatter(
            grad_expand_bias.astype(jnp.bfloat16), "frame", scatter_dimension=0, tiled=True
        ).astype(jnp.float32),
        lax.psum_scatter(
            grad_reduce_weight.astype(jnp.bfloat16), "frame", scatter_dimension=0, tiled=True
        ).astype(jnp.float32),
        lax.psum_scatter(
            grad_reduce_bias.astype(jnp.bfloat16), "frame", scatter_dimension=0, tiled=True
        ).astype(jnp.float32),
    )
    totals = (
        lax.psum(shares[0].astype(jnp.bfloat16), "clip").astype(jnp.float32),
        lax.psum(shares[1].astype(jnp.bfloat16), "clip").astype(jnp.float32),
        lax.psum(shares[2].astype(jnp.bfloat16), "clip").astype(jnp.float32),
        lax.psum(shares[3].astype(jnp.bfloat16), "clip").astype(jnp.float32),
        lax.psum(shares[4].astype(jnp.bfloat16), "clip").astype(jnp.float32),
        lax.psum(shares[5].astype(jnp.bfloat16), "clip").astype(jnp.float32),
        lax.psum(shares[6].astype(jnp.bfloat16), "clip").astype(jnp.float32),
        lax.psum(shares[7].astype(jnp.bfloat16), "clip").astype(jnp.float32),
        lax.psum(shares[8].astype(jnp.bfloat16), "clip").astype(jnp.float32),
        lax.psum(shares[9].astype(jnp.bfloat16), "clip").astype(jnp.float32),
        lax.psum(shares[10].astype(jnp.bfloat16), "clip").astype(jnp.float32),
        lax.psum(shares[11].astype(jnp.bfloat16), "clip").astype(jnp.float32),
    )
    return (
        layer_out,
        grad_tokens,
        totals[0],
        totals[1],
        totals[2],
        totals[3],
        totals[4],
        totals[5],
        totals[6],
        totals[7],
        totals[8],
        totals[9],
        totals[10],
        totals[11],
    )


MESH = pl.DeviceIdType.MESH
BF = jnp.bfloat16
F32 = jnp.float32
K = 36
QR = 384
HR = 192
SLOT_COUNT = 8
ROWS = 512
PART = 256
FF = 3072
LOW = -1e30
LAGS = (0, 6, 12, 15, 18, 21, 24)
WAYS = "acbacabca"
TALL = ((0, 0, 0, 0, 128), (0, 128, 1, 0, 64), (1, 0, 1, 64, 128), (1, 64, 2, 0, 128))


def dot_nn(a, b):
    return lax.dot_general(a, b, (((1,), (0,)), ((), ())), preferred_element_type=F32)


def dot_nt(a, b):
    return lax.dot_general(a, b, (((1,), (1,)), ((), ())), preferred_element_type=F32)


def dot_tn(a, b):
    return lax.dot_general(a, b, (((0,), (0,)), ((), ())), preferred_element_type=F32)


def at128(index):
    return pl.ds(pl.multiple_of(index, 128), 128)


def at256(index):
    return pl.ds(pl.multiple_of(index, 256), 256)


def loop(low, high, body):
    def step(i, carry):
        body(i)
        return carry

    lax.fori_loop(low, high, step, 0)


class Place:
    def __init__(self):
        self.clip = lax.axis_index("clip")
        self.frame = lax.axis_index("frame")
        self.x = lax.rem(self.clip, 2)
        self.z = self.clip // 2
        self.core = lax.rem(self.frame, 2)
        self.y = self.frame // 2
        self.outer = jnp.logical_or(self.z == 0, self.z == 3)
        self.inner = jnp.logical_not(self.outer)
        self.to_core = (self.clip, self.y * 2 + (1 - self.core))
        self.to_y = (self.clip, (1 - self.y) * 2 + self.core)
        self.to_x = (self.z * 2 + (1 - self.x), self.frame)
        mate = self.z + 1 - 2 * lax.rem(self.z, 2)
        self.to_mate = (mate * 2 + self.x, self.frame)
        self.to_far = ((3 - self.z) * 2 + self.x, self.frame)
        self.h = jnp.where(self.inner, 1, 0)

    def seat(self, quarter):
        yy, cc = quarter // 2, quarter % 2
        return yy + 2 * (self.core if cc == 0 else 1 - self.core)


def enter(place):
    barrier = pltpu.get_barrier_semaphore()
    for peer in (place.to_core, place.to_y, place.to_x, place.to_mate, place.to_far):
        pl.semaphore_signal(barrier, inc=1, device_id=peer, device_id_type=MESH)
    pl.semaphore_wait(barrier, 5)


def remote(src, dst, send, recv, peer):
    return pltpu.make_async_remote_copy(
        src_ref=src, dst_ref=dst, send_sem=send, recv_sem=recv, device_id=peer, device_id_type=MESH
    )


class Reduce:
    def __init__(self, place, bufs, tot, send, recv, tsem):
        self.p = place
        self.own, self.nbr, self.rc, self.ry, self.rx, self.r1, self.r2 = bufs
        self.tot, self.send, self.recv, self.tsem = tot, send, recv, tsem

    def copy(self, src, dst, stage, k, peer):
        return remote(src, dst, self.send.at[stage, k], self.recv.at[stage, k], peer)

    def keep(self, src, dst, k):
        return pltpu.make_async_copy(src, dst, self.tsem.at[k])

    def part(self, far):
        return pl.ds(pl.multiple_of((1 - self.p.x if far else self.p.x) * 96, 96), 96)

    def c_core(self, k):
        return self.copy(self.nbr.at[lax.rem(k, SLOT_COUNT)], self.rc.at[k], 0, k, self.p.to_core)

    def a_y(self, k):
        return self.copy(self.own.at[k, 1 - self.p.y], self.ry.at[k], 1, k, self.p.to_y)

    def a_x(self, k):
        return self.copy(self.own.at[k, self.p.y, 1 - self.p.x], self.rx.at[k], 2, k, self.p.to_x)

    def b_x(self, k):
        return self.copy(self.own.at[k, :, 1 - self.p.x], self.ry.at[k], 1, k, self.p.to_x)

    def b_y(self, k):
        return self.copy(self.own.at[k, 1 - self.p.y, self.p.x], self.rx.at[k], 2, k, self.p.to_y)

    def half(self, k):
        return self.own.at[k, self.p.y, self.p.x]

    def l_in(self, k):
        return self.copy(self.half(k), self.r1.at[k], 3, k, self.p.to_mate)

    def l_mid(self, k):
        return self.copy(self.half(k), self.r2.at[k], 4, k, self.p.to_far)

    def l_out(self, k):
        return self.copy(self.r2.at[k], self.r1.at[k], 3, k, self.p.to_mate)

    def l_gather(self, k, inner):
        src = self.r2 if inner else self.r1
        return self.copy(src.at[k], self.tot.at[k, self.p.x], 5, k, self.p.to_x)

    def l_keep(self, k, inner):
        src = self.r2 if inner else self.r1
        return self.keep(src.at[k], self.tot.at[k, self.p.x], k)

    def q_pair(self, k):
        return self.copy(self.own.at[k, :, 1 - self.p.h], self.ry.at[k], 1, k, self.p.to_mate)

    def q_y(self, k):
        return self.copy(self.own.at[k, 1 - self.p.y, self.p.h], self.rx.at[k], 2, k, self.p.to_y)

    def q_x(self, k):
        src = self.own.at[k, self.p.y, self.p.h, self.part(True)]
        return self.copy(src, self.r1.at[k, pl.ds(0, 96)], 3, k, self.p.to_x)

    def q_far(self, k):
        src = self.own.at[k, self.p.y, self.p.h, self.part(False)]
        return self.copy(src, self.r1.at[k, pl.ds(96, 96)], 4, k, self.p.to_far)

    def q_gather(self, k):
        both = self.r2.at[k, self.part(False)]
        return self.copy(both, both, 5, k, self.p.to_x)

    def q_spread(self, k):
        return self.copy(self.r2.at[k], self.tot.at[k, self.p.h], 6, k, self.p.to_mate)

    def q_keep(self, k):
        return self.keep(self.r2.at[k], self.tot.at[k, self.p.h], k)

    def kinds(self, k):
        if isinstance(k, int):
            return WAYS[k % len(WAYS)]
        m = lax.rem(k, len(WAYS))
        out = {}
        for way in "abc":
            hit = m < 0
            for i, one in enumerate(WAYS):
                if one == way:
                    hit = jnp.logical_or(hit, m == i)
            out[way] = hit
        return out

    def split(self, k, a, b, c):
        kinds = self.kinds(k)
        if isinstance(kinds, str):
            {"a": a, "b": b, "c": c}[kinds](k)
            return
        if a is b:
            pl.when(jnp.logical_not(kinds["c"]))(lambda: a(k))
        else:
            pl.when(kinds["a"])(lambda: a(k))
            pl.when(kinds["b"])(lambda: b(k))
        pl.when(kinds["c"])(lambda: c(k))

    def slot(self, k):
        @pl.when(k >= SLOT_COUNT)
        def _():
            self.c_core(k - SLOT_COUNT).wait_send()

        return lax.rem(k, SLOT_COUNT)

    def emit_wide(self, k, grad):
        slot = self.slot(k)
        for yy in range(2):
            for side in range(2):
                cols = slice(side * 128, (side + 1) * 128)
                self.own[k, yy, side] = grad[yy * HR : (yy + 1) * HR, cols]
                self.nbr[slot, yy, side] = grad[QR + yy * HR : QR + (yy + 1) * HR, cols]
        self.c_core(k).start()

    def emit_tall(self, k, grad, first):
        slot = self.slot(k)
        for yy in range(2):
            for side, to, block, low, high in TALL:
                cols = slice(first + block * 128, first + (block + 1) * 128)
                rows = slice(to, to + high - low)
                self.own[k, yy, side, rows] = grad[yy * 128 + low : yy * 128 + high, cols]
                self.nbr[slot, yy, side, rows] = grad[256 + yy * 128 + low : 256 + yy * 128 + high, cols]
        self.c_core(k).start()

    def stage_1(self, k):
        self.c_core(k).wait_recv()
        self.own[k] = self.own[k] + self.rc[k]
        self.split(
            k,
            lambda k: self.a_y(k).start(),
            lambda k: self.b_x(k).start(),
            lambda k: self.q_pair(k).start(),
        )

    def stage_2(self, k):
        self.a_y(k).wait_recv()

        def a(k):
            self.own[k, self.p.y] = self.own[k, self.p.y] + self.ry[k]
            self.a_x(k).start()

        def b(k):
            self.own[k, :, self.p.x] = self.own[k, :, self.p.x] + self.ry[k]
            self.b_y(k).start()

        def c(k):
            self.own[k, :, self.p.h] = self.own[k, :, self.p.h] + self.ry[k]
            self.q_y(k).start()

        self.split(k, a, b, c)

    def stage_3(self, k):
        self.a_x(k).wait_recv()

        def line(k):
            self.own[k, self.p.y, self.p.x] = self.own[k, self.p.y, self.p.x] + self.rx[k]
            pl.when(self.p.outer)(lambda: self.l_in(k).start())

        def c(k):
            self.own[k, self.p.y, self.p.h] = self.own[k, self.p.y, self.p.h] + self.rx[k]
            self.q_x(k).start()

        self.split(k, line, line, c)

    def stage_4(self, k):
        def line(k):
            @pl.when(self.p.inner)
            def _():
                self.l_in(k).wait_recv()
                self.own[k, self.p.y, self.p.x] = self.own[k, self.p.y, self.p.x] + self.r1[k]
                self.l_mid(k).start()

        def c(k):
            self.q_x(k).wait_recv()
            mine = self.own.at[k, self.p.y, self.p.h, self.part(False)]
            mine[...] = mine[...] + self.r1[k, pl.ds(0, 96)]
            self.q_far(k).start()

        self.split(k, line, line, c)

    def stage_5(self, k):
        def line(k):
            @pl.when(self.p.inner)
            def _():
                self.l_mid(k).wait_recv()
                self.r2[k] = self.r2[k] + self.own[k, self.p.y, self.p.x]
                self.l_out(k).start()
                self.l_gather(k, True).start()
                self.l_keep(k, True).start()

        def c(k):
            self.q_far(k).wait_recv()
            mine = self.own.at[k, self.p.y, self.p.h, self.part(False)]
            self.r2[k, self.part(False)] = mine[...] + self.r1[k, pl.ds(96, 96)]
            self.q_gather(k).start()

        self.split(k, line, line, c)

    def stage_6(self, k):
        def line(k):
            @pl.when(self.p.outer)
            def _():
                self.l_in(k).wait_recv()
                self.l_gather(k, False).start()
                self.l_keep(k, False).start()

        def c(k):
            self.q_gather(k).wait_recv()
            self.q_spread(k).start()
            self.q_keep(k).start()

        self.split(k, line, line, c)

    def stage_7(self, k):
        self.a_y(k).wait_send()
        self.a_x(k).wait_send()

        @pl.when(k >= K - SLOT_COUNT)
        def _():
            self.c_core(k).wait_send()

        def line(k):
            self.l_gather(k, True).wait()
            self.l_in(k).wait_send()
            self.l_keep(k, True).wait()
            pl.when(self.p.inner)(lambda: self.l_mid(k).wait_send())

        def c(k):
            self.q_spread(k).wait()
            self.q_x(k).wait_send()
            self.q_far(k).wait_send()
            self.q_gather(k).wait_send()
            self.q_keep(k).wait()

        self.split(k, line, line, c)

    def tick(self, t):
        stages = (self.stage_1, self.stage_2, self.stage_3, self.stage_4, self.stage_5, self.stage_6, self.stage_7)
        for lag, stage in zip(LAGS, stages):
            k = t - lag
            if isinstance(k, int):
                if 0 <= k < K:
                    stage(k)
            else:
                pl.when(jnp.logical_and(k >= 0, k < K))(lambda stage=stage, k=k: stage(k))


def norm_parts(values):
    mean = jnp.mean(values, axis=-1, keepdims=True)
    centred = values - mean
    spread = jnp.mean(centred * centred, axis=-1, keepdims=True)
    scale = lax.rsqrt(spread + epsilon)
    return centred * scale, scale


def norm_back(hat, scale, gain, grad):
    lifted = grad * gain
    level = jnp.mean(lifted, axis=-1, keepdims=True)
    slope = jnp.mean(lifted * hat, axis=-1, keepdims=True)
    return scale * (lifted - level - hat * slope)


def three_parts(values):
    high = values.astype(BF).astype(F32)
    rest = values - high
    middle = rest.astype(BF).astype(F32)
    return high, middle, rest - middle


def layer_kernel(
    tok_ref, cot_ref, cnt_ref, fg_ref, fb_ref, ib_ref, ob_ref, sg_ref, sb_ref, eb_ref, rb_ref,
    wi_ref, wo_ref, we_ref, wr_ref,
    tot_ref, vs, lo_ref, gto_ref, gtr_ref,
    own, nbr, rc, ry, rx, r1, r2, vec,
    tokx, dyx, w1, wo, wr, qkv, kvr, rowb, kaug, qaug, att, mid, low2, turned, g_t, du_t, y_sum, h_sum,
    d_out, dp, dkv_own, dkv_send, dkv_recv, lo, gts, vr,
    send, recv, tsem, lsem, xsend, xrecv, ksend, krecv, vsend, vrecv,
):
    p = Place()
    loads = [
        pltpu.make_async_copy(tok_ref.at[p.y, 0], tokx.at[pl.ds(0, PART)], lsem.at[0]),
        pltpu.make_async_copy(wi_ref, w1.at[:, pl.ds(0, 2304)], lsem.at[1]),
        pltpu.make_async_copy(cot_ref.at[p.y, 0], dyx.at[pl.ds(0, PART)], lsem.at[2]),
        pltpu.make_async_copy(wo_ref, wo, lsem.at[3]),
        pltpu.make_async_copy(wr_ref, wr, lsem.at[4]),
    ]
    for one in loads:
        one.start()
    enter(p)
    red = Reduce(p, (own, nbr, rc, ry, rx, r1, r2), tot_ref, send, recv, tsem)

    def swap(index, src, dst, peer):
        return remote(src, dst, xsend.at[index], xrecv.at[index], peer)

    c_tok = swap(0, tok_ref.at[1 - p.y, 0], tokx.at[pl.ds(PART, PART)], p.to_y)
    c_cot = swap(1, cot_ref.at[1 - p.y, 0], dyx.at[pl.ds(PART, PART)], p.to_y)
    c_row = swap(2, rowb.at[2], rowb.at[1], p.to_y)
    c_aug = swap(3, kaug.at[pl.ds(0, ROWS)], kaug.at[pl.ds(ROWS, ROWS)], p.to_core)
    c_kv = [
        swap(4 + r, qkv.at[pl.ds(r * PART, PART), pl.ds(768, 1536)], kvr.at[pl.ds(r * PART, PART)], p.to_core)
        for r in range(2)
    ]
    c_tok.start()

    for row, ref in ((0, fg_ref), (1, fb_ref), (4, ob_ref), (5, sg_ref), (6, sb_ref), (7, rb_ref)):
        vec[row : row + 1] = ref[...].astype(F32).reshape(1, D)
    vec[2:4] = ib_ref[...].astype(F32)
    for f in range(4):
        vec[8 + f : 9 + f] = eb_ref[f * D : (f + 1) * D].astype(F32).reshape(1, D)

    lane = lax.broadcasted_iota(jnp.int32, (16, PART), 1)

    def bias_row(m):
        frame = lane // SLOTS
        kept = jnp.zeros_like(lane)
        for j in range(FRAME_DEV):
            kept = jnp.where(frame == j, cnt_ref[m, 0, j], kept)
        return jnp.where(lane - frame * SLOTS < kept, 0.0, LOW).astype(BF)

    rowb[0] = bias_row(p.y)
    rowb[2] = bias_row(1 - p.y)
    c_row.start()
    pick = jnp.where(
        jnp.logical_and(
            lax.broadcasted_iota(jnp.int32, (16, 128), 0) == 0,
            lax.broadcasted_iota(jnp.int32, (16, 128), 1) == 0,
        ),
        1.0,
        0.0,
    ).astype(BF)
    kaug[pl.ds(0, PART)] = dot_tn(rowb[0], pick).astype(BF)
    lane_q = lax.broadcasted_iota(jnp.int32, (PART, 128), 1)
    lane_row = lax.broadcasted_iota(jnp.int32, (1, 128), 1)
    head_mask = [
        jnp.where((lane_row < 64) == (h == 0), 1.0, 0.0).astype(BF) for h in range(2)
    ]
    qaug[...] = jnp.where(lax.broadcasted_iota(jnp.int32, (ROWS, 128), 1) == 0, 1.0, 0.0)
    vs[...] = jnp.zeros_like(vs)

    def project(r):
        rows = pl.ds(r * PART, PART)
        hat, _ = norm_parts(tokx[rows].astype(F32))
        low2[rows] = (hat * vec[0:1] + vec[1:2]).astype(BF)

        def column(j):
            col = pl.multiple_of(j * 256, 256)
            part = lax.rem(j, 3) * 256
            shift = jnp.where(
                j < 3, vec[2:3, at256(part)], jnp.where(j >= 6, vec[3:4, at256(part)], 0.0)
            )
            value = dot_nn(low2[rows], w1[:, pl.ds(col, 256)]) + shift
            qkv[rows, pl.ds(col, 256)] = (value * jnp.where(j < 3, 0.125, 1.0)).astype(BF)

        loop(3, 9, column)
        c_kv[r].start()
        loop(0, 3, column)

    loads[0].wait()
    loads[1].wait()
    project(0)
    c_tok.wait_recv()
    c_row.wait_recv()
    c_cot.start()
    kaug[pl.ds(PART, PART)] = dot_tn(rowb[1], pick).astype(BF)
    c_aug.start()
    project(1)
    load_we = pltpu.make_async_copy(we_ref, w1, lsem.at[5])
    load_we.start()
    c_kv[0].wait_recv()
    c_kv[1].wait_recv()
    c_aug.wait_recv()

    def attend(pair):
        col = pl.multiple_of(pair * 128, 128)
        ones = jnp.ones((ROWS, 128), BF)
        first = jnp.where(lane_q == 0, 1.0, 0.0).astype(BF)
        k_here = jnp.concatenate([qkv[:, at128(768 + col)], kaug[pl.ds(0, ROWS)]], axis=1)
        k_there = jnp.concatenate([kvr[:, at128(col)], kaug[pl.ds(ROWS, ROWS)]], axis=1)
        v_here = jnp.concatenate([qkv[:, at128(1536 + col)], ones], axis=1)
        v_there = jnp.concatenate([kvr[:, at128(768 + col)], ones], axis=1)
        for block in range(2):
            rows = pl.ds(block * PART, PART)
            query = qkv[rows, at128(col)]
            extra = qaug[rows]
            outs = []
            for h in range(2):
                lifted = jnp.concatenate([query * head_mask[h], first], axis=1)
                s_here = dot_nt(lifted, k_here)
                s_there = dot_nt(lifted, k_there)
                top = jnp.maximum(
                    jnp.max(s_here, axis=-1, keepdims=True), jnp.max(s_there, axis=-1, keepdims=True)
                )
                e_here = jnp.exp(s_here - top).astype(BF)
                e_there = jnp.exp(s_there - top).astype(BF)
                both = dot_nn(e_here, v_here) + dot_nn(e_there, v_there)
                total = both[:, 128:]
                outs.append(both[:, :128] / total)
                parts = three_parts(top + jnp.log(total))
                base = 1 + 3 * (2 * pair + h)
                for i in range(3):
                    extra = jnp.where(lane_q == base + i, -parts[i], extra)
            qaug[rows] = extra
            att[rows, at128(col)] = jnp.where(lane_q < 64, outs[0], outs[1]).astype(BF)

    loop(0, 6, attend)

    def turn(rows, block):
        flipped = block.T
        for quarter in range(4):
            seat = pl.multiple_of(p.seat(quarter) * HR, HR)
            turned[pl.ds(seat, HR), rows] = flipped[quarter * HR : (quarter + 1) * HR]

    loads[3].wait()

    def middle(i):
        rows = at256(i * PART)
        value = tokx[rows].astype(F32) + dot_nn(att[rows], wo[...]) + vec[4:5]
        mid[rows] = value
        hat, _ = norm_parts(value)
        block = (hat * vec[5:6] + vec[6:7]).astype(BF)
        low2[rows] = block
        turn(rows, block)

    loop(0, 2, middle)
    loads[2].wait()
    loads[4].wait()
    load_we.wait()
    c_cot.wait_recv()
    y_sum[...] = jnp.zeros_like(y_sum)
    h_sum[...] = jnp.zeros_like(h_sum)

    def feed(t):
        starts = []
        for side in range(2):
            cc = p.core if side == 0 else 1 - p.core
            for yy in range(2):
                starts.append((yy * 2 + cc) * 768 + t * 128)
        w_up = jnp.concatenate([w1[:, at128(s)] for s in starts], axis=1)
        shifts = vec[8:12, at128(t * 128)]
        zeroth = p.core == 0
        shift = jnp.concatenate(
            [
                jnp.where(zeroth, shifts[yy * 2 + s : yy * 2 + s + 1], shifts[yy * 2 + 1 - s : yy * 2 + 2 - s])
                for s in range(2)
                for yy in range(2)
            ],
            axis=1,
        )
        before = dot_nn(low2[...], w_up) + shift
        half = 0.5 + 0.5 * lax.erf(before * 0.7071067811865476)
        active = (before * half).astype(BF)
        slope = half + before * (jnp.exp(before * before * -0.5) * 0.3989422804014327)
        g_t[...] = active
        w_down = jnp.concatenate([wr[at128(s), :] for s in starts], axis=0)
        du_t[...] = (dot_nt(dyx[...], w_down) * slope).astype(BF)
        tall = dot_nn(g_t[...].T, dyx[...]).astype(BF)
        red.emit_tall(4 * t, tall, 0)
        red.emit_tall(4 * t + 1, tall, QR)
        for e in range(2):
            seats = [e + 2 * (p.core if cc == 0 else 1 - p.core) for cc in range(2)]
            right = jnp.concatenate([du_t[:, at128(s * 128)] for s in seats], axis=1)
            red.emit_wide(4 * t + 2 + e, dot_nn(turned[...], right).astype(BF))
        sums = jnp.sum(du_t[...].astype(F32), axis=0, keepdims=True)
        seat = [sums[:, i * 128 : (i + 1) * 128] for i in range(4)]
        vs[8:12, at128(t * 128)] = jnp.concatenate(
            [
                jnp.where(zeroth, seat[yy + 2 * cc], seat[yy + 2 - 2 * cc])
                for yy in range(2)
                for cc in range(2)
            ],
            axis=0,
        )
        red.tick(2 * t)
        y_sum[...] += dot_nn(g_t[...], w_down)
        h_sum[...] += dot_nt(du_t[...], w_up)
        red.tick(2 * t + 1)

    loop(0, 6, feed)
    reload_wi = pltpu.make_async_copy(wi_ref, w1.at[:, pl.ds(0, 2304)], lsem.at[6])
    reload_wi.start()

    def second(i):
        rows = at256(i * PART)
        value = mid[rows]
        lo[rows] = (value + y_sum[rows] + vec[7:8]).astype(BF)
        hat, scale = norm_parts(value)
        grad = h_sum[rows]
        upstream = dyx[rows].astype(F32)
        vs[5:6] += jnp.sum(grad * hat, axis=0, keepdims=True)
        vs[6:7] += jnp.sum(grad, axis=0, keepdims=True)
        vs[7:8] += jnp.sum(upstream, axis=0, keepdims=True)
        total = upstream + norm_back(hat, scale, vec[5:6], grad)
        mid[rows] = total
        block = total.astype(BF)
        low2[rows] = block
        vs[4:5] += jnp.sum(block.astype(F32), axis=0, keepdims=True)
        d_out[rows] = dot_nt(block, wo[...]).astype(BF)
        turn(rows, att[rows])

    loop(0, 2, second)
    red.tick(12)

    def out_grad(n):
        red.emit_wide(24 + n, dot_nn(turned[...], low2[:, at256(n * 256)]).astype(BF))

    loop(0, 3, out_grad)
    red.tick(13)

    def c_dkv(pair):
        return remote(
            dkv_send.at[lax.rem(pair, 2)], dkv_recv.at[pair], ksend.at[pair], krecv.at[pair], p.to_core
        )

    def settle(pair):
        c_dkv(pair).wait_recv()
        slot = lax.rem(pair, 2)
        for i in range(2):
            total = dkv_own[slot, i] + dkv_recv[pair, i].astype(F32)
            dp[:, at128(768 * (i + 1) + pair * 128)] = total.astype(BF)

    lane_k = lax.broadcasted_iota(jnp.int32, (ROWS, 128), 1)

    def attend_back(pair):
        col = pl.multiple_of(pair * 128, 128)
        slot = lax.rem(pair, 2)
        query = qkv[:, at128(col)]
        extra_q = qaug[...].astype(BF)
        grads = d_out[:, at128(col)]
        outs = att[:, at128(col)].astype(F32)
        three = jnp.where(lane_k < 3, 1.0, 0.0).astype(BF)
        dq = jnp.zeros((128, ROWS), F32)
        dk = [jnp.zeros((ROWS, 128), F32)] * 2
        dv = [jnp.zeros((ROWS, 128), F32)] * 2
        for h in range(2):
            q_h = query * head_mask[h]
            g_h = grads * head_mask[h]
            parts = three_parts(jnp.sum(g_h.astype(F32) * outs, axis=-1, keepdims=True))
            extra_g = jnp.zeros((ROWS, 128), F32)
            for i in range(3):
                extra_g = jnp.where(lane_k == i, -parts[i], extra_g)
            q_wide = jnp.concatenate([q_h, extra_q], axis=1)
            g_wide = jnp.concatenate([g_h, extra_g.astype(BF)], axis=1)
            base = 1 + 3 * (2 * pair + h)
            mark = jnp.where(
                jnp.logical_and(lane_k >= base, lane_k < base + 3), 1.0, 0.0
            ).astype(BF)
            for side in range(2):
                if side == 0:
                    key, value = qkv[:, at128(768 + col)], qkv[:, at128(1536 + col)]
                else:
                    key, value = kvr[:, at128(col)], kvr[:, at128(768 + col)]
                k_wide = jnp.concatenate([key, kaug[pl.ds(side * ROWS, ROWS)] + mark], axis=1)
                v_wide = jnp.concatenate([value, three], axis=1)
                weight = jnp.exp(dot_nt(k_wide, q_wide))
                slope = (weight * dot_nt(v_wide, g_wide)).astype(BF)
                dv[side] = dv[side] + dot_nn(weight.astype(BF), g_h)
                dk[side] = dk[side] + dot_nn(slope, q_h)
                dq = dq + dot_nn((key * head_mask[h]).T, slope)
        dp[:, at128(col)] = (dq.T.astype(BF).astype(F32) * 0.125).astype(BF)

        @pl.when(pair >= 1)
        def _():
            settle(pair - 1)

        @pl.when(pair >= 2)
        def _():
            c_dkv(pair - 2).wait_send()

        dkv_own[slot, 0] = dk[0]
        dkv_own[slot, 1] = dv[0]
        dkv_send[slot, 0] = dk[1].astype(BF)
        dkv_send[slot, 1] = dv[1].astype(BF)
        c_dkv(pair).start()
        red.tick(14 + 2 * pair)
        red.tick(15 + 2 * pair)

    loop(0, 6, attend_back)
    settle(5)
    c_dkv(4).wait_send()
    c_dkv(5).wait_send()

    def turn_first(i):
        rows = at256(i * PART)
        hat, _ = norm_parts(tokx[rows].astype(F32))
        turn(rows, (hat * vec[0:1] + vec[1:2]).astype(BF))

    loop(0, 2, turn_first)

    def in_grad(n):
        red.emit_wide(27 + n, dot_nn(turned[...], dp[:, at256(n * 256)]).astype(BF))
        red.tick(26 + n)

    loop(0, 9, in_grad)
    vs[2:3] = jnp.sum(dp[:, 0:768].astype(F32), axis=0, keepdims=True)
    vs[3:4] = jnp.sum(dp[:, 1536:2304].astype(F32), axis=0, keepdims=True)
    reload_wi.wait()
    c_lo = swap(6, lo.at[pl.ds(PART, PART)], lo_ref.at[p.y], p.to_y)
    keep_lo = pltpu.make_async_copy(lo.at[pl.ds(0, PART)], lo_ref.at[p.y], lsem.at[7])
    keep_lo.start()

    def first_back(i):
        rows = at256(i * PART)
        grad = dot_nt(dp[rows], w1[:, pl.ds(0, 2304)])
        hat, scale = norm_parts(tokx[rows].astype(F32))
        vs[0:1] += jnp.sum(grad * hat, axis=0, keepdims=True)
        vs[1:2] += jnp.sum(grad, axis=0, keepdims=True)
        y_sum[rows] = mid[rows] + norm_back(hat, scale, vec[0:1], grad)

    loop(0, 2, first_back)
    gts[...] = y_sum[pl.ds(PART, PART)].astype(BF)
    c_gt = swap(7, gts, gtr_ref, p.to_y)
    keep_gt = pltpu.make_async_copy(y_sum.at[pl.ds(0, PART)], gto_ref, lsem.at[8])
    keep_gt.start()

    def c_vec(stage, peer):
        return remote(vr.at[2 * stage], vr.at[2 * stage + 1], vsend.at[stage], vrecv.at[stage], peer)

    def vec_pair(stage, peer):
        vr[2 * stage] = vs[...]
        c_vec(stage, peer).start()

    def vec_take(stage, peer):
        c_vec(stage, peer).wait()
        vs[...] += vr[2 * stage + 1]

    vec_pair(0, p.to_core)
    red.tick(35)
    vec_take(0, p.to_core)
    vec_pair(1, p.to_y)
    red.tick(36)
    vec_take(1, p.to_y)
    vec_pair(2, p.to_x)
    red.tick(37)
    vec_take(2, p.to_x)

    @pl.when(p.outer)
    def _():
        vec_pair(3, p.to_mate)

    red.tick(38)

    @pl.when(p.inner)
    def _():
        c_vec(3, p.to_mate).wait_recv()
        vs[...] += vr[7]
        vec_pair(4, p.to_far)

    red.tick(39)

    @pl.when(p.inner)
    def _():
        vec_take(4, p.to_far)
        vec_pair(3, p.to_mate)

    red.tick(40)

    @pl.when(p.outer)
    def _():
        c_vec(3, p.to_mate).wait_recv()
        vs[...] = vr[7]

    c_vec(3, p.to_mate).wait_send()
    c_lo.start()
    c_gt.start()

    def drain(t):
        red.tick(t)

    loop(41, K + LAGS[-1], drain)
    c_tok.wait_send()
    c_row.wait_send()
    c_cot.wait_send()
    c_aug.wait_send()
    c_kv[0].wait_send()
    c_kv[1].wait_send()
    c_lo.wait()
    c_gt.wait()
    keep_lo.wait()
    keep_gt.wait()


def finish_kernel(
    tot_ref, vs, lo_in, gto, gtr_ref,
    lo_out, gt, g0, g1, wi_out, g2, wo_out, g4, g5, g6, we_out, g8, wr_out, g7,
    tot, gtr, gt_s, lo_s, wi, wo, we, wr, in_sem, out_sem,
):
    y = lax.axis_index("frame") // 2
    frame = lax.axis_index("frame")
    spans = [(4 * t, 4) for t in range(6)] + [(24, 3)] + [(27 + 3 * i, 3) for i in range(3)]
    loads = [
        pltpu.make_async_copy(tot_ref.at[pl.ds(k, n)], tot.at[pl.ds(k, n)], in_sem.at[i])
        for i, (k, n) in enumerate(spans)
    ]
    loads += [
        pltpu.make_async_copy(gtr_ref, gtr, in_sem.at[10]),
        pltpu.make_async_copy(gto, gt_s.at[0], in_sem.at[11]),
        pltpu.make_async_copy(lo_in, lo_s, in_sem.at[12]),
    ]
    for one in loads:
        one.start()
    outs = []

    def leave(src, dst):
        one = pltpu.make_async_copy(src, dst, out_sem.at[len(outs)])
        one.start()
        outs.append(one)

    for t in range(6):
        loads[t].wait()
        for hh in range(2):
            for side, to, block, low, high in TALL:
                col = (3 * hh + block) * 128
                wr[t * 128 + low : t * 128 + high, col : col + 128] = tot[
                    4 * t + hh, side, to : to + high - low
                ].astype(F32)
        rows = pl.ds(t * 128, 128)
        leave(wr.at[rows], wr_out.at[rows])
        for j in range(4):
            cols = pl.ds(j * 768 + t * 128, 128)
            we[:, cols] = tot[4 * t + 2 + j // 2, j % 2].astype(F32)
    leave(we, we_out)
    for i, (src, dst) in enumerate([(wo, wo_out)] + [(wi, wi_out)] * 3):
        loads[6 + i].wait()
        base = 24 + 3 * i
        start = 768 * max(i - 1, 0)
        for n in range(3):
            for side in range(2):
                col = start + n * 256 + side * 128
                src[:, col : col + 128] = tot[base + n, side].astype(F32)
        cols = pl.ds(start, 768)
        leave(src.at[:, cols], dst.at[:, cols])
    loads[10].wait()
    gt_s[1] = gtr[...].astype(F32)
    leave(gt_s.at[1], gt.at[1 - y, 0])
    loads[11].wait()
    leave(gt_s.at[0], gt.at[y, 0])
    loads[12].wait()
    leave(lo_s.at[0], lo_out.at[0, 0])
    leave(lo_s.at[1], lo_out.at[1, 0])
    mine = vs[0:8, 0:HR]
    row = vs[8:9]
    for f in range(1, 4):
        mine = jnp.where(frame == f, vs[0:8, f * HR : (f + 1) * HR], mine)
        row = jnp.where(frame == f, vs[8 + f : 9 + f], row)
    g0[...] = mine[0]
    g1[...] = mine[1]
    g2[...] = mine[2:4]
    g4[...] = mine[4]
    g5[...] = mine[5]
    g6[...] = mine[6]
    g7[...] = mine[7]
    g8[...] = row[0]
    for one in outs:
        one.wait()


def local_slice(
    tokens,
    counts,
    first_gain,
    first_bias,
    input_weight,
    input_bias,
    output_weight,
    output_bias,
    second_gain,
    second_bias,
    expand_weight,
    expand_bias,
    reduce_weight,
    reduce_bias,
    cotangent,
):
    anywhere = pl.BlockSpec(memory_space=pl.ANY)
    vmem = pl.BlockSpec(memory_space=pltpu.VMEM)
    smem = pl.BlockSpec(memory_space=pltpu.SMEM)
    shape = jax.ShapeDtypeStruct
    dma = pltpu.SemaphoreType.DMA
    tot, vs, lo, gto, gtr = pl.pallas_call(
        layer_kernel,
        out_shape=(
            shape((K, 2, HR, 128), BF),
            shape((16, D), F32),
            shape((2, PART, D), BF),
            shape((PART, D), F32),
            shape((PART, D), BF),
        ),
        in_specs=[anywhere, anywhere, smem] + [vmem] * 8 + [anywhere] * 4,
        out_specs=(anywhere, vmem, anywhere, anywhere, anywhere),
        scratch_shapes=[
            pltpu.VMEM((K, 2, 2, HR, 128), BF),
            pltpu.VMEM((SLOT_COUNT, 2, 2, HR, 128), BF),
            pltpu.VMEM((K, 2, 2, HR, 128), BF),
            pltpu.VMEM((K, 2, HR, 128), BF),
            pltpu.VMEM((K, HR, 128), BF),
            pltpu.VMEM((K, HR, 128), BF),
            pltpu.VMEM((K, HR, 128), BF),
            pltpu.VMEM((12, D), F32),
            pltpu.VMEM((ROWS, D), BF),
            pltpu.VMEM((ROWS, D), BF),
            pltpu.VMEM((D, FF), BF),
            pltpu.VMEM((D, D), BF),
            pltpu.VMEM((FF, D), BF),
            pltpu.VMEM((ROWS, 3 * D), BF),
            pltpu.VMEM((ROWS, 2 * D), BF),
            pltpu.VMEM((3, 16, PART), BF),
            pltpu.VMEM((2 * ROWS, 128), BF),
            pltpu.VMEM((ROWS, 128), F32),
            pltpu.VMEM((ROWS, D), BF),
            pltpu.VMEM((ROWS, D), F32),
            pltpu.VMEM((ROWS, D), BF),
            pltpu.VMEM((D, ROWS), BF),
            pltpu.VMEM((ROWS, ROWS), BF),
            pltpu.VMEM((ROWS, ROWS), BF),
            pltpu.VMEM((ROWS, D), F32),
            pltpu.VMEM((ROWS, D), F32),
            pltpu.VMEM((ROWS, D), BF),
            pltpu.VMEM((ROWS, 3 * D), BF),
            pltpu.VMEM((2, 2, ROWS, 128), F32),
            pltpu.VMEM((2, 2, ROWS, 128), BF),
            pltpu.VMEM((6, 2, ROWS, 128), BF),
            pltpu.VMEM((ROWS, D), BF),
            pltpu.VMEM((PART, D), BF),
            pltpu.VMEM((10, 16, D), F32),
            dma((7, K)),
            dma((7, K)),
            dma((K,)),
            dma((9,)),
            dma((8,)),
            dma((8,)),
            dma((6,)),
            dma((6,)),
            dma((5,)),
            dma((5,)),
        ],
        compiler_params=pltpu.CompilerParams(
            collective_id=0, has_side_effects=True, vmem_limit_bytes=62 << 20
        ),
    )(
        tokens,
        cotangent,
        counts,
        first_gain,
        first_bias,
        input_bias,
        output_bias,
        second_gain,
        second_bias,
        expand_bias,
        reduce_bias,
        input_weight,
        output_weight,
        expand_weight,
        reduce_weight,
    )
    return pl.pallas_call(
        finish_kernel,
        out_shape=(
            shape((MICRO, 1, PART, D), BF),
            shape((MICRO, 1, PART, D), F32),
            shape((HR,), F32),
            shape((HR,), F32),
            shape((HR, 3 * D), F32),
            shape((2, HR), F32),
            shape((HR, D), F32),
            shape((HR,), F32),
            shape((HR,), F32),
            shape((HR,), F32),
            shape((HR, FF), F32),
            shape((D,), F32),
            shape((D, D), F32),
            shape((HR,), F32),
        ),
        in_specs=[anywhere, vmem, anywhere, anywhere, anywhere],
        out_specs=tuple(anywhere if i in (0, 1, 4, 6, 10, 12) else vmem for i in range(14)),
        scratch_shapes=[
            pltpu.VMEM((K, 2, HR, 128), BF),
            pltpu.VMEM((PART, D), BF),
            pltpu.VMEM((2, PART, D), F32),
            pltpu.VMEM((2, PART, D), BF),
            pltpu.VMEM((HR, 3 * D), F32),
            pltpu.VMEM((HR, D), F32),
            pltpu.VMEM((HR, FF), F32),
            pltpu.VMEM((D, D), F32),
            dma((13,)),
            dma((16,)),
        ],
        compiler_params=pltpu.CompilerParams(vmem_limit_bytes=62 << 20),
    )(tot, vs, lo, gto, gtr)


def solution(mesh):
    fits = mesh.shape["clip"] == 8 and mesh.shape["frame"] == 4
    return jax.shard_map(
        local_slice if fits else local,
        mesh=mesh,
        in_specs=(
            P(None, "clip", "frame", None),
            P(None, "clip", "frame"),
            P(),
            P(),
            P(),
            P(),
            P(),
            P(),
            P(),
            P(),
            P(),
            P(),
            P(),
            P(),
            P(None, "clip", "frame", None),
        ),
        out_specs=(
            P(None, "clip", "frame", None),
            P(None, "clip", "frame", None),
            P("frame"),
            P("frame"),
            P("frame", None),
            P(None, "frame"),
            P("frame", None),
            P("frame"),
            P("frame"),
            P("frame"),
            P("frame", None),
            P("frame"),
            P("frame", None),
            P("frame"),
        ),
        check_vma=False,
    )
```

```python
import jax
import jax.numpy as jnp
from jax import lax
from jax.experimental import pallas as pl
from jax.experimental.pallas import tpu as pltpu
from jax.sharding import PartitionSpec as P

D = 768
H = 12
HD = 64
MICRO = 2
FRAME_DEV = 4
SLOTS = 64
BLOCK = 256


epsilon = 1e-06


def from_behind(block, axis, distance):
    devices = range(lax.axis_size(axis))
    route = [((i - distance) % len(devices), i) for i in devices]
    return lax.ppermute(block, axis, route)


def norm_rows(values, gain, shift):
    mean = jnp.mean(values, axis=-1, keepdims=True)
    centred = values - mean
    spread = jnp.mean(centred * centred, axis=-1, keepdims=True)
    return centred * lax.rsqrt(spread + epsilon) * gain + shift


def gelu_exact(values):
    return jax.nn.gelu(values, approximate=False)


def key_valid(every_count, source):
    frame_counts = lax.dynamic_slice_in_dim(every_count, source * FRAME_DEV, FRAME_DEV, 1)
    slot_index = jnp.arange(SLOTS, dtype=jnp.int32)
    return (slot_index[None, None, :] < frame_counts[:, :, None]).reshape(MICRO, BLOCK)


def scores_of(query, keys, valid):
    key_heads = keys.reshape(MICRO, BLOCK, H, HD)
    scores = jnp.einsum("mqhd,mkhd->mhqk", query, key_heads, preferred_element_type=jnp.float32)
    return jnp.where(valid[:, None, None, :], scores, -1e30)


def absorb(state, query, keys, values, valid):
    top, total, summed = state
    scores = scores_of(query, keys, valid)
    new_top = jnp.maximum(top, jnp.max(scores, axis=-1, keepdims=True))
    factor = jnp.exp(top - new_top)
    lifted = jnp.exp(scores - new_top)
    total = total * factor + jnp.sum(lifted, axis=-1, keepdims=True)
    value_heads = values.reshape(MICRO, BLOCK, H, HD)
    summed = summed * factor + jnp.einsum(
        "mhqk,mkhd->mhqd",
        lifted.astype(jnp.bfloat16),
        value_heads,
        preferred_element_type=jnp.float32,
    )
    return (new_top, total, summed)


def block_back(query, keys, values, valid, log_total, delta, grad_heads):
    scores = scores_of(query, keys, valid)
    weights = jnp.exp(scores - log_total)
    key_heads = keys.reshape(MICRO, BLOCK, H, HD)
    value_heads = values.reshape(MICRO, BLOCK, H, HD)
    grad_weights = jnp.einsum(
        "mqhd,mkhd->mhqk", grad_heads, value_heads, preferred_element_type=jnp.float32
    )
    grad_scores = (weights * (grad_weights - delta)).astype(jnp.bfloat16)
    grad_query = jnp.einsum(
        "mhqk,mkhd->mqhd", grad_scores, key_heads, preferred_element_type=jnp.float32
    )
    grad_keys = jnp.einsum(
        "mhqk,mqhd->mkhd", grad_scores, query, preferred_element_type=jnp.float32
    )
    grad_values = jnp.einsum(
        "mhqk,mqhd->mkhd",
        weights.astype(jnp.bfloat16),
        grad_heads,
        preferred_element_type=jnp.float32,
    )
    return (grad_query, grad_keys.reshape(MICRO, BLOCK, D), grad_values.reshape(MICRO, BLOCK, D))


def local(
    tokens,
    counts,
    first_gain,
    first_bias,
    input_weight,
    input_bias,
    output_weight,
    output_bias,
    second_gain,
    second_bias,
    expand_weight,
    expand_bias,
    reduce_weight,
    reduce_bias,
    cotangent,
):
    members = lax.axis_size("frame")
    myself = lax.axis_index("frame")
    total_rows = MICRO * BLOCK
    seq_in = tokens.reshape(total_rows, D).astype(jnp.float32)
    every_count = lax.all_gather(counts.reshape(MICRO, FRAME_DEV), "frame", axis=1, tiled=True)
    gain_one = first_gain.astype(jnp.float32)
    shift_one = first_bias.astype(jnp.float32)
    gain_two = second_gain.astype(jnp.float32)
    shift_two = second_bias.astype(jnp.float32)
    qv_bias = input_bias.astype(jnp.float32)
    first_low = norm_rows(seq_in, gain_one, shift_one).astype(jnp.bfloat16)
    projected = jnp.dot(first_low, input_weight, preferred_element_type=jnp.float32)
    query = (
        ((projected[:, :D] + qv_bias[0]) * 0.125).astype(jnp.bfloat16).reshape(MICRO, BLOCK, H, HD)
    )
    keys = projected[:, D : 2 * D].astype(jnp.bfloat16).reshape(MICRO, BLOCK, D)
    values = (projected[:, 2 * D :] + qv_bias[1]).astype(jnp.bfloat16).reshape(MICRO, BLOCK, D)
    start = (
        jnp.full((MICRO, H, BLOCK, 1), -1e30, jnp.float32),
        jnp.zeros((MICRO, H, BLOCK, 1), jnp.float32),
        jnp.zeros((MICRO, H, BLOCK, HD), jnp.float32),
    )
    state = absorb(start, query, keys, values, key_valid(every_count, myself))
    stored = ()

    def forward_hop(step, carry):
        state_now, moving, kept = carry
        moving = from_behind((moving[0], moving[1]), "frame", 1)
        source = (myself - step) % members
        state_now = absorb(state_now, query, moving[0], moving[1], key_valid(every_count, source))
        return (state_now, moving, kept)

    state, _, stored = lax.fori_loop(1, members, forward_hop, (state, (keys, values), stored))
    top, total, summed = state
    log_total = top + jnp.log(total)
    attend_full = jnp.transpose(summed / total, (0, 2, 1, 3))
    attend_low = attend_full.reshape(total_rows, D).astype(jnp.bfloat16)
    middle = (
        seq_in
        + jnp.dot(attend_low, output_weight, preferred_element_type=jnp.float32)
        + output_bias.astype(jnp.float32)
    )
    second_low = norm_rows(middle, gain_two, shift_two).astype(jnp.bfloat16)
    before = jnp.dot(
        second_low, expand_weight, preferred_element_type=jnp.float32
    ) + expand_bias.astype(jnp.float32)
    active_low = gelu_exact(before).astype(jnp.bfloat16)
    result = (
        middle
        + jnp.dot(active_low, reduce_weight, preferred_element_type=jnp.float32)
        + reduce_bias.astype(jnp.float32)
    )
    layer_out = result.astype(jnp.bfloat16).reshape(MICRO, 1, BLOCK, D)
    upstream_low = cotangent.reshape(total_rows, D)
    upstream = upstream_low.astype(jnp.float32)
    grad_reduce_weight = jnp.dot(active_low.T, upstream_low, preferred_element_type=jnp.float32)
    grad_reduce_bias = jnp.sum(upstream, axis=0)
    grad_active = jnp.dot(upstream_low, reduce_weight.T, preferred_element_type=jnp.float32)
    _, gelu_back = jax.vjp(gelu_exact, before)
    grad_before = gelu_back(grad_active)[0].astype(jnp.bfloat16)
    grad_expand_weight = jnp.dot(second_low.T, grad_before, preferred_element_type=jnp.float32)
    grad_expand_bias = jnp.sum(grad_before.astype(jnp.float32), axis=0)
    grad_second = jnp.dot(grad_before, expand_weight.T, preferred_element_type=jnp.float32)
    _, second_back = jax.vjp(norm_rows, middle, gain_two, shift_two)
    middle_part, grad_second_gain, grad_second_bias = second_back(grad_second)
    grad_middle = upstream + middle_part
    grad_branch = grad_middle.astype(jnp.bfloat16)
    grad_output_weight = jnp.dot(attend_low.T, grad_branch, preferred_element_type=jnp.float32)
    grad_output_bias = jnp.sum(grad_branch.astype(jnp.float32), axis=0)
    grad_attend = jnp.dot(grad_branch, output_weight.T, preferred_element_type=jnp.float32).astype(
        jnp.bfloat16
    )
    grad_heads = grad_attend.reshape(MICRO, BLOCK, H, HD)
    delta = jnp.transpose(
        jnp.sum(grad_heads.astype(jnp.float32) * attend_full, axis=-1), (0, 2, 1)
    )[..., None]
    first_terms = block_back(
        query, keys, values, key_valid(every_count, myself), log_total, delta, grad_heads
    )

    def backward_hop(step, carry):
        grad_query, running, moving = carry
        running = (
            from_behind(running[0].astype(jnp.bfloat16), "frame", 1).astype(jnp.float32),
            from_behind(running[1].astype(jnp.bfloat16), "frame", 1).astype(jnp.float32),
        )
        current = from_behind((moving[0], moving[1]), "frame", 1)
        source = (myself - step) % members
        add_query, add_keys, add_values = block_back(
            query,
            current[0],
            current[1],
            key_valid(every_count, source),
            log_total,
            delta,
            grad_heads,
        )
        return (grad_query + add_query, (running[0] + add_keys, running[1] + add_values), current)

    grad_query, running, _ = lax.fori_loop(
        1, members, backward_hop, (first_terms[0], (first_terms[1], first_terms[2]), (keys, values))
    )
    finished = (
        from_behind(running[0].astype(jnp.bfloat16), "frame", 1).astype(jnp.float32),
        from_behind(running[1].astype(jnp.bfloat16), "frame", 1).astype(jnp.float32),
    )
    query_low = grad_query.astype(jnp.bfloat16).reshape(total_rows, D) * 0.125
    keys_low = finished[0].astype(jnp.bfloat16).reshape(total_rows, D)
    values_low = finished[1].astype(jnp.bfloat16).reshape(total_rows, D)
    grad_projected = jnp.concatenate([query_low, keys_low, values_low], axis=1)
    grad_input_weight = jnp.dot(first_low.T, grad_projected, preferred_element_type=jnp.float32)
    grad_input_bias = jnp.stack(
        [
            jnp.sum(query_low.astype(jnp.float32), axis=0),
            jnp.sum(values_low.astype(jnp.float32), axis=0),
        ]
    )
    grad_first = jnp.dot(grad_projected, input_weight.T, preferred_element_type=jnp.float32)
    _, first_back = jax.vjp(norm_rows, seq_in, gain_one, shift_one)
    input_part, grad_first_gain, grad_first_bias = first_back(grad_first)
    grad_tokens = (grad_middle + input_part).reshape(MICRO, 1, BLOCK, D)
    shares = (
        lax.psum_scatter(
            grad_first_gain.astype(jnp.bfloat16), "frame", scatter_dimension=0, tiled=True
        ).astype(jnp.float32),
        lax.psum_scatter(
            grad_first_bias.astype(jnp.bfloat16), "frame", scatter_dimension=0, tiled=True
        ).astype(jnp.float32),
        lax.psum_scatter(
            grad_input_weight.astype(jnp.bfloat16), "frame", scatter_dimension=0, tiled=True
        ).astype(jnp.float32),
        lax.psum_scatter(
            grad_input_bias.astype(jnp.bfloat16), "frame", scatter_dimension=1, tiled=True
        ).astype(jnp.float32),
        lax.psum_scatter(
            grad_output_weight.astype(jnp.bfloat16), "frame", scatter_dimension=0, tiled=True
        ).astype(jnp.float32),
        lax.psum_scatter(
            grad_output_bias.astype(jnp.bfloat16), "frame", scatter_dimension=0, tiled=True
        ).astype(jnp.float32),
        lax.psum_scatter(
            grad_second_gain.astype(jnp.bfloat16), "frame", scatter_dimension=0, tiled=True
        ).astype(jnp.float32),
        lax.psum_scatter(
            grad_second_bias.astype(jnp.bfloat16), "frame", scatter_dimension=0, tiled=True
        ).astype(jnp.float32),
        lax.psum_scatter(
            grad_expand_weight.astype(jnp.bfloat16), "frame", scatter_dimension=0, tiled=True
        ).astype(jnp.float32),
        lax.psum_scatter(
            grad_expand_bias.astype(jnp.bfloat16), "frame", scatter_dimension=0, tiled=True
        ).astype(jnp.float32),
        lax.psum_scatter(
            grad_reduce_weight.astype(jnp.bfloat16), "frame", scatter_dimension=0, tiled=True
        ).astype(jnp.float32),
        lax.psum_scatter(
            grad_reduce_bias.astype(jnp.bfloat16), "frame", scatter_dimension=0, tiled=True
        ).astype(jnp.float32),
    )
    totals = (
        lax.psum(shares[0].astype(jnp.bfloat16), "clip").astype(jnp.float32),
        lax.psum(shares[1].astype(jnp.bfloat16), "clip").astype(jnp.float32),
        lax.psum(shares[2].astype(jnp.bfloat16), "clip").astype(jnp.float32),
        lax.psum(shares[3].astype(jnp.bfloat16), "clip").astype(jnp.float32),
        lax.psum(shares[4].astype(jnp.bfloat16), "clip").astype(jnp.float32),
        lax.psum(shares[5].astype(jnp.bfloat16), "clip").astype(jnp.float32),
        lax.psum(shares[6].astype(jnp.bfloat16), "clip").astype(jnp.float32),
        lax.psum(shares[7].astype(jnp.bfloat16), "clip").astype(jnp.float32),
        lax.psum(shares[8].astype(jnp.bfloat16), "clip").astype(jnp.float32),
        lax.psum(shares[9].astype(jnp.bfloat16), "clip").astype(jnp.float32),
        lax.psum(shares[10].astype(jnp.bfloat16), "clip").astype(jnp.float32),
        lax.psum(shares[11].astype(jnp.bfloat16), "clip").astype(jnp.float32),
    )
    return (
        layer_out,
        grad_tokens,
        totals[0],
        totals[1],
        totals[2],
        totals[3],
        totals[4],
        totals[5],
        totals[6],
        totals[7],
        totals[8],
        totals[9],
        totals[10],
        totals[11],
    )


MESH = pl.DeviceIdType.MESH
BF = jnp.bfloat16
F32 = jnp.float32
K = 18
QR = 768
HR = 384
CR = 192
SLOT_COUNT = 4
ROWS = 512
PART = 256
FF = 3072
LOW = -1e30
COLUMNS = (0, 1, 2, 3, 4, 5, 0, 1, 6, 7, 12, 13, 2, 3, 8, 9, 14, 15, 4, 5, 10, 11, 16, 17)
WAYS = "accbabbccbabccbaaa"
FEED_STEPS = (((), (), (101, 102), (104,), (200, 106), (203, 108, 204, 109)), ((), (100,), (103,), (105,), (201, 107), (202,)))
NORM_STEPS = ((301, 205, 110), (111,))
OUT_STEPS = (300, 303, 207)
ATTEND_STEPS = (((302,), (208,), (403,), (503, 308, 212, 405, 211), (505, 406, 408), (504, 309, 213)), ((), (304,), (307, 209), (402,), (502,), ()), ((112,), (400,), (401,), (600, 404, 113, 114), (), (312, 605, 410, 601, 506, 214, 115)), ((305, 206), (210,), (500, 306), (501, 310, 603, 407), (), (507, 311, 508)))
PROJECT_STEPS = (602, 604, 313)
LAST_STEPS = ((510, 409, 412, 314, 116), (606, 607, 608, 411, 117))
DRAIN_STEPS = (215, 509, 610, 0, 413, 512, 216, 414, 1, 511, 315, 2, 217, 514, 609, 3, 612, 513, 415, 316, 4, 611, 317, 5, 614, 515, 416, 613, 417, 615, 516, 517, 616, 617)


def dot_nn(a, b):
    return lax.dot_general(a, b, (((1,), (0,)), ((), ())), preferred_element_type=F32)


def dot_nt(a, b):
    return lax.dot_general(a, b, (((1,), (1,)), ((), ())), preferred_element_type=F32)


def dot_tn(a, b):
    return lax.dot_general(a, b, (((0,), (0,)), ((), ())), preferred_element_type=F32)


def at128(index):
    return pl.ds(pl.multiple_of(index, 128), 128)


def at256(index):
    return pl.ds(pl.multiple_of(index, 256), 256)


def loop(low, high, body):
    def step(i, carry):
        body(i)
        return carry

    lax.fori_loop(low, high, step, 0)


class Place:
    def __init__(self):
        self.clip = lax.axis_index("clip")
        self.frame = lax.axis_index("frame")
        self.x = lax.rem(self.clip, 2)
        self.z = self.clip // 2
        self.core = lax.rem(self.frame, 2)
        self.y = self.frame // 2
        self.outer = jnp.logical_or(self.z == 0, self.z == 3)
        self.inner = jnp.logical_not(self.outer)
        self.to_core = (self.clip, self.y * 2 + (1 - self.core))
        self.to_y = (self.clip, (1 - self.y) * 2 + self.core)
        self.to_x = (self.z * 2 + (1 - self.x), self.frame)
        mate = self.z + 1 - 2 * lax.rem(self.z, 2)
        self.to_mate = (mate * 2 + self.x, self.frame)
        self.to_far = ((3 - self.z) * 2 + self.x, self.frame)
        self.h = jnp.where(self.inner, 1, 0)

    def seat(self, quarter):
        yy, cc = quarter // 2, quarter % 2
        return yy + 2 * (self.core if cc == 0 else 1 - self.core)


def enter(place):
    barrier = pltpu.get_barrier_semaphore()
    for peer in (place.to_core, place.to_y, place.to_x, place.to_mate, place.to_far):
        pl.semaphore_signal(barrier, inc=1, device_id=peer, device_id_type=MESH)
    pl.semaphore_wait(barrier, 5)


def remote(src, dst, send, recv, peer):
    return pltpu.make_async_remote_copy(
        src_ref=src, dst_ref=dst, send_sem=send, recv_sem=recv, device_id=peer, device_id_type=MESH
    )


class Reduce:
    def __init__(self, place, bufs, tot, csend, send, recv):
        self.p = place
        self.own, self.nbr, self.rc, self.ry, self.rx, self.r1, self.r2 = bufs
        self.tot, self.csend, self.send, self.recv = tot, csend, send, recv

    def copy(self, src, dst, kind, stage, k, peer):
        return remote(src, dst, self.send.at[kind], self.recv.at[stage, k], peer)

    def last(self, src, dst, kind, end, peer):
        return remote(src, dst, self.send.at[kind], self.send.at[end], peer)

    def part(self, far):
        return pl.ds(pl.multiple_of((1 - self.p.x if far else self.p.x) * CR, CR), CR)

    def c_core(self, k):
        slot = self.seat(k)
        return remote(self.nbr.at[slot], self.rc.at[k], self.csend.at[slot], self.recv.at[0, k], self.p.to_core)

    def a_y(self, k):
        return self.copy(self.own.at[k, 1 - self.p.y], self.ry.at[k], 0, 1, k, self.p.to_y)

    def a_x(self, k):
        return self.copy(self.own.at[k, self.p.y, 1 - self.p.x], self.rx.at[k], 1, 2, k, self.p.to_x)

    def b_x(self, k):
        return self.copy(self.own.at[k, :, 1 - self.p.x], self.ry.at[k], 0, 1, k, self.p.to_x)

    def b_y(self, k):
        return self.copy(self.own.at[k, 1 - self.p.y, self.p.x], self.rx.at[k], 1, 2, k, self.p.to_y)

    def half(self, k):
        return self.own.at[k, self.p.y, self.p.x]

    def l_in(self, k):
        return self.copy(self.half(k), self.r1.at[k], 2, 3, k, self.p.to_mate)

    def l_mid(self, k):
        return self.copy(self.half(k), self.r2.at[k], 3, 4, k, self.p.to_far)

    def l_out(self, k):
        return self.copy(self.r2.at[k], self.r1.at[k], 2, 3, k, self.p.to_mate)

    def l_leave(self, k, inner):
        src = self.r2 if inner else self.r1
        self.last(src.at[k], self.tot.at[k, self.p.x], 4, 5, self.p.to_x).start()
        self.keep(src.at[k], self.tot.at[k, self.p.x]).start()

    def q_pair(self, k):
        return self.copy(self.own.at[k, :, 1 - self.p.h], self.ry.at[k], 0, 1, k, self.p.to_mate)

    def q_y(self, k):
        return self.copy(self.own.at[k, 1 - self.p.y, self.p.h], self.rx.at[k], 1, 2, k, self.p.to_y)

    def q_x(self, k):
        src = self.own.at[k, self.p.y, self.p.h, self.part(True)]
        return self.copy(src, self.r1.at[k, pl.ds(0, CR)], 6, 3, k, self.p.to_x)

    def q_far(self, k):
        src = self.own.at[k, self.p.y, self.p.h, self.part(False)]
        return self.copy(src, self.r1.at[k, pl.ds(CR, CR)], 7, 4, k, self.p.to_far)

    def q_gather(self, k):
        both = self.r2.at[k, self.part(False)]
        return self.copy(both, both, 8, 5, k, self.p.to_x)

    def q_leave(self, k):
        self.last(self.r2.at[k], self.tot.at[k, self.p.h], 9, 10, self.p.to_mate).start()
        self.keep(self.r2.at[k], self.tot.at[k, self.p.h]).start()

    def keep(self, src, dst):
        return pltpu.make_async_copy(src, dst, self.send.at[11])

    def split(self, k, a, b, c):
        {"a": a, "b": b, "c": c}[WAYS[k]](k)

    def seat(self, k):
        return k % SLOT_COUNT if isinstance(k, int) else lax.rem(k, SLOT_COUNT)

    def slot(self, k):
        if isinstance(k, int):
            self.c_core(k - SLOT_COUNT).wait_send()
        else:
            pl.when(k >= SLOT_COUNT)(lambda: self.c_core(k - SLOT_COUNT).wait_send())

    def put_wide(self, k, side, grad):
        slot = self.seat(k)
        for yy in range(2):
            for i in range(2):
                rows = slice(i * CR, (i + 1) * CR)
                cols = slice(i * 128, (i + 1) * 128)
                self.own[k, yy, side, rows] = grad[yy * CR : (yy + 1) * CR, cols]
                self.nbr[slot, yy, side, rows] = grad[(2 + yy) * CR : (3 + yy) * CR, cols]

    def put_tall(self, k, grad):
        slot = self.seat(k)
        for yy in range(2):
            for i in range(6):
                rows = slice(i % 3 * 128, (i % 3 + 1) * 128)
                cols = slice(i * 128, (i + 1) * 128)
                self.own[k, yy, i // 3, rows] = grad[yy * 128 : (yy + 1) * 128, cols]
                self.nbr[slot, yy, i // 3, rows] = grad[(2 + yy) * 128 : (3 + yy) * 128, cols]

    def stage_1(self, k):
        self.c_core(k).wait_recv()
        self.own[k] = self.own[k] + self.rc[k]
        self.split(
            k,
            lambda k: self.a_y(k).start(),
            lambda k: self.b_x(k).start(),
            lambda k: self.q_pair(k).start(),
        )

    def stage_2(self, k):
        self.a_y(k).wait_recv()

        def a(k):
            self.own[k, self.p.y] = self.own[k, self.p.y] + self.ry[k]
            self.a_x(k).start()

        def b(k):
            self.own[k, :, self.p.x] = self.own[k, :, self.p.x] + self.ry[k]
            self.b_y(k).start()

        def c(k):
            self.own[k, :, self.p.h] = self.own[k, :, self.p.h] + self.ry[k]
            self.q_y(k).start()

        self.split(k, a, b, c)

    def stage_3(self, k):
        self.a_x(k).wait_recv()

        def line(k):
            self.own[k, self.p.y, self.p.x] = self.own[k, self.p.y, self.p.x] + self.rx[k]
            pl.when(self.p.outer)(lambda: self.l_in(k).start())

        def c(k):
            self.own[k, self.p.y, self.p.h] = self.own[k, self.p.y, self.p.h] + self.rx[k]
            self.q_x(k).start()

        self.split(k, line, line, c)

    def stage_4(self, k):
        def line(k):
            @pl.when(self.p.inner)
            def _():
                self.l_in(k).wait_recv()
                self.own[k, self.p.y, self.p.x] = self.own[k, self.p.y, self.p.x] + self.r1[k]
                self.l_mid(k).start()

        def c(k):
            self.q_x(k).wait_recv()
            mine = self.own.at[k, self.p.y, self.p.h, self.part(False)]
            mine[...] = mine[...] + self.r1[k, pl.ds(0, CR)]
            self.q_far(k).start()

        self.split(k, line, line, c)

    def stage_5(self, k):
        def line(k):
            @pl.when(self.p.inner)
            def _():
                self.l_mid(k).wait_recv()
                self.r2[k] = self.r2[k] + self.own[k, self.p.y, self.p.x]
                self.l_out(k).start()
                self.l_leave(k, True)

        def c(k):
            self.q_far(k).wait_recv()
            mine = self.own.at[k, self.p.y, self.p.h, self.part(False)]
            self.r2[k, self.part(False)] = mine[...] + self.r1[k, pl.ds(CR, CR)]
            self.q_gather(k).start()

        self.split(k, line, line, c)

    def stage_6(self, k):
        def line(k):
            @pl.when(self.p.outer)
            def _():
                self.l_in(k).wait_recv()
                self.l_leave(k, False)

        def c(k):
            self.q_gather(k).wait_recv()
            self.q_leave(k)

        self.split(k, line, line, c)

    def close(self):
        rest = WAYS.count("c")
        line = K - rest
        peer = self.p.to_x

        def whole(ref, count, kind):
            span = ref.at[pl.ds(0, count)]
            return remote(span, span, self.send.at[kind], self.send.at[kind], peer)

        def parts(kind):
            span = self.r1.at[pl.ds(0, rest), pl.ds(0, CR)]
            return remote(span, span, self.send.at[kind], self.send.at[kind], peer)

        for k in range(K - SLOT_COUNT, K):
            self.c_core(k).wait_send()
        whole(self.ry, K, 0).wait_send()
        whole(self.rx, K, 1).wait_send()
        whole(self.r1, line, 2).wait_send()
        pl.when(self.p.inner)(lambda: whole(self.r1, line, 3).wait_send())
        whole(self.r1, line, 4).wait_send()
        whole(self.r1, line, 5).wait_recv()
        parts(6).wait_send()
        parts(7).wait_send()
        parts(8).wait_send()
        whole(self.r1, rest, 9).wait_send()
        whole(self.r1, rest, 10).wait_recv()
        pltpu.make_async_copy(self.r1, self.r2, self.send.at[11]).wait()

    def run(self, steps):
        stages = (self.stage_1, self.stage_2, self.stage_3, self.stage_4, self.stage_5, self.stage_6)
        for step in steps:
            stages[step // 100 - 1](step % 100)

    def run_at(self, index, table):
        for i, steps in enumerate(table):
            if steps:
                pl.when(index == i)(lambda steps=steps: self.run(steps))


def norm_parts(values):
    mean = jnp.mean(values, axis=-1, keepdims=True)
    centred = values - mean
    spread = jnp.mean(centred * centred, axis=-1, keepdims=True)
    scale = lax.rsqrt(spread + epsilon)
    return centred * scale, scale


def norm_back(hat, scale, gain, grad):
    lifted = grad * gain
    level = jnp.mean(lifted, axis=-1, keepdims=True)
    slope = jnp.mean(lifted * hat, axis=-1, keepdims=True)
    return scale * (lifted - level - hat * slope)


def three_parts(values):
    high = values.astype(BF).astype(F32)
    rest = values - high
    middle = rest.astype(BF).astype(F32)
    return high, middle, rest - middle


def layer_kernel(
    tok_ref, cot_ref, cnt_ref, fg_ref, fb_ref, ib_ref, ob_ref, sg_ref, sb_ref, eb_ref, rb_ref,
    wi_ref, wo_ref, we_ref, wr_ref,
    tot_ref, vs, lo_ref, gto_ref, gtr_ref,
    own, nbr, rc, ry, rx, r1, r2, vec,
    tokx, dyx, w1, wo, wr, qkv, kvr, rowb, kaug, qaug, att, mid, low2, turned, g_t, du_t, y_sum, h_sum,
    d_out, dp, dq_sum, dkv_own, dkv_far, dkv_send, dkv_recv, lo, gts, vr,
    csend, send, recv, lsem, xsend, xrecv, ksend, krecv, vsend, vrecv,
):
    p = Place()
    loads = [
        pltpu.make_async_copy(tok_ref.at[p.y, 0], tokx.at[pl.ds(0, PART)], lsem.at[0]),
        pltpu.make_async_copy(wi_ref, w1.at[:, pl.ds(0, 2304)], lsem.at[1]),
        pltpu.make_async_copy(cot_ref.at[p.y, 0], dyx.at[pl.ds(0, PART)], lsem.at[2]),
        pltpu.make_async_copy(wo_ref, wo, lsem.at[3]),
        pltpu.make_async_copy(wr_ref, wr, lsem.at[4]),
    ]
    for one in loads:
        one.start()
    enter(p)
    red = Reduce(p, (own, nbr, rc, ry, rx, r1, r2), tot_ref, csend, send, recv)

    def swap(index, src, dst, peer):
        return remote(src, dst, xsend.at[index], xrecv.at[index], peer)

    c_tok = swap(0, tok_ref.at[1 - p.y, 0], tokx.at[pl.ds(PART, PART)], p.to_y)
    c_cot = swap(1, cot_ref.at[1 - p.y, 0], dyx.at[pl.ds(PART, PART)], p.to_y)
    c_row = swap(2, rowb.at[2], rowb.at[1], p.to_y)
    c_aug = swap(3, kaug.at[pl.ds(0, ROWS)], kaug.at[pl.ds(ROWS, ROWS)], p.to_core)
    c_kv = [
        swap(4 + r, qkv.at[pl.ds(r * PART, PART), pl.ds(768, 1536)], kvr.at[pl.ds(r * PART, PART)], p.to_core)
        for r in range(2)
    ]
    c_tok.start()

    for row, ref in ((0, fg_ref), (1, fb_ref), (4, ob_ref), (5, sg_ref), (6, sb_ref), (7, rb_ref)):
        vec[row : row + 1] = ref[...].astype(F32).reshape(1, D)
    vec[2:4] = ib_ref[...].astype(F32)
    for f in range(4):
        vec[8 + f : 9 + f] = eb_ref[f * D : (f + 1) * D].astype(F32).reshape(1, D)

    lane = lax.broadcasted_iota(jnp.int32, (16, PART), 1)

    def bias_row(m):
        frame = lane // SLOTS
        kept = jnp.zeros_like(lane)
        for j in range(FRAME_DEV):
            kept = jnp.where(frame == j, cnt_ref[m, 0, j], kept)
        return jnp.where(lane - frame * SLOTS < kept, 0.0, LOW).astype(BF)

    rowb[0] = bias_row(p.y)
    rowb[2] = bias_row(1 - p.y)
    c_row.start()
    pick = jnp.where(
        jnp.logical_and(
            lax.broadcasted_iota(jnp.int32, (16, 128), 0) == 0,
            lax.broadcasted_iota(jnp.int32, (16, 128), 1) == 0,
        ),
        1.0,
        0.0,
    ).astype(BF)
    kaug[pl.ds(0, PART)] = dot_tn(rowb[0], pick).astype(BF)
    lane_q = lax.broadcasted_iota(jnp.int32, (PART, 128), 1)
    lane_row = lax.broadcasted_iota(jnp.int32, (1, 128), 1)
    head_mask = [
        jnp.where((lane_row < 64) == (h == 0), 1.0, 0.0).astype(BF) for h in range(2)
    ]
    qaug[...] = jnp.where(lax.broadcasted_iota(jnp.int32, (ROWS, 128), 1) == 0, 1.0, 0.0)
    vs[...] = jnp.zeros_like(vs)

    def project(r):
        rows = pl.ds(r * PART, PART)
        hat, _ = norm_parts(tokx[rows].astype(F32))
        low2[rows] = (hat * vec[0:1] + vec[1:2]).astype(BF)

        def column(j):
            col = pl.multiple_of(j * 256, 256)
            part = lax.rem(j, 3) * 256
            shift = jnp.where(
                j < 3, vec[2:3, at256(part)], jnp.where(j >= 6, vec[3:4, at256(part)], 0.0)
            )
            value = dot_nn(low2[rows], w1[:, pl.ds(col, 256)]) + shift
            qkv[rows, pl.ds(col, 256)] = (value * jnp.where(j < 3, 0.125, 1.0)).astype(BF)

        loop(3, 9, column)
        c_kv[r].start()
        loop(0, 3, column)

    loads[0].wait()
    loads[1].wait()
    project(0)
    c_tok.wait_recv()
    c_row.wait_recv()
    c_cot.start()
    kaug[pl.ds(PART, PART)] = dot_tn(rowb[1], pick).astype(BF)
    c_aug.start()
    project(1)
    load_we = pltpu.make_async_copy(we_ref, w1, lsem.at[5])
    load_we.start()
    c_kv[0].wait_recv()
    c_kv[1].wait_recv()
    c_aug.wait_recv()

    def attend(pair):
        col = pl.multiple_of(pair * 128, 128)
        ones = jnp.ones((ROWS, 128), BF)
        first = jnp.where(lane_q == 0, 1.0, 0.0).astype(BF)
        k_here = jnp.concatenate([qkv[:, at128(768 + col)], kaug[pl.ds(0, ROWS)]], axis=1)
        k_there = jnp.concatenate([kvr[:, at128(col)], kaug[pl.ds(ROWS, ROWS)]], axis=1)
        v_here = jnp.concatenate([qkv[:, at128(1536 + col)], ones], axis=1)
        v_there = jnp.concatenate([kvr[:, at128(768 + col)], ones], axis=1)
        for block in range(2):
            rows = pl.ds(block * PART, PART)
            query = qkv[rows, at128(col)]
            extra = qaug[rows]
            outs = []
            for h in range(2):
                lifted = jnp.concatenate([query * head_mask[h], first], axis=1)
                s_here = dot_nt(lifted, k_here)
                s_there = dot_nt(lifted, k_there)
                top = jnp.maximum(
                    jnp.max(s_here, axis=-1, keepdims=True), jnp.max(s_there, axis=-1, keepdims=True)
                )
                e_here = jnp.exp(s_here - top).astype(BF)
                e_there = jnp.exp(s_there - top).astype(BF)
                both = dot_nn(e_here, v_here) + dot_nn(e_there, v_there)
                total = both[:, 128:]
                outs.append(both[:, :128] / total)
                parts = three_parts(top + jnp.log(total))
                base = 1 + 3 * (2 * pair + h)
                for i in range(3):
                    extra = jnp.where(lane_q == base + i, -parts[i], extra)
            qaug[rows] = extra
            att[rows, at128(col)] = jnp.where(lane_q < 64, outs[0], outs[1]).astype(BF)

    loop(0, 6, attend)

    def turn(rows, block):
        flipped = block.T
        for quarter in range(4):
            seat = pl.multiple_of(p.seat(quarter) * CR, CR)
            turned[pl.ds(seat, CR), rows] = flipped[quarter * CR : (quarter + 1) * CR]

    loads[3].wait()

    def middle(i):
        rows = at256(i * PART)
        value = tokx[rows].astype(F32) + dot_nn(att[rows], wo[...]) + vec[4:5]
        mid[rows] = value
        hat, _ = norm_parts(value)
        block = (hat * vec[5:6] + vec[6:7]).astype(BF)
        low2[rows] = block
        turn(rows, block)

    loop(0, 2, middle)
    loads[2].wait()
    loads[4].wait()
    load_we.wait()
    c_cot.wait_recv()
    y_sum[...] = jnp.zeros_like(y_sum)
    h_sum[...] = jnp.zeros_like(h_sum)

    def feed(t):
        starts = []
        for side in range(2):
            cc = p.core if side == 0 else 1 - p.core
            for yy in range(2):
                starts.append((yy * 2 + cc) * 768 + t * 128)
        w_up = jnp.concatenate([w1[:, at128(s)] for s in starts], axis=1)
        shifts = vec[8:12, at128(t * 128)]
        zeroth = p.core == 0
        shift = jnp.concatenate(
            [
                jnp.where(zeroth, shifts[yy * 2 + s : yy * 2 + s + 1], shifts[yy * 2 + 1 - s : yy * 2 + 2 - s])
                for s in range(2)
                for yy in range(2)
            ],
            axis=1,
        )
        before = dot_nn(low2[...], w_up) + shift
        half = 0.5 + 0.5 * lax.erf(before * 0.7071067811865476)
        active = (before * half).astype(BF)
        slope = half + before * (jnp.exp(before * before * -0.5) * 0.3989422804014327)
        g_t[...] = active
        w_down = jnp.concatenate([wr[at128(s), :] for s in starts], axis=0)
        du_t[...] = (dot_nt(dyx[...], w_down) * slope).astype(BF)
        tall = dot_nn(g_t[...].T, dyx[...]).astype(BF)
        red.slot(2 * t)
        red.put_tall(2 * t, tall)
        red.c_core(2 * t).start()
        red.slot(2 * t + 1)
        for e in range(2):
            seats = [e + 2 * (p.core if cc == 0 else 1 - p.core) for cc in range(2)]
            right = jnp.concatenate([du_t[:, at128(s * 128)] for s in seats], axis=1)
            red.put_wide(2 * t + 1, e, dot_nn(turned[...], right).astype(BF))
        red.c_core(2 * t + 1).start()
        sums = jnp.sum(du_t[...].astype(F32), axis=0, keepdims=True)
        seat = [sums[:, i * 128 : (i + 1) * 128] for i in range(4)]
        vs[8:12, at128(t * 128)] = jnp.concatenate(
            [
                jnp.where(zeroth, seat[yy + 2 * cc], seat[yy + 2 - 2 * cc])
                for yy in range(2)
                for cc in range(2)
            ],
            axis=0,
        )
        red.run_at(t, FEED_STEPS[0])
        y_sum[...] += dot_nn(g_t[...], w_down)
        h_sum[...] += dot_nt(du_t[...], w_up)
        red.run_at(t, FEED_STEPS[1])

    loop(0, 6, feed)
    reload_wi = pltpu.make_async_copy(wi_ref, w1.at[:, pl.ds(0, 2304)], lsem.at[6])
    reload_wi.start()

    def second(i):
        rows = at256(i * PART)
        value = mid[rows]
        lo[rows] = (value + y_sum[rows] + vec[7:8]).astype(BF)
        hat, scale = norm_parts(value)
        grad = h_sum[rows]
        upstream = dyx[rows].astype(F32)
        vs[5:6] += jnp.sum(grad * hat, axis=0, keepdims=True)
        vs[6:7] += jnp.sum(grad, axis=0, keepdims=True)
        vs[7:8] += jnp.sum(upstream, axis=0, keepdims=True)
        total = upstream + norm_back(hat, scale, vec[5:6], grad)
        mid[rows] = total
        block = total.astype(BF)
        low2[rows] = block
        vs[4:5] += jnp.sum(block.astype(F32), axis=0, keepdims=True)
        d_out[rows] = dot_nt(block, wo[...]).astype(BF)
        turn(rows, att[rows])
        red.run_at(i, NORM_STEPS)

    loop(0, 2, second)
    c_lo = swap(6, lo.at[pl.ds(PART, PART)], lo_ref.at[p.y], p.to_y)
    keep_lo = pltpu.make_async_copy(lo.at[pl.ds(0, PART)], lo_ref.at[p.y], lsem.at[7])
    keep_lo.start()

    red.slot(12)
    red.slot(13)
    for k, side, first in ((12, 0, 0), (12, 1, 256), (13, 0, 512)):
        red.put_wide(k, side, dot_nn(turned[...], low2[:, first : first + 256]).astype(BF))
    red.c_core(12).start()
    red.run(OUT_STEPS)

    def turn_first(i):
        rows = at256(i * PART)
        hat, _ = norm_parts(tokx[rows].astype(F32))
        turn(rows, (hat * vec[0:1] + vec[1:2]).astype(BF))

    loop(0, 2, turn_first)

    def in_grads(group):
        def one(i):
            at = 3 * group + i + 1
            k, side = 13 + at // 2, lax.rem(at, 2)
            pl.when(side == 0)(lambda: red.slot(k))
            cols = at256(i * 768 + group * 256)
            red.put_wide(k, side, dot_nn(turned[...], dp[:, cols]).astype(BF))
            pl.when(side == 1)(lambda: red.c_core(k).start())

        loop(0, 3, one)

    def c_dkv(pair):
        return remote(
            dkv_send.at[lax.rem(pair, 2)], dkv_recv.at[pair], ksend.at[pair], krecv.at[pair], p.to_core
        )

    def settle(pair):
        c_dkv(pair).wait_recv()
        slot = lax.rem(pair, 2)
        for i in range(2):
            total = dkv_own[slot, i] + dkv_recv[pair, i].astype(F32)
            dp[:, at128(768 * (i + 1) + pair * 128)] = total.astype(BF)

    lane_k = lax.broadcasted_iota(jnp.int32, (ROWS, 128), 1)

    def attend_back(pair):
        col = pl.multiple_of(pair * 128, 128)
        slot = lax.rem(pair, 2)
        query = qkv[:, at128(col)]
        extra_q = qaug[...].astype(BF)
        grads = d_out[:, at128(col)]
        outs = att[:, at128(col)].astype(F32)
        three = jnp.where(lane_k < 3, 1.0, 0.0).astype(BF)

        @pl.when(pair >= 1)
        def _():
            settle(pair - 1)

        for h in range(2):
            q_h = query * head_mask[h]
            g_h = grads * head_mask[h]
            parts = three_parts(jnp.sum(g_h.astype(F32) * outs, axis=-1, keepdims=True))
            extra_g = jnp.zeros((ROWS, 128), F32)
            for i in range(3):
                extra_g = jnp.where(lane_k == i, -parts[i], extra_g)
            q_wide = jnp.concatenate([q_h, extra_q], axis=1)
            g_wide = jnp.concatenate([g_h, extra_g.astype(BF)], axis=1)
            base = 1 + 3 * (2 * pair + h)
            mark = jnp.where(
                jnp.logical_and(lane_k >= base, lane_k < base + 3), 1.0, 0.0
            ).astype(BF)
            for side in range(2):
                if side == 0:
                    key, value = qkv[:, at128(768 + col)], qkv[:, at128(1536 + col)]
                else:
                    key, value = kvr[:, at128(col)], kvr[:, at128(768 + col)]
                k_wide = jnp.concatenate([key, kaug[pl.ds(side * ROWS, ROWS)] + mark], axis=1)
                v_wide = jnp.concatenate([value, three], axis=1)
                weight = jnp.exp(dot_nt(k_wide, q_wide))
                slope = (weight * dot_nt(v_wide, g_wide)).astype(BF)
                add_k, add_v = dot_nn(slope, q_h), dot_nn(weight.astype(BF), g_h)
                add_q = dot_nn((key * head_mask[h]).T, slope)
                if h == 0 and side == 0:
                    dq_sum[...] = add_q
                else:
                    dq_sum[...] += add_q
                sums = dkv_own.at[slot] if side == 0 else dkv_far
                if h == 0:
                    sums[0] = add_k
                    sums[1] = add_v
                else:
                    sums[0] += add_k
                    sums[1] += add_v
                red.run_at(pair, ATTEND_STEPS[2 * h + side])
        dp[:, at128(col)] = (dq_sum[...].T.astype(BF).astype(F32) * 0.125).astype(BF)

        @pl.when(pair >= 2)
        def _():
            c_dkv(pair - 2).wait_send()

        dkv_send[slot] = dkv_far[...].astype(BF)
        c_dkv(pair).start()
        pl.when(jnp.logical_and(pair >= 2, lax.rem(pair, 2) == 0))(lambda: in_grads(pair // 2 - 1))
        pl.when(pair == 1)(lambda: c_lo.start())

    loop(0, 6, attend_back)
    settle(5)
    c_dkv(4).wait_send()
    c_dkv(5).wait_send()

    in_grads(2)
    red.run(PROJECT_STEPS)
    vs[2:3] = jnp.sum(dp[:, 0:768].astype(F32), axis=0, keepdims=True)
    vs[3:4] = jnp.sum(dp[:, 1536:2304].astype(F32), axis=0, keepdims=True)
    reload_wi.wait()

    def first_back(i):
        rows = at256(i * PART)
        grad = dot_nt(dp[rows], w1[:, pl.ds(0, 2304)])
        hat, scale = norm_parts(tokx[rows].astype(F32))
        vs[0:1] += jnp.sum(grad * hat, axis=0, keepdims=True)
        vs[1:2] += jnp.sum(grad, axis=0, keepdims=True)
        y_sum[rows] = mid[rows] + norm_back(hat, scale, vec[0:1], grad)
        red.run_at(i, LAST_STEPS)

    loop(0, 2, first_back)
    gts[...] = y_sum[pl.ds(PART, PART)].astype(BF)
    c_gt = swap(7, gts, gtr_ref, p.to_y)
    keep_gt = pltpu.make_async_copy(y_sum.at[pl.ds(0, PART)], gto_ref, lsem.at[8])
    c_gt.start()
    keep_gt.start()

    def c_vec(stage, peer):
        return remote(vr.at[2 * stage], vr.at[2 * stage + 1], vsend.at[stage], vrecv.at[stage], peer)

    def vec_pair(stage, peer):
        vr[2 * stage] = vs[...]
        c_vec(stage, peer).start()

    def vec_take(stage, peer):
        c_vec(stage, peer).wait()
        vs[...] += vr[2 * stage + 1]

    def vec_0():
        vec_take(0, p.to_core)
        vec_pair(1, p.to_y)

    def vec_1():
        vec_take(1, p.to_y)
        vec_pair(2, p.to_x)

    def vec_2():
        vec_take(2, p.to_x)

        @pl.when(p.outer)
        def _():
            vec_pair(3, p.to_mate)

    def vec_3():
        @pl.when(p.inner)
        def _():
            c_vec(3, p.to_mate).wait_recv()
            vs[...] += vr[7]
            vec_pair(4, p.to_far)

    def vec_4():
        @pl.when(p.inner)
        def _():
            vec_take(4, p.to_far)
            vec_pair(3, p.to_mate)

    def vec_5():
        @pl.when(p.outer)
        def _():
            c_vec(3, p.to_mate).wait_recv()
            vs[...] = vr[7]

        c_vec(3, p.to_mate).wait_send()

    vec_pair(0, p.to_core)
    vec_steps = (vec_0, vec_1, vec_2, vec_3, vec_4, vec_5)
    for step in DRAIN_STEPS:
        if step < 100:
            vec_steps[step]()
        else:
            red.run((step,))
    red.close()
    c_tok.wait_send()
    c_row.wait_send()
    c_cot.wait_send()
    c_aug.wait_send()
    c_kv[0].wait_send()
    c_kv[1].wait_send()
    c_lo.wait()
    c_gt.wait()
    keep_lo.wait()
    keep_gt.wait()


def finish_kernel(
    tot_ref, vs, lo_in, gto, gtr_ref,
    lo_out, gt, g0, g1, wi_out, g2, wo_out, g4, g5, g6, we_out, g8, wr_out, g7,
    tot, gtr, gt_s, lo_s, wi, wo, we, wr, in_sem, out_sem,
):
    y = lax.axis_index("frame") // 2
    frame = lax.axis_index("frame")
    spans = [(2 * t, 2) for t in range(6)] + [(12, 2), (14, 2), (16, 2)]
    loads = [
        pltpu.make_async_copy(tot_ref.at[pl.ds(k, n)], tot.at[pl.ds(k, n)], in_sem.at[i])
        for i, (k, n) in enumerate(spans)
    ]
    loads += [
        pltpu.make_async_copy(gtr_ref, gtr, in_sem.at[9]),
        pltpu.make_async_copy(gto, gt_s.at[0], in_sem.at[10]),
        pltpu.make_async_copy(lo_in, lo_s, in_sem.at[11]),
    ]
    for one in loads:
        one.start()
    outs = []

    def leave(src, dst):
        one = pltpu.make_async_copy(src, dst, out_sem.at[len(outs)])
        one.start()
        outs.append(one)

    for t in range(6):
        loads[t].wait()
        rows = pl.ds(t * 128, 128)
        for i in range(6):
            block = slice(i % 3 * 128, (i % 3 + 1) * 128)
            wr[rows, i * 128 : (i + 1) * 128] = tot[2 * t, i // 3, block].astype(F32)
        leave(wr.at[rows], wr_out.at[rows])
        for j in range(4):
            cols = pl.ds(j * 768 + t * 128, 128)
            block = slice(j % 2 * CR, (j % 2 + 1) * CR)
            we[:, cols] = tot[2 * t + 1, j // 2, block].astype(F32)
    leave(we, we_out)
    for n, col in enumerate(COLUMNS):
        if n % 8 == 0:
            loads[6 + n // 8].wait()
        block = slice(n % 2 * CR, (n % 2 + 1) * CR)
        value = tot[12 + n // 4, n % 4 // 2, block].astype(F32)
        if n < 6:
            wo[:, col * 128 : (col + 1) * 128] = value
        else:
            wi[:, col * 128 : (col + 1) * 128] = value
        if n == 5:
            leave(wo, wo_out)
    leave(wi, wi_out)
    loads[9].wait()
    gt_s[1] = gtr[...].astype(F32)
    leave(gt_s.at[1], gt.at[1 - y, 0])
    loads[10].wait()
    leave(gt_s.at[0], gt.at[y, 0])
    loads[11].wait()
    leave(lo_s.at[0], lo_out.at[0, 0])
    leave(lo_s.at[1], lo_out.at[1, 0])
    mine = vs[0:8, 0:CR]
    row = vs[8:9]
    for f in range(1, 4):
        mine = jnp.where(frame == f, vs[0:8, f * CR : (f + 1) * CR], mine)
        row = jnp.where(frame == f, vs[8 + f : 9 + f], row)
    g0[...] = mine[0]
    g1[...] = mine[1]
    g2[...] = mine[2:4]
    g4[...] = mine[4]
    g5[...] = mine[5]
    g6[...] = mine[6]
    g7[...] = mine[7]
    g8[...] = row[0]
    for one in outs:
        one.wait()


def local_slice(
    tokens,
    counts,
    first_gain,
    first_bias,
    input_weight,
    input_bias,
    output_weight,
    output_bias,
    second_gain,
    second_bias,
    expand_weight,
    expand_bias,
    reduce_weight,
    reduce_bias,
    cotangent,
):
    anywhere = pl.BlockSpec(memory_space=pl.ANY)
    vmem = pl.BlockSpec(memory_space=pltpu.VMEM)
    smem = pl.BlockSpec(memory_space=pltpu.SMEM)
    shape = jax.ShapeDtypeStruct
    dma = pltpu.SemaphoreType.DMA
    tot, vs, lo, gto, gtr = pl.pallas_call(
        layer_kernel,
        out_shape=(
            shape((K, 2, HR, 128), BF),
            shape((16, D), F32),
            shape((2, PART, D), BF),
            shape((PART, D), F32),
            shape((PART, D), BF),
        ),
        in_specs=[anywhere, anywhere, smem] + [vmem] * 8 + [anywhere] * 4,
        out_specs=(anywhere, vmem, anywhere, anywhere, anywhere),
        scratch_shapes=[
            pltpu.VMEM((K, 2, 2, HR, 128), BF),
            pltpu.VMEM((SLOT_COUNT, 2, 2, HR, 128), BF),
            pltpu.VMEM((K, 2, 2, HR, 128), BF),
            pltpu.VMEM((K, 2, HR, 128), BF),
            pltpu.VMEM((K, HR, 128), BF),
            pltpu.VMEM((K, HR, 128), BF),
            pltpu.VMEM((K, HR, 128), BF),
            pltpu.VMEM((12, D), F32),
            pltpu.VMEM((ROWS, D), BF),
            pltpu.VMEM((ROWS, D), BF),
            pltpu.VMEM((D, FF), BF),
            pltpu.VMEM((D, D), BF),
            pltpu.VMEM((FF, D), BF),
            pltpu.VMEM((ROWS, 3 * D), BF),
            pltpu.VMEM((ROWS, 2 * D), BF),
            pltpu.VMEM((3, 16, PART), BF),
            pltpu.VMEM((2 * ROWS, 128), BF),
            pltpu.VMEM((ROWS, 128), F32),
            pltpu.VMEM((ROWS, D), BF),
            pltpu.VMEM((ROWS, D), F32),
            pltpu.VMEM((ROWS, D), BF),
            pltpu.VMEM((D, ROWS), BF),
            pltpu.VMEM((ROWS, ROWS), BF),
            pltpu.VMEM((ROWS, ROWS), BF),
            pltpu.VMEM((ROWS, D), F32),
            pltpu.VMEM((ROWS, D), F32),
            pltpu.VMEM((ROWS, D), BF),
            pltpu.VMEM((ROWS, 3 * D), BF),
            pltpu.VMEM((128, ROWS), F32),
            pltpu.VMEM((2, 2, ROWS, 128), F32),
            pltpu.VMEM((2, ROWS, 128), F32),
            pltpu.VMEM((2, 2, ROWS, 128), BF),
            pltpu.VMEM((6, 2, ROWS, 128), BF),
            pltpu.VMEM((ROWS, D), BF),
            pltpu.VMEM((PART, D), BF),
            pltpu.VMEM((10, 16, D), F32),
            dma((SLOT_COUNT,)),
            dma((12,)),
            dma((6, K)),
            dma((9,)),
            dma((8,)),
            dma((8,)),
            dma((6,)),
            dma((6,)),
            dma((5,)),
            dma((5,)),
        ],
        compiler_params=pltpu.CompilerParams(
            collective_id=0, has_side_effects=True, vmem_limit_bytes=62 << 20
        ),
    )(
        tokens,
        cotangent,
        counts,
        first_gain,
        first_bias,
        input_bias,
        output_bias,
        second_gain,
        second_bias,
        expand_bias,
        reduce_bias,
        input_weight,
        output_weight,
        expand_weight,
        reduce_weight,
    )
    return pl.pallas_call(
        finish_kernel,
        out_shape=(
            shape((MICRO, 1, PART, D), BF),
            shape((MICRO, 1, PART, D), F32),
            shape((CR,), F32),
            shape((CR,), F32),
            shape((CR, 3 * D), F32),
            shape((2, CR), F32),
            shape((CR, D), F32),
            shape((CR,), F32),
            shape((CR,), F32),
            shape((CR,), F32),
            shape((CR, FF), F32),
            shape((D,), F32),
            shape((D, D), F32),
            shape((CR,), F32),
        ),
        in_specs=[anywhere, vmem, anywhere, anywhere, anywhere],
        out_specs=tuple(anywhere if i in (0, 1, 4, 6, 10, 12) else vmem for i in range(14)),
        scratch_shapes=[
            pltpu.VMEM((K, 2, HR, 128), BF),
            pltpu.VMEM((PART, D), BF),
            pltpu.VMEM((2, PART, D), F32),
            pltpu.VMEM((2, PART, D), BF),
            pltpu.VMEM((CR, 3 * D), F32),
            pltpu.VMEM((CR, D), F32),
            pltpu.VMEM((CR, FF), F32),
            pltpu.VMEM((D, D), F32),
            dma((12,)),
            dma((16,)),
        ],
        compiler_params=pltpu.CompilerParams(vmem_limit_bytes=62 << 20),
    )(tot, vs, lo, gto, gtr)


def solution(mesh):
    fits = mesh.shape["clip"] == 8 and mesh.shape["frame"] == 4
    return jax.shard_map(
        local_slice if fits else local,
        mesh=mesh,
        in_specs=(
            P(None, "clip", "frame", None),
            P(None, "clip", "frame"),
            P(),
            P(),
            P(),
            P(),
            P(),
            P(),
            P(),
            P(),
            P(),
            P(),
            P(),
            P(),
            P(None, "clip", "frame", None),
        ),
        out_specs=(
            P(None, "clip", "frame", None),
            P(None, "clip", "frame", None),
            P("frame"),
            P("frame"),
            P("frame", None),
            P(None, "frame"),
            P("frame", None),
            P("frame"),
            P("frame"),
            P("frame"),
            P("frame", None),
            P("frame"),
            P("frame", None),
            P("frame"),
        ),
        check_vma=False,
    )
```

```python
import jax
import jax.numpy as jnp
from jax import lax
from jax.experimental import pallas as pl
from jax.experimental.pallas import tpu as pltpu
from jax.sharding import PartitionSpec as P

D = 768
H = 12
HD = 64
MICRO = 2
FRAME_DEV = 4
SLOTS = 64
BLOCK = 256


epsilon = 1e-06


def from_behind(block, axis, distance):
    devices = range(lax.axis_size(axis))
    route = [((i - distance) % len(devices), i) for i in devices]
    return lax.ppermute(block, axis, route)


def norm_rows(values, gain, shift):
    mean = jnp.mean(values, axis=-1, keepdims=True)
    centred = values - mean
    spread = jnp.mean(centred * centred, axis=-1, keepdims=True)
    return centred * lax.rsqrt(spread + epsilon) * gain + shift


def gelu_exact(values):
    return jax.nn.gelu(values, approximate=False)


def key_valid(every_count, source):
    frame_counts = lax.dynamic_slice_in_dim(every_count, source * FRAME_DEV, FRAME_DEV, 1)
    slot_index = jnp.arange(SLOTS, dtype=jnp.int32)
    return (slot_index[None, None, :] < frame_counts[:, :, None]).reshape(MICRO, BLOCK)


def scores_of(query, keys, valid):
    key_heads = keys.reshape(MICRO, BLOCK, H, HD)
    scores = jnp.einsum("mqhd,mkhd->mhqk", query, key_heads, preferred_element_type=jnp.float32)
    return jnp.where(valid[:, None, None, :], scores, -1e30)


def absorb(state, query, keys, values, valid):
    top, total, summed = state
    scores = scores_of(query, keys, valid)
    new_top = jnp.maximum(top, jnp.max(scores, axis=-1, keepdims=True))
    factor = jnp.exp(top - new_top)
    lifted = jnp.exp(scores - new_top)
    total = total * factor + jnp.sum(lifted, axis=-1, keepdims=True)
    value_heads = values.reshape(MICRO, BLOCK, H, HD)
    summed = summed * factor + jnp.einsum(
        "mhqk,mkhd->mhqd",
        lifted.astype(jnp.bfloat16),
        value_heads,
        preferred_element_type=jnp.float32,
    )
    return (new_top, total, summed)


def block_back(query, keys, values, valid, log_total, delta, grad_heads):
    scores = scores_of(query, keys, valid)
    weights = jnp.exp(scores - log_total)
    key_heads = keys.reshape(MICRO, BLOCK, H, HD)
    value_heads = values.reshape(MICRO, BLOCK, H, HD)
    grad_weights = jnp.einsum(
        "mqhd,mkhd->mhqk", grad_heads, value_heads, preferred_element_type=jnp.float32
    )
    grad_scores = (weights * (grad_weights - delta)).astype(jnp.bfloat16)
    grad_query = jnp.einsum(
        "mhqk,mkhd->mqhd", grad_scores, key_heads, preferred_element_type=jnp.float32
    )
    grad_keys = jnp.einsum(
        "mhqk,mqhd->mkhd", grad_scores, query, preferred_element_type=jnp.float32
    )
    grad_values = jnp.einsum(
        "mhqk,mqhd->mkhd",
        weights.astype(jnp.bfloat16),
        grad_heads,
        preferred_element_type=jnp.float32,
    )
    return (grad_query, grad_keys.reshape(MICRO, BLOCK, D), grad_values.reshape(MICRO, BLOCK, D))


def local(
    tokens,
    counts,
    first_gain,
    first_bias,
    input_weight,
    input_bias,
    output_weight,
    output_bias,
    second_gain,
    second_bias,
    expand_weight,
    expand_bias,
    reduce_weight,
    reduce_bias,
    cotangent,
):
    members = lax.axis_size("frame")
    myself = lax.axis_index("frame")
    total_rows = MICRO * BLOCK
    seq_in = tokens.reshape(total_rows, D).astype(jnp.float32)
    every_count = lax.all_gather(counts.reshape(MICRO, FRAME_DEV), "frame", axis=1, tiled=True)
    gain_one = first_gain.astype(jnp.float32)
    shift_one = first_bias.astype(jnp.float32)
    gain_two = second_gain.astype(jnp.float32)
    shift_two = second_bias.astype(jnp.float32)
    qv_bias = input_bias.astype(jnp.float32)
    first_low = norm_rows(seq_in, gain_one, shift_one).astype(jnp.bfloat16)
    projected = jnp.dot(first_low, input_weight, preferred_element_type=jnp.float32)
    query = (
        ((projected[:, :D] + qv_bias[0]) * 0.125).astype(jnp.bfloat16).reshape(MICRO, BLOCK, H, HD)
    )
    keys = projected[:, D : 2 * D].astype(jnp.bfloat16).reshape(MICRO, BLOCK, D)
    values = (projected[:, 2 * D :] + qv_bias[1]).astype(jnp.bfloat16).reshape(MICRO, BLOCK, D)
    start = (
        jnp.full((MICRO, H, BLOCK, 1), -1e30, jnp.float32),
        jnp.zeros((MICRO, H, BLOCK, 1), jnp.float32),
        jnp.zeros((MICRO, H, BLOCK, HD), jnp.float32),
    )
    state = absorb(start, query, keys, values, key_valid(every_count, myself))
    stored = ()

    def forward_hop(step, carry):
        state_now, moving, kept = carry
        moving = from_behind((moving[0], moving[1]), "frame", 1)
        source = (myself - step) % members
        state_now = absorb(state_now, query, moving[0], moving[1], key_valid(every_count, source))
        return (state_now, moving, kept)

    state, _, stored = lax.fori_loop(1, members, forward_hop, (state, (keys, values), stored))
    top, total, summed = state
    log_total = top + jnp.log(total)
    attend_full = jnp.transpose(summed / total, (0, 2, 1, 3))
    attend_low = attend_full.reshape(total_rows, D).astype(jnp.bfloat16)
    middle = (
        seq_in
        + jnp.dot(attend_low, output_weight, preferred_element_type=jnp.float32)
        + output_bias.astype(jnp.float32)
    )
    second_low = norm_rows(middle, gain_two, shift_two).astype(jnp.bfloat16)
    before = jnp.dot(
        second_low, expand_weight, preferred_element_type=jnp.float32
    ) + expand_bias.astype(jnp.float32)
    active_low = gelu_exact(before).astype(jnp.bfloat16)
    result = (
        middle
        + jnp.dot(active_low, reduce_weight, preferred_element_type=jnp.float32)
        + reduce_bias.astype(jnp.float32)
    )
    layer_out = result.astype(jnp.bfloat16).reshape(MICRO, 1, BLOCK, D)
    upstream_low = cotangent.reshape(total_rows, D)
    upstream = upstream_low.astype(jnp.float32)
    grad_reduce_weight = jnp.dot(active_low.T, upstream_low, preferred_element_type=jnp.float32)
    grad_reduce_bias = jnp.sum(upstream, axis=0)
    grad_active = jnp.dot(upstream_low, reduce_weight.T, preferred_element_type=jnp.float32)
    _, gelu_back = jax.vjp(gelu_exact, before)
    grad_before = gelu_back(grad_active)[0].astype(jnp.bfloat16)
    grad_expand_weight = jnp.dot(second_low.T, grad_before, preferred_element_type=jnp.float32)
    grad_expand_bias = jnp.sum(grad_before.astype(jnp.float32), axis=0)
    grad_second = jnp.dot(grad_before, expand_weight.T, preferred_element_type=jnp.float32)
    _, second_back = jax.vjp(norm_rows, middle, gain_two, shift_two)
    middle_part, grad_second_gain, grad_second_bias = second_back(grad_second)
    grad_middle = upstream + middle_part
    grad_branch = grad_middle.astype(jnp.bfloat16)
    grad_output_weight = jnp.dot(attend_low.T, grad_branch, preferred_element_type=jnp.float32)
    grad_output_bias = jnp.sum(grad_branch.astype(jnp.float32), axis=0)
    grad_attend = jnp.dot(grad_branch, output_weight.T, preferred_element_type=jnp.float32).astype(
        jnp.bfloat16
    )
    grad_heads = grad_attend.reshape(MICRO, BLOCK, H, HD)
    delta = jnp.transpose(
        jnp.sum(grad_heads.astype(jnp.float32) * attend_full, axis=-1), (0, 2, 1)
    )[..., None]
    first_terms = block_back(
        query, keys, values, key_valid(every_count, myself), log_total, delta, grad_heads
    )

    def backward_hop(step, carry):
        grad_query, running, moving = carry
        running = (
            from_behind(running[0].astype(jnp.bfloat16), "frame", 1).astype(jnp.float32),
            from_behind(running[1].astype(jnp.bfloat16), "frame", 1).astype(jnp.float32),
        )
        current = from_behind((moving[0], moving[1]), "frame", 1)
        source = (myself - step) % members
        add_query, add_keys, add_values = block_back(
            query,
            current[0],
            current[1],
            key_valid(every_count, source),
            log_total,
            delta,
            grad_heads,
        )
        return (grad_query + add_query, (running[0] + add_keys, running[1] + add_values), current)

    grad_query, running, _ = lax.fori_loop(
        1, members, backward_hop, (first_terms[0], (first_terms[1], first_terms[2]), (keys, values))
    )
    finished = (
        from_behind(running[0].astype(jnp.bfloat16), "frame", 1).astype(jnp.float32),
        from_behind(running[1].astype(jnp.bfloat16), "frame", 1).astype(jnp.float32),
    )
    query_low = grad_query.astype(jnp.bfloat16).reshape(total_rows, D) * 0.125
    keys_low = finished[0].astype(jnp.bfloat16).reshape(total_rows, D)
    values_low = finished[1].astype(jnp.bfloat16).reshape(total_rows, D)
    grad_projected = jnp.concatenate([query_low, keys_low, values_low], axis=1)
    grad_input_weight = jnp.dot(first_low.T, grad_projected, preferred_element_type=jnp.float32)
    grad_input_bias = jnp.stack(
        [
            jnp.sum(query_low.astype(jnp.float32), axis=0),
            jnp.sum(values_low.astype(jnp.float32), axis=0),
        ]
    )
    grad_first = jnp.dot(grad_projected, input_weight.T, preferred_element_type=jnp.float32)
    _, first_back = jax.vjp(norm_rows, seq_in, gain_one, shift_one)
    input_part, grad_first_gain, grad_first_bias = first_back(grad_first)
    grad_tokens = (grad_middle + input_part).reshape(MICRO, 1, BLOCK, D)
    shares = (
        lax.psum_scatter(
            grad_first_gain.astype(jnp.bfloat16), "frame", scatter_dimension=0, tiled=True
        ).astype(jnp.float32),
        lax.psum_scatter(
            grad_first_bias.astype(jnp.bfloat16), "frame", scatter_dimension=0, tiled=True
        ).astype(jnp.float32),
        lax.psum_scatter(
            grad_input_weight.astype(jnp.bfloat16), "frame", scatter_dimension=0, tiled=True
        ).astype(jnp.float32),
        lax.psum_scatter(
            grad_input_bias.astype(jnp.bfloat16), "frame", scatter_dimension=1, tiled=True
        ).astype(jnp.float32),
        lax.psum_scatter(
            grad_output_weight.astype(jnp.bfloat16), "frame", scatter_dimension=0, tiled=True
        ).astype(jnp.float32),
        lax.psum_scatter(
            grad_output_bias.astype(jnp.bfloat16), "frame", scatter_dimension=0, tiled=True
        ).astype(jnp.float32),
        lax.psum_scatter(
            grad_second_gain.astype(jnp.bfloat16), "frame", scatter_dimension=0, tiled=True
        ).astype(jnp.float32),
        lax.psum_scatter(
            grad_second_bias.astype(jnp.bfloat16), "frame", scatter_dimension=0, tiled=True
        ).astype(jnp.float32),
        lax.psum_scatter(
            grad_expand_weight.astype(jnp.bfloat16), "frame", scatter_dimension=0, tiled=True
        ).astype(jnp.float32),
        lax.psum_scatter(
            grad_expand_bias.astype(jnp.bfloat16), "frame", scatter_dimension=0, tiled=True
        ).astype(jnp.float32),
        lax.psum_scatter(
            grad_reduce_weight.astype(jnp.bfloat16), "frame", scatter_dimension=0, tiled=True
        ).astype(jnp.float32),
        lax.psum_scatter(
            grad_reduce_bias.astype(jnp.bfloat16), "frame", scatter_dimension=0, tiled=True
        ).astype(jnp.float32),
    )
    totals = (
        lax.psum(shares[0].astype(jnp.bfloat16), "clip").astype(jnp.float32),
        lax.psum(shares[1].astype(jnp.bfloat16), "clip").astype(jnp.float32),
        lax.psum(shares[2].astype(jnp.bfloat16), "clip").astype(jnp.float32),
        lax.psum(shares[3].astype(jnp.bfloat16), "clip").astype(jnp.float32),
        lax.psum(shares[4].astype(jnp.bfloat16), "clip").astype(jnp.float32),
        lax.psum(shares[5].astype(jnp.bfloat16), "clip").astype(jnp.float32),
        lax.psum(shares[6].astype(jnp.bfloat16), "clip").astype(jnp.float32),
        lax.psum(shares[7].astype(jnp.bfloat16), "clip").astype(jnp.float32),
        lax.psum(shares[8].astype(jnp.bfloat16), "clip").astype(jnp.float32),
        lax.psum(shares[9].astype(jnp.bfloat16), "clip").astype(jnp.float32),
        lax.psum(shares[10].astype(jnp.bfloat16), "clip").astype(jnp.float32),
        lax.psum(shares[11].astype(jnp.bfloat16), "clip").astype(jnp.float32),
    )
    return (
        layer_out,
        grad_tokens,
        totals[0],
        totals[1],
        totals[2],
        totals[3],
        totals[4],
        totals[5],
        totals[6],
        totals[7],
        totals[8],
        totals[9],
        totals[10],
        totals[11],
    )


MESH = pl.DeviceIdType.MESH
BF = jnp.bfloat16
F32 = jnp.float32
K = 20
BUFFERS = 18
QR = 768
HR = 384
CR = 192
SLOT_COUNT = 4
ROWS = 512
PART = 256
FF = 3072
LOW = -1e30
COLUMNS = (0, 1, 2, 3, 4, 5, 0, 1, 6, 7, 12, 13, 2, 3, 8, 9, 14, 4, 15, 5, 10, 16, 11, 17)
LAST_BIG = 16
WAYS = "acababbccbabccbaaaab"
CUTS = (0, 1, 2, 3)
FEED_STEPS = (((), (), (101, 102), (104,), (200, 106), (203, 202, 108, 109)), ((), (100,), (103,), (105,), (201, 107), ()))
NORM_STEPS = ((), (205, 110, 204, 111))
OUT_STEPS = (207, 300)
ATTEND_STEPS = (((301,), (400, 302), (209, 500), (600, 306, 402, 211, 401), (501,), (213, 605, 312, 410)), ((), (), (307, 212, 304), (603, 404, 113, 505, 310, 114), (), (507, 214, 311, 506, 115, 601, 116, 508)), ((303, 112, 208, 206), (403,), (503, 308), (407,), (), (602,)), ((305,), (210,), (405,), (406, 408, 502), (309, 504), (409, 313, 604, 510, 412)))
PROJECT_STEPS = (411, 314, 607, 606, 608, 509)
LAST_STEPS = ((215, 117, 413, 118, 119, 610, 512, 216), (414, 511))
DRAIN_STEPS = (217, 315, 0, 218, 609, 219, 514, 513, 1, 415, 611, 612, 2, 316, 614, 317, 3, 515, 318, 4, 416, 319, 417, 613, 615, 418, 5, 516, 419, 517, 518, 519, 616, 617, 618, 619)


def dot_nn(a, b):
    return lax.dot_general(a, b, (((1,), (0,)), ((), ())), preferred_element_type=F32)


def dot_nt(a, b):
    return lax.dot_general(a, b, (((1,), (1,)), ((), ())), preferred_element_type=F32)


def dot_tn(a, b):
    return lax.dot_general(a, b, (((0,), (0,)), ((), ())), preferred_element_type=F32)


def at128(index):
    return pl.ds(pl.multiple_of(index, 128), 128)


def at256(index):
    return pl.ds(pl.multiple_of(index, 256), 256)


def loop(low, high, body):
    def step(i, carry):
        body(i)
        return carry

    lax.fori_loop(low, high, step, 0)


class Place:
    def __init__(self):
        self.clip = lax.axis_index("clip")
        self.frame = lax.axis_index("frame")
        self.x = lax.rem(self.clip, 2)
        self.z = self.clip // 2
        self.core = lax.rem(self.frame, 2)
        self.y = self.frame // 2
        self.outer = jnp.logical_or(self.z == 0, self.z == 3)
        self.inner = jnp.logical_not(self.outer)
        self.to_core = (self.clip, self.y * 2 + (1 - self.core))
        self.to_y = (self.clip, (1 - self.y) * 2 + self.core)
        self.to_x = (self.z * 2 + (1 - self.x), self.frame)
        mate = self.z + 1 - 2 * lax.rem(self.z, 2)
        self.to_mate = (mate * 2 + self.x, self.frame)
        self.to_far = ((3 - self.z) * 2 + self.x, self.frame)
        self.h = jnp.where(self.inner, 1, 0)

    def seat(self, quarter):
        yy, cc = quarter // 2, quarter % 2
        return yy + 2 * (self.core if cc == 0 else 1 - self.core)


def enter(place):
    barrier = pltpu.get_barrier_semaphore()
    for peer in (place.to_core, place.to_y, place.to_x, place.to_mate, place.to_far):
        pl.semaphore_signal(barrier, inc=1, device_id=peer, device_id_type=MESH)
    pl.semaphore_wait(barrier, 5)


def remote(src, dst, send, recv, peer):
    return pltpu.make_async_remote_copy(
        src_ref=src, dst_ref=dst, send_sem=send, recv_sem=recv, device_id=peer, device_id_type=MESH
    )


class Reduce:
    def __init__(self, place, bufs, tot, csend, send, recv):
        self.p = place
        self.own, self.nbr, self.rc, self.ry, self.rx, self.r1, self.r2 = bufs
        self.tot, self.csend, self.send, self.recv = tot, csend, send, recv

    def copy(self, src, dst, kind, stage, k, peer):
        return remote(src, dst, self.send.at[kind], self.recv.at[stage, k], peer)

    def last(self, src, dst, kind, end, peer):
        return remote(src, dst, self.send.at[kind], self.send.at[end], peer)

    def place(self, k):
        if k < LAST_BIG:
            return k, 0, HR
        return LAST_BIG + (k - LAST_BIG) // 2, (k - LAST_BIG) % 2 * CR, CR

    def part(self, k, far):
        _, low, rows = self.place(k)
        side = 1 - self.p.x if far else self.p.x
        return pl.ds(pl.multiple_of(low + side * (rows // 2), 32), rows // 2)

    def c_core(self, k):
        slot = self.seat(k)
        src, dst = self.nbr.at[slot], self.rc.at[k] if not isinstance(k, int) or k < LAST_BIG else None
        if dst is None:
            b, low, rows = self.place(k)
            src, dst = self.nbr.at[slot, :, :, pl.ds(0, rows)], self.rc.at[b, :, :, pl.ds(low, rows)]
        return remote(src, dst, self.csend.at[slot], self.recv.at[0, k], self.p.to_core)

    def side(self, ref, k, *lead):
        b, low, rows = self.place(k)
        return ref.at[(b, *lead, pl.ds(low, rows))]

    def a_y(self, k):
        return self.copy(
            self.side(self.own, k, 1 - self.p.y, slice(None)), self.side(self.ry, k, slice(None)), 0, 1, k, self.p.to_y
        )

    def a_x(self, k):
        return self.copy(
            self.side(self.own, k, self.p.y, 1 - self.p.x), self.side(self.rx, k), 1, 2, k, self.p.to_x
        )

    def b_x(self, k):
        return self.copy(
            self.side(self.own, k, slice(None), 1 - self.p.x), self.side(self.ry, k, slice(None)), 0, 1, k, self.p.to_x
        )

    def b_y(self, k):
        return self.copy(
            self.side(self.own, k, 1 - self.p.y, self.p.x), self.side(self.rx, k), 1, 2, k, self.p.to_y
        )

    def half(self, k):
        return self.side(self.own, k, self.p.y, self.p.x)

    def l_in(self, k):
        return self.copy(self.half(k), self.side(self.r1, k), 2, 3, k, self.p.to_mate)

    def l_mid(self, k):
        return self.copy(self.half(k), self.side(self.r2, k), 3, 4, k, self.p.to_far)

    def l_out(self, k):
        return self.copy(self.side(self.r2, k), self.side(self.r1, k), 2, 3, k, self.p.to_mate)

    def l_leave(self, k, inner):
        src = self.side(self.r2 if inner else self.r1, k)
        dst = self.side(self.tot, k, self.p.x)
        self.last(src, dst, 4, 5, self.p.to_x).start()
        self.keep(src, dst).start()

    def q_pair(self, k):
        return self.copy(
            self.side(self.own, k, slice(None), 1 - self.p.h),
            self.side(self.ry, k, slice(None)),
            0,
            1,
            k,
            self.p.to_mate,
        )

    def q_y(self, k):
        return self.copy(
            self.side(self.own, k, 1 - self.p.y, self.p.h), self.side(self.rx, k), 1, 2, k, self.p.to_y
        )

    def q_own(self, k, far):
        return self.own.at[self.place(k)[0], self.p.y, self.p.h, self.part(k, far)]

    def q_in(self, k, second):
        b, low, rows = self.place(k)
        return self.r1.at[b, pl.ds(low + second * (rows // 2), rows // 2)]

    def q_x(self, k):
        return self.copy(self.q_own(k, True), self.q_in(k, 0), 6, 3, k, self.p.to_x)

    def q_far(self, k):
        return self.copy(self.q_own(k, False), self.q_in(k, 1), 7, 4, k, self.p.to_far)

    def q_gather(self, k):
        both = self.r2.at[self.place(k)[0], self.part(k, False)]
        return self.copy(both, both, 8, 5, k, self.p.to_x)

    def q_leave(self, k):
        src, dst = self.side(self.r2, k), self.side(self.tot, k, self.p.h)
        self.last(src, dst, 9, 10, self.p.to_mate).start()
        self.keep(src, dst).start()

    def keep(self, src, dst):
        return pltpu.make_async_copy(src, dst, self.send.at[11])

    def split(self, k, a, b, c):
        {"a": a, "b": b, "c": c}[WAYS[k]](k)

    def seat(self, k):
        return k % SLOT_COUNT if isinstance(k, int) else lax.rem(k, SLOT_COUNT)

    def slot(self, k):
        if isinstance(k, int):
            self.c_core(k - SLOT_COUNT).wait_send()
        else:
            pl.when(k >= SLOT_COUNT)(lambda: self.c_core(k - SLOT_COUNT).wait_send())

    def put_wide(self, k, side, grad):
        slot = self.seat(k)
        for yy in range(2):
            for i in range(2):
                rows = slice(i * CR, (i + 1) * CR)
                cols = slice(i * 128, (i + 1) * 128)
                self.own[k, yy, side, rows] = grad[yy * CR : (yy + 1) * CR, cols]
                self.nbr[slot, yy, side, rows] = grad[(2 + yy) * CR : (3 + yy) * CR, cols]

    def put_small(self, k, grad):
        slot = self.seat(k)
        b, low, rows = self.place(k)
        for yy in range(2):
            for i in range(2):
                cols = slice(i * 128, (i + 1) * 128)
                self.own[b, yy, i, low : low + rows] = grad[yy * CR : (yy + 1) * CR, cols]
                self.nbr[slot, yy, i, 0:rows] = grad[(2 + yy) * CR : (3 + yy) * CR, cols]

    def put_tall(self, k, grad):
        slot = self.seat(k)
        for yy in range(2):
            for i in range(6):
                rows = slice(i % 3 * 128, (i % 3 + 1) * 128)
                cols = slice(i * 128, (i + 1) * 128)
                self.own[k, yy, i // 3, rows] = grad[yy * 128 : (yy + 1) * 128, cols]
                self.nbr[slot, yy, i // 3, rows] = grad[(2 + yy) * 128 : (3 + yy) * 128, cols]

    def add(self, to, more):
        to[...] = to[...] + more[...]

    def stage_1(self, k):
        self.c_core(k).wait_recv()
        both = (slice(None), slice(None))
        self.add(self.side(self.own, k, *both), self.side(self.rc, k, *both))
        self.split(
            k,
            lambda k: self.a_y(k).start(),
            lambda k: self.b_x(k).start(),
            lambda k: self.q_pair(k).start(),
        )

    def stage_2(self, k):
        self.a_y(k).wait_recv()
        came = self.side(self.ry, k, slice(None))

        def a(k):
            self.add(self.side(self.own, k, self.p.y, slice(None)), came)
            self.a_x(k).start()

        def b(k):
            self.add(self.side(self.own, k, slice(None), self.p.x), came)
            self.b_y(k).start()

        def c(k):
            self.add(self.side(self.own, k, slice(None), self.p.h), came)
            self.q_y(k).start()

        self.split(k, a, b, c)

    def stage_3(self, k):
        self.a_x(k).wait_recv()
        came = self.side(self.rx, k)

        def line(k):
            self.add(self.half(k), came)
            pl.when(self.p.outer)(lambda: self.l_in(k).start())

        def c(k):
            self.add(self.side(self.own, k, self.p.y, self.p.h), came)
            self.q_x(k).start()

        self.split(k, line, line, c)

    def stage_4(self, k):
        def line(k):
            @pl.when(self.p.inner)
            def _():
                self.l_in(k).wait_recv()
                self.add(self.half(k), self.side(self.r1, k))
                self.l_mid(k).start()

        def c(k):
            self.q_x(k).wait_recv()
            self.add(self.q_own(k, False), self.q_in(k, 0))
            self.q_far(k).start()

        self.split(k, line, line, c)

    def stage_5(self, k):
        def line(k):
            @pl.when(self.p.inner)
            def _():
                self.l_mid(k).wait_recv()
                self.add(self.side(self.r2, k), self.half(k))
                self.l_out(k).start()
                self.l_leave(k, True)

        def c(k):
            self.q_far(k).wait_recv()
            total = self.q_own(k, False)[...] + self.q_in(k, 1)[...]
            self.r2[self.place(k)[0], self.part(k, False)] = total
            self.q_gather(k).start()

        self.split(k, line, line, c)

    def stage_6(self, k):
        def line(k):
            @pl.when(self.p.outer)
            def _():
                self.l_in(k).wait_recv()
                self.l_leave(k, False)

        def c(k):
            self.q_gather(k).wait_recv()
            self.q_leave(k)

        self.split(k, line, line, c)

    def close(self):
        rest = WAYS[:LAST_BIG].count("c") + WAYS[LAST_BIG:].count("c") // 2
        line = BUFFERS - rest
        peer = self.p.to_x

        def whole(ref, count, kind):
            span = ref.at[pl.ds(0, count)]
            return remote(span, span, self.send.at[kind], self.send.at[kind], peer)

        def parts(kind):
            span = self.r1.at[pl.ds(0, rest), pl.ds(0, CR)]
            return remote(span, span, self.send.at[kind], self.send.at[kind], peer)

        for k in range(K - SLOT_COUNT, K):
            self.c_core(k).wait_send()
        whole(self.ry, BUFFERS, 0).wait_send()
        whole(self.rx, BUFFERS, 1).wait_send()
        whole(self.r1, line, 2).wait_send()
        pl.when(self.p.inner)(lambda: whole(self.r1, line, 3).wait_send())
        whole(self.r1, line, 4).wait_send()
        whole(self.r1, line, 5).wait_recv()
        parts(6).wait_send()
        parts(7).wait_send()
        parts(8).wait_send()
        whole(self.r1, rest, 9).wait_send()
        whole(self.r1, rest, 10).wait_recv()
        pltpu.make_async_copy(self.r1, self.r2, self.send.at[11]).wait()

    def run(self, steps):
        stages = (self.stage_1, self.stage_2, self.stage_3, self.stage_4, self.stage_5, self.stage_6)
        for step in steps:
            stages[step // 100 - 1](step % 100)

    def run_at(self, index, table):
        for i, steps in enumerate(table):
            if steps:
                pl.when(index == i)(lambda steps=steps: self.run(steps))


def norm_parts(values):
    mean = jnp.mean(values, axis=-1, keepdims=True)
    centred = values - mean
    spread = jnp.mean(centred * centred, axis=-1, keepdims=True)
    scale = lax.rsqrt(spread + epsilon)
    return centred * scale, scale


def norm_back(hat, scale, gain, grad):
    lifted = grad * gain
    level = jnp.mean(lifted, axis=-1, keepdims=True)
    slope = jnp.mean(lifted * hat, axis=-1, keepdims=True)
    return scale * (lifted - level - hat * slope)


def three_parts(values):
    high = values.astype(BF).astype(F32)
    rest = values - high
    middle = rest.astype(BF).astype(F32)
    return high, middle, rest - middle


def layer_kernel(
    tok_ref, cot_ref, cnt_ref, fg_ref, fb_ref, ib_ref, ob_ref, sg_ref, sb_ref, eb_ref, rb_ref,
    wi_ref, wo_ref, we_ref, wr_ref,
    tot_ref, vs, lo_ref, gto_ref, gtr_ref,
    own, nbr, rc, ry, rx, r1, r2, vec,
    tokx, dyx, w1, wo, wr, qkv, kvr, rowb, kaug, qaug, att, mid, low2, turned, g_t, du_t, y_sum, h_sum,
    d_out, dp, dq_sum, dkv_own, dkv_far, dkv_send, dkv_recv, lo, gts, vr,
    csend, send, recv, lsem, xsend, xrecv, ksend, krecv, vsend, vrecv,
):
    p = Place()
    loads = [
        pltpu.make_async_copy(tok_ref.at[p.y, 0], tokx.at[pl.ds(0, PART)], lsem.at[0]),
        pltpu.make_async_copy(wi_ref, w1.at[:, pl.ds(0, 2304)], lsem.at[1]),
        pltpu.make_async_copy(cot_ref.at[p.y, 0], dyx.at[pl.ds(0, PART)], lsem.at[2]),
        pltpu.make_async_copy(wo_ref, wo, lsem.at[3]),
        pltpu.make_async_copy(wr_ref, wr, lsem.at[4]),
    ]
    for one in loads:
        one.start()
    enter(p)
    red = Reduce(p, (own, nbr, rc, ry, rx, r1, r2), tot_ref, csend, send, recv)

    def swap(index, src, dst, peer):
        return remote(src, dst, xsend.at[index], xrecv.at[index], peer)

    c_tok = swap(0, tok_ref.at[1 - p.y, 0], tokx.at[pl.ds(PART, PART)], p.to_y)
    c_cot = swap(1, cot_ref.at[1 - p.y, 0], dyx.at[pl.ds(PART, PART)], p.to_y)
    c_row = swap(2, rowb.at[2], rowb.at[1], p.to_y)
    c_aug = swap(3, kaug.at[pl.ds(0, ROWS)], kaug.at[pl.ds(ROWS, ROWS)], p.to_core)
    c_kv = [
        swap(4 + r, qkv.at[pl.ds(r * PART, PART), pl.ds(768, 1536)], kvr.at[pl.ds(r * PART, PART)], p.to_core)
        for r in range(2)
    ]
    c_tok.start()

    for row, ref in ((0, fg_ref), (1, fb_ref), (4, ob_ref), (5, sg_ref), (6, sb_ref), (7, rb_ref)):
        vec[row : row + 1] = ref[...].astype(F32).reshape(1, D)
    vec[2:4] = ib_ref[...].astype(F32)
    for f in range(4):
        vec[8 + f : 9 + f] = eb_ref[f * D : (f + 1) * D].astype(F32).reshape(1, D)

    lane = lax.broadcasted_iota(jnp.int32, (16, PART), 1)

    def bias_row(m):
        frame = lane // SLOTS
        kept = jnp.zeros_like(lane)
        for j in range(FRAME_DEV):
            kept = jnp.where(frame == j, cnt_ref[m, 0, j], kept)
        return jnp.where(lane - frame * SLOTS < kept, 0.0, LOW).astype(BF)

    rowb[0] = bias_row(p.y)
    rowb[2] = bias_row(1 - p.y)
    c_row.start()
    pick = jnp.where(
        jnp.logical_and(
            lax.broadcasted_iota(jnp.int32, (16, 128), 0) == 0,
            lax.broadcasted_iota(jnp.int32, (16, 128), 1) == 0,
        ),
        1.0,
        0.0,
    ).astype(BF)
    kaug[pl.ds(0, PART)] = dot_tn(rowb[0], pick).astype(BF)
    lane_q = lax.broadcasted_iota(jnp.int32, (PART, 128), 1)
    lane_row = lax.broadcasted_iota(jnp.int32, (1, 128), 1)
    head_mask = [
        jnp.where((lane_row < 64) == (h == 0), 1.0, 0.0).astype(BF) for h in range(2)
    ]
    qaug[...] = jnp.where(lax.broadcasted_iota(jnp.int32, (ROWS, 128), 1) == 0, 1.0, 0.0)
    vs[...] = jnp.zeros_like(vs)

    def project(r):
        rows = pl.ds(r * PART, PART)
        hat, _ = norm_parts(tokx[rows].astype(F32))
        low2[rows] = (hat * vec[0:1] + vec[1:2]).astype(BF)

        def column(j):
            col = pl.multiple_of(j * 256, 256)
            part = lax.rem(j, 3) * 256
            shift = jnp.where(
                j < 3, vec[2:3, at256(part)], jnp.where(j >= 6, vec[3:4, at256(part)], 0.0)
            )
            value = dot_nn(low2[rows], w1[:, pl.ds(col, 256)]) + shift
            qkv[rows, pl.ds(col, 256)] = (value * jnp.where(j < 3, 0.125, 1.0)).astype(BF)

        loop(3, 9, column)
        c_kv[r].start()
        loop(0, 3, column)

    loads[0].wait()
    loads[1].wait()
    project(0)
    c_tok.wait_recv()
    c_row.wait_recv()
    c_cot.start()
    kaug[pl.ds(PART, PART)] = dot_tn(rowb[1], pick).astype(BF)
    c_aug.start()
    project(1)
    load_we = pltpu.make_async_copy(we_ref, w1, lsem.at[5])
    load_we.start()
    c_kv[0].wait_recv()
    c_kv[1].wait_recv()
    c_aug.wait_recv()

    def attend(pair):
        col = pl.multiple_of(pair * 128, 128)
        ones = jnp.ones((ROWS, 128), BF)
        first = jnp.where(lane_q == 0, 1.0, 0.0).astype(BF)
        k_here = jnp.concatenate([qkv[:, at128(768 + col)], kaug[pl.ds(0, ROWS)]], axis=1)
        k_there = jnp.concatenate([kvr[:, at128(col)], kaug[pl.ds(ROWS, ROWS)]], axis=1)
        v_here = jnp.concatenate([qkv[:, at128(1536 + col)], ones], axis=1)
        v_there = jnp.concatenate([kvr[:, at128(768 + col)], ones], axis=1)
        def scores(unit):
            block, h = unit // 2, unit % 2
            query = qkv[pl.ds(block * PART, PART), at128(col)]
            lifted = jnp.concatenate([query * head_mask[h], first], axis=1)
            return dot_nt(lifted, k_here), dot_nt(lifted, k_there)

        ready = scores(0)
        for unit in range(4):
            block, h = unit // 2, unit % 2
            rows = pl.ds(block * PART, PART)
            s_here, s_there = ready
            if unit < 3:
                ready = scores(unit + 1)
            top = jnp.maximum(
                jnp.max(s_here, axis=-1, keepdims=True), jnp.max(s_there, axis=-1, keepdims=True)
            )
            e_here = jnp.exp(s_here - top).astype(BF)
            e_there = jnp.exp(s_there - top).astype(BF)
            both = dot_nn(e_here, v_here) + dot_nn(e_there, v_there)
            total = both[:, 128:]
            out = both[:, :128] / total
            parts = three_parts(top + jnp.log(total))
            base = 1 + 3 * (2 * pair + h)
            extra = qaug[rows] if h == 0 else extra
            for i in range(3):
                extra = jnp.where(lane_q == base + i, -parts[i], extra)
            if h == 0:
                held = out
            else:
                qaug[rows] = extra
                att[rows, at128(col)] = jnp.where(lane_q < 64, held, out).astype(BF)

    loop(0, 6, attend)

    def turn(rows, block):
        flipped = block.T
        for quarter in range(4):
            seat = pl.multiple_of(p.seat(quarter) * CR, CR)
            turned[pl.ds(seat, CR), rows] = flipped[quarter * CR : (quarter + 1) * CR]

    loads[3].wait()

    def middle(i):
        rows = at256(i * PART)
        value = tokx[rows].astype(F32) + dot_nn(att[rows], wo[...]) + vec[4:5]
        mid[rows] = value
        hat, _ = norm_parts(value)
        block = (hat * vec[5:6] + vec[6:7]).astype(BF)
        low2[rows] = block
        turn(rows, block)

    loop(0, 2, middle)
    loads[2].wait()
    loads[4].wait()
    load_we.wait()
    c_cot.wait_recv()
    y_sum[...] = jnp.zeros_like(y_sum)
    h_sum[...] = jnp.zeros_like(h_sum)

    def feed(t):
        starts = []
        for side in range(2):
            cc = p.core if side == 0 else 1 - p.core
            for yy in range(2):
                starts.append((yy * 2 + cc) * 768 + t * 128)
        w_up = jnp.concatenate([w1[:, at128(s)] for s in starts], axis=1)
        shifts = vec[8:12, at128(t * 128)]
        zeroth = p.core == 0
        shift = jnp.concatenate(
            [
                jnp.where(zeroth, shifts[yy * 2 + s : yy * 2 + s + 1], shifts[yy * 2 + 1 - s : yy * 2 + 2 - s])
                for s in range(2)
                for yy in range(2)
            ],
            axis=1,
        )
        before = dot_nn(low2[...], w_up) + shift
        half = 0.5 + 0.5 * lax.erf(before * 0.7071067811865476)
        active = (before * half).astype(BF)
        slope = half + before * (jnp.exp(before * before * -0.5) * 0.3989422804014327)
        g_t[...] = active
        w_down = jnp.concatenate([wr[at128(s), :] for s in starts], axis=0)
        du_t[...] = (dot_nt(dyx[...], w_down) * slope).astype(BF)
        tall = dot_nn(g_t[...].T, dyx[...]).astype(BF)
        red.slot(2 * t)
        red.put_tall(2 * t, tall)
        red.c_core(2 * t).start()
        red.slot(2 * t + 1)
        for e in range(2):
            seats = [e + 2 * (p.core if cc == 0 else 1 - p.core) for cc in range(2)]
            right = jnp.concatenate([du_t[:, at128(s * 128)] for s in seats], axis=1)
            red.put_wide(2 * t + 1, e, dot_nn(turned[...], right).astype(BF))
        red.c_core(2 * t + 1).start()
        sums = jnp.sum(du_t[...].astype(F32), axis=0, keepdims=True)
        seat = [sums[:, i * 128 : (i + 1) * 128] for i in range(4)]
        vs[8:12, at128(t * 128)] = jnp.concatenate(
            [
                jnp.where(zeroth, seat[yy + 2 * cc], seat[yy + 2 - 2 * cc])
                for yy in range(2)
                for cc in range(2)
            ],
            axis=0,
        )
        red.run_at(t, FEED_STEPS[0])
        y_sum[...] += dot_nn(g_t[...], w_down)
        h_sum[...] += dot_nt(du_t[...], w_up)
        red.run_at(t, FEED_STEPS[1])

    loop(0, 6, feed)
    reload_wi = pltpu.make_async_copy(wi_ref, w1.at[:, pl.ds(0, 2304)], lsem.at[6])
    reload_wi.start()

    def second(i):
        rows = at256(i * PART)
        value = mid[rows]
        lo[rows] = (value + y_sum[rows] + vec[7:8]).astype(BF)
        hat, scale = norm_parts(value)
        grad = h_sum[rows]
        upstream = dyx[rows].astype(F32)
        vs[5:6] += jnp.sum(grad * hat, axis=0, keepdims=True)
        vs[6:7] += jnp.sum(grad, axis=0, keepdims=True)
        vs[7:8] += jnp.sum(upstream, axis=0, keepdims=True)
        total = upstream + norm_back(hat, scale, vec[5:6], grad)
        mid[rows] = total
        block = total.astype(BF)
        low2[rows] = block
        vs[4:5] += jnp.sum(block.astype(F32), axis=0, keepdims=True)
        d_out[rows] = dot_nt(block, wo[...]).astype(BF)
        turn(rows, att[rows])
        red.run_at(i, NORM_STEPS)

    loop(0, 2, second)
    c_lo = swap(6, lo.at[pl.ds(PART, PART)], lo_ref.at[p.y], p.to_y)
    keep_lo = pltpu.make_async_copy(lo.at[pl.ds(0, PART)], lo_ref.at[p.y], lsem.at[7])
    keep_lo.start()

    red.slot(12)
    red.slot(13)
    for k, side, first in ((12, 0, 0), (12, 1, 256), (13, 0, 512)):
        red.put_wide(k, side, dot_nn(turned[...], low2[:, first : first + 256]).astype(BF))
    red.c_core(12).start()
    red.run(OUT_STEPS)

    def turn_first(i):
        rows = at256(i * PART)
        hat, _ = norm_parts(tokx[rows].astype(F32))
        turn(rows, (hat * vec[0:1] + vec[1:2]).astype(BF))

    loop(0, 2, turn_first)

    def in_grad(first):
        return dot_nn(turned[...], dp[:, at256(first)]).astype(BF)

    def put_side(at):
        k, side = 13 + at // 2, lax.rem(at, 2)
        pl.when(side == 0)(lambda: red.slot(k))
        red.put_wide(k, side, in_grad(lax.rem(at - 1, 3) * 768 + (at - 1) // 3 * 256))
        pl.when(side == 1)(lambda: red.c_core(k).start())

    def put_last(k):
        red.slot(k)
        red.put_small(k, in_grad((k + 1) % 3 * 768 + (k - 11) // 3 * 256))
        red.c_core(k).start()

    def in_grads(pair):
        pl.when(pair == 2)(lambda: loop(1, 4, put_side))

        @pl.when(pair == 4)
        def _():
            loop(4, 6, put_side)
            put_last(16)

    def c_dkv(pair):
        return remote(
            dkv_send.at[lax.rem(pair, 2)], dkv_recv.at[pair], ksend.at[pair], krecv.at[pair], p.to_core
        )

    def settle(pair):
        c_dkv(pair).wait_recv()
        slot = lax.rem(pair, 2)
        for i in range(2):
            total = dkv_own[slot, i] + dkv_recv[pair, i].astype(F32)
            dp[:, at128(768 * (i + 1) + pair * 128)] = total.astype(BF)

    lane_k = lax.broadcasted_iota(jnp.int32, (ROWS, 128), 1)

    def attend_back(pair):
        col = pl.multiple_of(pair * 128, 128)
        slot = lax.rem(pair, 2)
        query = qkv[:, at128(col)]
        extra_q = qaug[...].astype(BF)
        grads = d_out[:, at128(col)]
        outs = att[:, at128(col)].astype(F32)
        three = jnp.where(lane_k < 3, 1.0, 0.0).astype(BF)

        @pl.when(pair >= 1)
        def _():
            settle(pair - 1)

        def products(unit):
            h, side = unit // 2, unit % 2
            q_h = query * head_mask[h]
            g_h = grads * head_mask[h]
            parts = three_parts(jnp.sum(g_h.astype(F32) * outs, axis=-1, keepdims=True))
            extra_g = jnp.zeros((ROWS, 128), F32)
            for i in range(3):
                extra_g = jnp.where(lane_k == i, -parts[i], extra_g)
            q_wide = jnp.concatenate([q_h, extra_q], axis=1)
            g_wide = jnp.concatenate([g_h, extra_g.astype(BF)], axis=1)
            base = 1 + 3 * (2 * pair + h)
            mark = jnp.where(
                jnp.logical_and(lane_k >= base, lane_k < base + 3), 1.0, 0.0
            ).astype(BF)
            if side == 0:
                key, value = qkv[:, at128(768 + col)], qkv[:, at128(1536 + col)]
            else:
                key, value = kvr[:, at128(col)], kvr[:, at128(768 + col)]
            k_wide = jnp.concatenate([key, kaug[pl.ds(side * ROWS, ROWS)] + mark], axis=1)
            v_wide = jnp.concatenate([value, three], axis=1)
            return dot_nt(k_wide, q_wide), dot_nt(v_wide, g_wide), q_h, g_h, (key * head_mask[h]).T

        ready = products(0)
        for unit in range(4):
            h, side = unit // 2, unit % 2
            score, slope, q_h, g_h, key_t = ready
            if unit < 3 and unit not in CUTS:
                ready = products(unit + 1)
            weight = jnp.exp(score)
            slope = (weight * slope).astype(BF)
            add_k, add_v = dot_nn(slope, q_h), dot_nn(weight.astype(BF), g_h)
            add_q = dot_nn(key_t, slope)
            if unit == 0:
                dq_sum[...] = add_q
            else:
                dq_sum[...] += add_q
            sums = dkv_own.at[slot] if side == 0 else dkv_far
            if h == 0:
                sums[0] = add_k
                sums[1] = add_v
            else:
                sums[0] += add_k
                sums[1] += add_v
            if unit in CUTS:
                red.run_at(pair, ATTEND_STEPS[CUTS.index(unit)])
                if unit < 3:
                    ready = products(unit + 1)
        dp[:, at128(col)] = (dq_sum[...].T.astype(BF).astype(F32) * 0.125).astype(BF)

        @pl.when(pair >= 2)
        def _():
            c_dkv(pair - 2).wait_send()

        dkv_send[slot] = dkv_far[...].astype(BF)
        c_dkv(pair).start()
        in_grads(pair)
        pl.when(pair == 1)(lambda: c_lo.start())

    loop(0, 6, attend_back)
    settle(5)
    c_dkv(4).wait_send()
    c_dkv(5).wait_send()

    for k in range(17, 20):
        put_last(k)
    red.run(PROJECT_STEPS)
    vs[2:3] = jnp.sum(dp[:, 0:768].astype(F32), axis=0, keepdims=True)
    vs[3:4] = jnp.sum(dp[:, 1536:2304].astype(F32), axis=0, keepdims=True)
    reload_wi.wait()

    def first_back(i):
        rows = at256(i * PART)
        grad = dot_nt(dp[rows], w1[:, pl.ds(0, 2304)])
        hat, scale = norm_parts(tokx[rows].astype(F32))
        vs[0:1] += jnp.sum(grad * hat, axis=0, keepdims=True)
        vs[1:2] += jnp.sum(grad, axis=0, keepdims=True)
        y_sum[rows] = mid[rows] + norm_back(hat, scale, vec[0:1], grad)
        red.run_at(i, LAST_STEPS)

    loop(0, 2, first_back)
    gts[...] = y_sum[pl.ds(PART, PART)].astype(BF)
    c_gt = swap(7, gts, gtr_ref, p.to_y)
    keep_gt = pltpu.make_async_copy(y_sum.at[pl.ds(0, PART)], gto_ref, lsem.at[8])
    c_gt.start()
    keep_gt.start()

    def c_vec(stage, peer):
        return remote(vr.at[2 * stage], vr.at[2 * stage + 1], vsend.at[stage], vrecv.at[stage], peer)

    def vec_pair(stage, peer):
        vr[2 * stage] = vs[...]
        c_vec(stage, peer).start()

    def vec_take(stage, peer):
        c_vec(stage, peer).wait()
        vs[...] += vr[2 * stage + 1]

    def vec_0():
        vec_take(0, p.to_core)
        vec_pair(1, p.to_y)

    def vec_1():
        vec_take(1, p.to_y)
        vec_pair(2, p.to_x)

    def vec_2():
        vec_take(2, p.to_x)

        @pl.when(p.outer)
        def _():
            vec_pair(3, p.to_mate)

    def vec_3():
        @pl.when(p.inner)
        def _():
            c_vec(3, p.to_mate).wait_recv()
            vs[...] += vr[7]
            vec_pair(4, p.to_far)

    def vec_4():
        @pl.when(p.inner)
        def _():
            vec_take(4, p.to_far)
            vec_pair(3, p.to_mate)

    def vec_5():
        @pl.when(p.outer)
        def _():
            c_vec(3, p.to_mate).wait_recv()
            vs[...] = vr[7]

        c_vec(3, p.to_mate).wait_send()

    vec_pair(0, p.to_core)
    vec_steps = (vec_0, vec_1, vec_2, vec_3, vec_4, vec_5)
    for step in DRAIN_STEPS:
        if step < 100:
            vec_steps[step]()
        else:
            red.run((step,))
    red.close()
    c_tok.wait_send()
    c_row.wait_send()
    c_cot.wait_send()
    c_aug.wait_send()
    c_kv[0].wait_send()
    c_kv[1].wait_send()
    c_lo.wait()
    c_gt.wait()
    keep_lo.wait()
    keep_gt.wait()


def finish_kernel(
    tot_ref, vs, lo_in, gto, gtr_ref,
    lo_out, gt, g0, g1, wi_out, g2, wo_out, g4, g5, g6, we_out, g8, wr_out, g7,
    tot, gtr, gt_s, lo_s, wi, wo, we, wr, in_sem, out_sem,
):
    y = lax.axis_index("frame") // 2
    frame = lax.axis_index("frame")
    spans = [(2 * t, 2) for t in range(6)] + [(12, 2), (14, 2), (16, 2)]
    loads = [
        pltpu.make_async_copy(tot_ref.at[pl.ds(k, n)], tot.at[pl.ds(k, n)], in_sem.at[i])
        for i, (k, n) in enumerate(spans)
    ]
    loads += [
        pltpu.make_async_copy(gtr_ref, gtr, in_sem.at[9]),
        pltpu.make_async_copy(gto, gt_s.at[0], in_sem.at[10]),
        pltpu.make_async_copy(lo_in, lo_s, in_sem.at[11]),
    ]
    for one in loads:
        one.start()
    outs = []

    def leave(src, dst):
        one = pltpu.make_async_copy(src, dst, out_sem.at[len(outs)])
        one.start()
        outs.append(one)

    for t in range(6):
        loads[t].wait()
        rows = pl.ds(t * 128, 128)
        for i in range(6):
            block = slice(i % 3 * 128, (i % 3 + 1) * 128)
            wr[rows, i * 128 : (i + 1) * 128] = tot[2 * t, i // 3, block].astype(F32)
        leave(wr.at[rows], wr_out.at[rows])
        for j in range(4):
            cols = pl.ds(j * 768 + t * 128, 128)
            block = slice(j % 2 * CR, (j % 2 + 1) * CR)
            we[:, cols] = tot[2 * t + 1, j // 2, block].astype(F32)
    leave(we, we_out)
    for n, col in enumerate(COLUMNS):
        if n % 8 == 0:
            loads[6 + n // 8].wait()
        block = slice(n % 2 * CR, (n % 2 + 1) * CR)
        value = tot[12 + n // 4, n % 4 // 2, block].astype(F32)
        if n < 6:
            wo[:, col * 128 : (col + 1) * 128] = value
        else:
            wi[:, col * 128 : (col + 1) * 128] = value
        if n == 5:
            leave(wo, wo_out)
    leave(wi, wi_out)
    loads[9].wait()
    gt_s[1] = gtr[...].astype(F32)
    leave(gt_s.at[1], gt.at[1 - y, 0])
    loads[10].wait()
    leave(gt_s.at[0], gt.at[y, 0])
    loads[11].wait()
    leave(lo_s.at[0], lo_out.at[0, 0])
    leave(lo_s.at[1], lo_out.at[1, 0])
    mine = vs[0:8, 0:CR]
    row = vs[8:9]
    for f in range(1, 4):
        mine = jnp.where(frame == f, vs[0:8, f * CR : (f + 1) * CR], mine)
        row = jnp.where(frame == f, vs[8 + f : 9 + f], row)
    g0[...] = mine[0]
    g1[...] = mine[1]
    g2[...] = mine[2:4]
    g4[...] = mine[4]
    g5[...] = mine[5]
    g6[...] = mine[6]
    g7[...] = mine[7]
    g8[...] = row[0]
    for one in outs:
        one.wait()


def local_slice(
    tokens,
    counts,
    first_gain,
    first_bias,
    input_weight,
    input_bias,
    output_weight,
    output_bias,
    second_gain,
    second_bias,
    expand_weight,
    expand_bias,
    reduce_weight,
    reduce_bias,
    cotangent,
):
    anywhere = pl.BlockSpec(memory_space=pl.ANY)
    vmem = pl.BlockSpec(memory_space=pltpu.VMEM)
    smem = pl.BlockSpec(memory_space=pltpu.SMEM)
    shape = jax.ShapeDtypeStruct
    dma = pltpu.SemaphoreType.DMA
    tot, vs, lo, gto, gtr = pl.pallas_call(
        layer_kernel,
        out_shape=(
            shape((BUFFERS, 2, HR, 128), BF),
            shape((16, D), F32),
            shape((2, PART, D), BF),
            shape((PART, D), F32),
            shape((PART, D), BF),
        ),
        in_specs=[anywhere, anywhere, smem] + [vmem] * 8 + [anywhere] * 4,
        out_specs=(anywhere, vmem, anywhere, anywhere, anywhere),
        scratch_shapes=[
            pltpu.VMEM((BUFFERS, 2, 2, HR, 128), BF),
            pltpu.VMEM((SLOT_COUNT, 2, 2, HR, 128), BF),
            pltpu.VMEM((BUFFERS, 2, 2, HR, 128), BF),
            pltpu.VMEM((BUFFERS, 2, HR, 128), BF),
            pltpu.VMEM((BUFFERS, HR, 128), BF),
            pltpu.VMEM((BUFFERS, HR, 128), BF),
            pltpu.VMEM((BUFFERS, HR, 128), BF),
            pltpu.VMEM((12, D), F32),
            pltpu.VMEM((ROWS, D), BF),
            pltpu.VMEM((ROWS, D), BF),
            pltpu.VMEM((D, FF), BF),
            pltpu.VMEM((D, D), BF),
            pltpu.VMEM((FF, D), BF),
            pltpu.VMEM((ROWS, 3 * D), BF),
            pltpu.VMEM((ROWS, 2 * D), BF),
            pltpu.VMEM((3, 16, PART), BF),
            pltpu.VMEM((2 * ROWS, 128), BF),
            pltpu.VMEM((ROWS, 128), F32),
            pltpu.VMEM((ROWS, D), BF),
            pltpu.VMEM((ROWS, D), F32),
            pltpu.VMEM((ROWS, D), BF),
            pltpu.VMEM((D, ROWS), BF),
            pltpu.VMEM((ROWS, ROWS), BF),
            pltpu.VMEM((ROWS, ROWS), BF),
            pltpu.VMEM((ROWS, D), F32),
            pltpu.VMEM((ROWS, D), F32),
            pltpu.VMEM((ROWS, D), BF),
            pltpu.VMEM((ROWS, 3 * D), BF),
            pltpu.VMEM((128, ROWS), F32),
            pltpu.VMEM((2, 2, ROWS, 128), F32),
            pltpu.VMEM((2, ROWS, 128), F32),
            pltpu.VMEM((2, 2, ROWS, 128), BF),
            pltpu.VMEM((6, 2, ROWS, 128), BF),
            pltpu.VMEM((ROWS, D), BF),
            pltpu.VMEM((PART, D), BF),
            pltpu.VMEM((10, 16, D), F32),
            dma((SLOT_COUNT,)),
            dma((12,)),
            dma((6, K)),
            dma((9,)),
            dma((8,)),
            dma((8,)),
            dma((6,)),
            dma((6,)),
            dma((5,)),
            dma((5,)),
        ],
        compiler_params=pltpu.CompilerParams(
            collective_id=0, has_side_effects=True, vmem_limit_bytes=62 << 20
        ),
    )(
        tokens,
        cotangent,
        counts,
        first_gain,
        first_bias,
        input_bias,
        output_bias,
        second_gain,
        second_bias,
        expand_bias,
        reduce_bias,
        input_weight,
        output_weight,
        expand_weight,
        reduce_weight,
    )
    return pl.pallas_call(
        finish_kernel,
        out_shape=(
            shape((MICRO, 1, PART, D), BF),
            shape((MICRO, 1, PART, D), F32),
            shape((CR,), F32),
            shape((CR,), F32),
            shape((CR, 3 * D), F32),
            shape((2, CR), F32),
            shape((CR, D), F32),
            shape((CR,), F32),
            shape((CR,), F32),
            shape((CR,), F32),
            shape((CR, FF), F32),
            shape((D,), F32),
            shape((D, D), F32),
            shape((CR,), F32),
        ),
        in_specs=[anywhere, vmem, anywhere, anywhere, anywhere],
        out_specs=tuple(anywhere if i in (0, 1, 4, 6, 10, 12) else vmem for i in range(14)),
        scratch_shapes=[
            pltpu.VMEM((BUFFERS, 2, HR, 128), BF),
            pltpu.VMEM((PART, D), BF),
            pltpu.VMEM((2, PART, D), F32),
            pltpu.VMEM((2, PART, D), BF),
            pltpu.VMEM((CR, 3 * D), F32),
            pltpu.VMEM((CR, D), F32),
            pltpu.VMEM((CR, FF), F32),
            pltpu.VMEM((D, D), F32),
            dma((12,)),
            dma((16,)),
        ],
        compiler_params=pltpu.CompilerParams(vmem_limit_bytes=62 << 20),
    )(tot, vs, lo, gto, gtr)


def solution(mesh):
    fits = mesh.shape["clip"] == 8 and mesh.shape["frame"] == 4
    return jax.shard_map(
        local_slice if fits else local,
        mesh=mesh,
        in_specs=(
            P(None, "clip", "frame", None),
            P(None, "clip", "frame"),
            P(),
            P(),
            P(),
            P(),
            P(),
            P(),
            P(),
            P(),
            P(),
            P(),
            P(),
            P(),
            P(None, "clip", "frame", None),
        ),
        out_specs=(
            P(None, "clip", "frame", None),
            P(None, "clip", "frame", None),
            P("frame"),
            P("frame"),
            P("frame", None),
            P(None, "frame"),
            P("frame", None),
            P("frame"),
            P("frame"),
            P("frame"),
            P("frame", None),
            P("frame"),
            P("frame", None),
            P("frame"),
        ),
        check_vma=False,
    )
```

```python
import jax
import jax.numpy as jnp
from jax import lax
from jax.experimental import pallas as pl
from jax.experimental.pallas import tpu as pltpu
from jax.sharding import PartitionSpec as P

D = 768
H = 12
HD = 64
MICRO = 2
FRAME_DEV = 4
SLOTS = 64
BLOCK = 256


epsilon = 1e-06


def from_behind(block, axis, distance):
    devices = range(lax.axis_size(axis))
    route = [((i - distance) % len(devices), i) for i in devices]
    return lax.ppermute(block, axis, route)


def norm_rows(values, gain, shift):
    mean = jnp.mean(values, axis=-1, keepdims=True)
    centred = values - mean
    spread = jnp.mean(centred * centred, axis=-1, keepdims=True)
    return centred * lax.rsqrt(spread + epsilon) * gain + shift


def gelu_exact(values):
    return jax.nn.gelu(values, approximate=False)


def key_valid(every_count, source):
    frame_counts = lax.dynamic_slice_in_dim(every_count, source * FRAME_DEV, FRAME_DEV, 1)
    slot_index = jnp.arange(SLOTS, dtype=jnp.int32)
    return (slot_index[None, None, :] < frame_counts[:, :, None]).reshape(MICRO, BLOCK)


def scores_of(query, keys, valid):
    key_heads = keys.reshape(MICRO, BLOCK, H, HD)
    scores = jnp.einsum("mqhd,mkhd->mhqk", query, key_heads, preferred_element_type=jnp.float32)
    return jnp.where(valid[:, None, None, :], scores, -1e30)


def absorb(state, query, keys, values, valid):
    top, total, summed = state
    scores = scores_of(query, keys, valid)
    new_top = jnp.maximum(top, jnp.max(scores, axis=-1, keepdims=True))
    factor = jnp.exp(top - new_top)
    lifted = jnp.exp(scores - new_top)
    total = total * factor + jnp.sum(lifted, axis=-1, keepdims=True)
    value_heads = values.reshape(MICRO, BLOCK, H, HD)
    summed = summed * factor + jnp.einsum(
        "mhqk,mkhd->mhqd",
        lifted.astype(jnp.bfloat16),
        value_heads,
        preferred_element_type=jnp.float32,
    )
    return (new_top, total, summed)


def block_back(query, keys, values, valid, log_total, delta, grad_heads):
    scores = scores_of(query, keys, valid)
    weights = jnp.exp(scores - log_total)
    key_heads = keys.reshape(MICRO, BLOCK, H, HD)
    value_heads = values.reshape(MICRO, BLOCK, H, HD)
    grad_weights = jnp.einsum(
        "mqhd,mkhd->mhqk", grad_heads, value_heads, preferred_element_type=jnp.float32
    )
    grad_scores = (weights * (grad_weights - delta)).astype(jnp.bfloat16)
    grad_query = jnp.einsum(
        "mhqk,mkhd->mqhd", grad_scores, key_heads, preferred_element_type=jnp.float32
    )
    grad_keys = jnp.einsum(
        "mhqk,mqhd->mkhd", grad_scores, query, preferred_element_type=jnp.float32
    )
    grad_values = jnp.einsum(
        "mhqk,mqhd->mkhd",
        weights.astype(jnp.bfloat16),
        grad_heads,
        preferred_element_type=jnp.float32,
    )
    return (grad_query, grad_keys.reshape(MICRO, BLOCK, D), grad_values.reshape(MICRO, BLOCK, D))


def local(
    tokens,
    counts,
    first_gain,
    first_bias,
    input_weight,
    input_bias,
    output_weight,
    output_bias,
    second_gain,
    second_bias,
    expand_weight,
    expand_bias,
    reduce_weight,
    reduce_bias,
    cotangent,
):
    members = lax.axis_size("frame")
    myself = lax.axis_index("frame")
    total_rows = MICRO * BLOCK
    seq_in = tokens.reshape(total_rows, D).astype(jnp.float32)
    every_count = lax.all_gather(counts.reshape(MICRO, FRAME_DEV), "frame", axis=1, tiled=True)
    gain_one = first_gain.astype(jnp.float32)
    shift_one = first_bias.astype(jnp.float32)
    gain_two = second_gain.astype(jnp.float32)
    shift_two = second_bias.astype(jnp.float32)
    qv_bias = input_bias.astype(jnp.float32)
    first_low = norm_rows(seq_in, gain_one, shift_one).astype(jnp.bfloat16)
    projected = jnp.dot(first_low, input_weight, preferred_element_type=jnp.float32)
    query = (
        ((projected[:, :D] + qv_bias[0]) * 0.125).astype(jnp.bfloat16).reshape(MICRO, BLOCK, H, HD)
    )
    keys = projected[:, D : 2 * D].astype(jnp.bfloat16).reshape(MICRO, BLOCK, D)
    values = (projected[:, 2 * D :] + qv_bias[1]).astype(jnp.bfloat16).reshape(MICRO, BLOCK, D)
    start = (
        jnp.full((MICRO, H, BLOCK, 1), -1e30, jnp.float32),
        jnp.zeros((MICRO, H, BLOCK, 1), jnp.float32),
        jnp.zeros((MICRO, H, BLOCK, HD), jnp.float32),
    )
    state = absorb(start, query, keys, values, key_valid(every_count, myself))
    stored = ()

    def forward_hop(step, carry):
        state_now, moving, kept = carry
        moving = from_behind((moving[0], moving[1]), "frame", 1)
        source = (myself - step) % members
        state_now = absorb(state_now, query, moving[0], moving[1], key_valid(every_count, source))
        return (state_now, moving, kept)

    state, _, stored = lax.fori_loop(1, members, forward_hop, (state, (keys, values), stored))
    top, total, summed = state
    log_total = top + jnp.log(total)
    attend_full = jnp.transpose(summed / total, (0, 2, 1, 3))
    attend_low = attend_full.reshape(total_rows, D).astype(jnp.bfloat16)
    middle = (
        seq_in
        + jnp.dot(attend_low, output_weight, preferred_element_type=jnp.float32)
        + output_bias.astype(jnp.float32)
    )
    second_low = norm_rows(middle, gain_two, shift_two).astype(jnp.bfloat16)
    before = jnp.dot(
        second_low, expand_weight, preferred_element_type=jnp.float32
    ) + expand_bias.astype(jnp.float32)
    active_low = gelu_exact(before).astype(jnp.bfloat16)
    result = (
        middle
        + jnp.dot(active_low, reduce_weight, preferred_element_type=jnp.float32)
        + reduce_bias.astype(jnp.float32)
    )
    layer_out = result.astype(jnp.bfloat16).reshape(MICRO, 1, BLOCK, D)
    upstream_low = cotangent.reshape(total_rows, D)
    upstream = upstream_low.astype(jnp.float32)
    grad_reduce_weight = jnp.dot(active_low.T, upstream_low, preferred_element_type=jnp.float32)
    grad_reduce_bias = jnp.sum(upstream, axis=0)
    grad_active = jnp.dot(upstream_low, reduce_weight.T, preferred_element_type=jnp.float32)
    _, gelu_back = jax.vjp(gelu_exact, before)
    grad_before = gelu_back(grad_active)[0].astype(jnp.bfloat16)
    grad_expand_weight = jnp.dot(second_low.T, grad_before, preferred_element_type=jnp.float32)
    grad_expand_bias = jnp.sum(grad_before.astype(jnp.float32), axis=0)
    grad_second = jnp.dot(grad_before, expand_weight.T, preferred_element_type=jnp.float32)
    _, second_back = jax.vjp(norm_rows, middle, gain_two, shift_two)
    middle_part, grad_second_gain, grad_second_bias = second_back(grad_second)
    grad_middle = upstream + middle_part
    grad_branch = grad_middle.astype(jnp.bfloat16)
    grad_output_weight = jnp.dot(attend_low.T, grad_branch, preferred_element_type=jnp.float32)
    grad_output_bias = jnp.sum(grad_branch.astype(jnp.float32), axis=0)
    grad_attend = jnp.dot(grad_branch, output_weight.T, preferred_element_type=jnp.float32).astype(
        jnp.bfloat16
    )
    grad_heads = grad_attend.reshape(MICRO, BLOCK, H, HD)
    delta = jnp.transpose(
        jnp.sum(grad_heads.astype(jnp.float32) * attend_full, axis=-1), (0, 2, 1)
    )[..., None]
    first_terms = block_back(
        query, keys, values, key_valid(every_count, myself), log_total, delta, grad_heads
    )

    def backward_hop(step, carry):
        grad_query, running, moving = carry
        running = (
            from_behind(running[0].astype(jnp.bfloat16), "frame", 1).astype(jnp.float32),
            from_behind(running[1].astype(jnp.bfloat16), "frame", 1).astype(jnp.float32),
        )
        current = from_behind((moving[0], moving[1]), "frame", 1)
        source = (myself - step) % members
        add_query, add_keys, add_values = block_back(
            query,
            current[0],
            current[1],
            key_valid(every_count, source),
            log_total,
            delta,
            grad_heads,
        )
        return (grad_query + add_query, (running[0] + add_keys, running[1] + add_values), current)

    grad_query, running, _ = lax.fori_loop(
        1, members, backward_hop, (first_terms[0], (first_terms[1], first_terms[2]), (keys, values))
    )
    finished = (
        from_behind(running[0].astype(jnp.bfloat16), "frame", 1).astype(jnp.float32),
        from_behind(running[1].astype(jnp.bfloat16), "frame", 1).astype(jnp.float32),
    )
    query_low = grad_query.astype(jnp.bfloat16).reshape(total_rows, D) * 0.125
    keys_low = finished[0].astype(jnp.bfloat16).reshape(total_rows, D)
    values_low = finished[1].astype(jnp.bfloat16).reshape(total_rows, D)
    grad_projected = jnp.concatenate([query_low, keys_low, values_low], axis=1)
    grad_input_weight = jnp.dot(first_low.T, grad_projected, preferred_element_type=jnp.float32)
    grad_input_bias = jnp.stack(
        [
            jnp.sum(query_low.astype(jnp.float32), axis=0),
            jnp.sum(values_low.astype(jnp.float32), axis=0),
        ]
    )
    grad_first = jnp.dot(grad_projected, input_weight.T, preferred_element_type=jnp.float32)
    _, first_back = jax.vjp(norm_rows, seq_in, gain_one, shift_one)
    input_part, grad_first_gain, grad_first_bias = first_back(grad_first)
    grad_tokens = (grad_middle + input_part).reshape(MICRO, 1, BLOCK, D)
    shares = (
        lax.psum_scatter(
            grad_first_gain.astype(jnp.bfloat16), "frame", scatter_dimension=0, tiled=True
        ).astype(jnp.float32),
        lax.psum_scatter(
            grad_first_bias.astype(jnp.bfloat16), "frame", scatter_dimension=0, tiled=True
        ).astype(jnp.float32),
        lax.psum_scatter(
            grad_input_weight.astype(jnp.bfloat16), "frame", scatter_dimension=0, tiled=True
        ).astype(jnp.float32),
        lax.psum_scatter(
            grad_input_bias.astype(jnp.bfloat16), "frame", scatter_dimension=1, tiled=True
        ).astype(jnp.float32),
        lax.psum_scatter(
            grad_output_weight.astype(jnp.bfloat16), "frame", scatter_dimension=0, tiled=True
        ).astype(jnp.float32),
        lax.psum_scatter(
            grad_output_bias.astype(jnp.bfloat16), "frame", scatter_dimension=0, tiled=True
        ).astype(jnp.float32),
        lax.psum_scatter(
            grad_second_gain.astype(jnp.bfloat16), "frame", scatter_dimension=0, tiled=True
        ).astype(jnp.float32),
        lax.psum_scatter(
            grad_second_bias.astype(jnp.bfloat16), "frame", scatter_dimension=0, tiled=True
        ).astype(jnp.float32),
        lax.psum_scatter(
            grad_expand_weight.astype(jnp.bfloat16), "frame", scatter_dimension=0, tiled=True
        ).astype(jnp.float32),
        lax.psum_scatter(
            grad_expand_bias.astype(jnp.bfloat16), "frame", scatter_dimension=0, tiled=True
        ).astype(jnp.float32),
        lax.psum_scatter(
            grad_reduce_weight.astype(jnp.bfloat16), "frame", scatter_dimension=0, tiled=True
        ).astype(jnp.float32),
        lax.psum_scatter(
            grad_reduce_bias.astype(jnp.bfloat16), "frame", scatter_dimension=0, tiled=True
        ).astype(jnp.float32),
    )
    totals = (
        lax.psum(shares[0].astype(jnp.bfloat16), "clip").astype(jnp.float32),
        lax.psum(shares[1].astype(jnp.bfloat16), "clip").astype(jnp.float32),
        lax.psum(shares[2].astype(jnp.bfloat16), "clip").astype(jnp.float32),
        lax.psum(shares[3].astype(jnp.bfloat16), "clip").astype(jnp.float32),
        lax.psum(shares[4].astype(jnp.bfloat16), "clip").astype(jnp.float32),
        lax.psum(shares[5].astype(jnp.bfloat16), "clip").astype(jnp.float32),
        lax.psum(shares[6].astype(jnp.bfloat16), "clip").astype(jnp.float32),
        lax.psum(shares[7].astype(jnp.bfloat16), "clip").astype(jnp.float32),
        lax.psum(shares[8].astype(jnp.bfloat16), "clip").astype(jnp.float32),
        lax.psum(shares[9].astype(jnp.bfloat16), "clip").astype(jnp.float32),
        lax.psum(shares[10].astype(jnp.bfloat16), "clip").astype(jnp.float32),
        lax.psum(shares[11].astype(jnp.bfloat16), "clip").astype(jnp.float32),
    )
    return (
        layer_out,
        grad_tokens,
        totals[0],
        totals[1],
        totals[2],
        totals[3],
        totals[4],
        totals[5],
        totals[6],
        totals[7],
        totals[8],
        totals[9],
        totals[10],
        totals[11],
    )


MESH = pl.DeviceIdType.MESH
BF = jnp.bfloat16
F32 = jnp.float32
K = 20
BUFFERS = 18
QR = 768
HR = 384
CR = 192
SLOT_COUNT = 4
ROWS = 512
PART = 256
FF = 3072
LOW = -1e30
COLUMNS = (0, 1, 2, 3, 4, 5, 0, 1, 6, 7, 12, 13, 2, 3, 8, 9, 14, 4, 15, 5, 10, 16, 11, 17)
LAST_BIG = 16
WAYS = "acabcbbccbabcabaaaab"
CUTS = (0, 1, 2, 3)
FEED_STEPS = (((), (), (101, 102), (104,), (200, 106), (203, 202, 108, 109)), ((), (100,), (103,), (105,), (201, 107), (204,)))
NORM_STEPS = ((301, 205, 110), (111,))
OUT_STEPS = (303, 300, 207)
ATTEND_STEPS = (((304,), (302,), (401,), (405, 211, 309, 404, 603, 402), (504, 601), (311, 506, 214)), ((), (403,), (503, 306), (501, 310, 113, 600, 407, 114), (), (508, 604, 602, 115)), ((112, 305, 206), (210,), (212,), (406, 408, 505), (502, 410), (412, 116, 213, 607)), ((208,), (400, 307, 209), (308, 500), (409,), (312, 507, 605), (509, 411, 606, 314)))
PROJECT_STEPS = (510, 608, 512)
LAST_STEPS = ((215, 117, 511, 313, 118, 119, 216, 414, 609), (612, 610))
DRAIN_STEPS = (217, 315, 413, 514, 0, 218, 219, 611, 316, 1, 513, 415, 2, 416, 614, 3, 317, 515, 613, 318, 516, 4, 319, 417, 418, 615, 5, 616, 419, 517, 518, 519, 617, 618, 619)


def dot_nn(a, b):
    return lax.dot_general(a, b, (((1,), (0,)), ((), ())), preferred_element_type=F32)


def dot_nt(a, b):
    return lax.dot_general(a, b, (((1,), (1,)), ((), ())), preferred_element_type=F32)


def dot_tn(a, b):
    return lax.dot_general(a, b, (((0,), (0,)), ((), ())), preferred_element_type=F32)


def at128(index):
    return pl.ds(pl.multiple_of(index, 128), 128)


def at256(index):
    return pl.ds(pl.multiple_of(index, 256), 256)


def loop(low, high, body):
    def step(i, carry):
        body(i)
        return carry

    lax.fori_loop(low, high, step, 0)


class Place:
    def __init__(self):
        self.clip = lax.axis_index("clip")
        self.frame = lax.axis_index("frame")
        self.x = lax.rem(self.clip, 2)
        self.z = self.clip // 2
        self.core = lax.rem(self.frame, 2)
        self.y = self.frame // 2
        self.outer = jnp.logical_or(self.z == 0, self.z == 3)
        self.inner = jnp.logical_not(self.outer)
        self.to_core = (self.clip, self.y * 2 + (1 - self.core))
        self.to_y = (self.clip, (1 - self.y) * 2 + self.core)
        self.to_x = (self.z * 2 + (1 - self.x), self.frame)
        mate = self.z + 1 - 2 * lax.rem(self.z, 2)
        self.to_mate = (mate * 2 + self.x, self.frame)
        self.to_far = ((3 - self.z) * 2 + self.x, self.frame)
        self.h = jnp.where(self.inner, 1, 0)

    def seat(self, quarter):
        yy, cc = quarter // 2, quarter % 2
        return yy + 2 * (self.core if cc == 0 else 1 - self.core)


def enter(place):
    barrier = pltpu.get_barrier_semaphore()
    for peer in (place.to_core, place.to_y, place.to_x, place.to_mate, place.to_far):
        pl.semaphore_signal(barrier, inc=1, device_id=peer, device_id_type=MESH)
    pl.semaphore_wait(barrier, 5)


def remote(src, dst, send, recv, peer):
    return pltpu.make_async_remote_copy(
        src_ref=src, dst_ref=dst, send_sem=send, recv_sem=recv, device_id=peer, device_id_type=MESH
    )


class Reduce:
    def __init__(self, place, bufs, tot, csend, send, recv):
        self.p = place
        self.own, self.nbr, self.rc, self.ry, self.rx, self.r1, self.r2 = bufs
        self.tot, self.csend, self.send, self.recv = tot, csend, send, recv

    def copy(self, src, dst, kind, stage, k, peer):
        return remote(src, dst, self.send.at[kind], self.recv.at[stage, k], peer)

    def last(self, src, dst, kind, end, peer):
        return remote(src, dst, self.send.at[kind], self.send.at[end], peer)

    def place(self, k):
        if k < LAST_BIG:
            return k, 0, HR
        return LAST_BIG + (k - LAST_BIG) // 2, (k - LAST_BIG) % 2 * CR, CR

    def part(self, k, far):
        _, low, rows = self.place(k)
        side = 1 - self.p.x if far else self.p.x
        return pl.ds(pl.multiple_of(low + side * (rows // 2), 32), rows // 2)

    def c_core(self, k):
        slot = self.seat(k)
        src, dst = self.nbr.at[slot], self.rc.at[k] if not isinstance(k, int) or k < LAST_BIG else None
        if dst is None:
            b, low, rows = self.place(k)
            src, dst = self.nbr.at[slot, :, :, pl.ds(0, rows)], self.rc.at[b, :, :, pl.ds(low, rows)]
        return remote(src, dst, self.csend.at[slot], self.recv.at[0, k], self.p.to_core)

    def side(self, ref, k, *lead):
        b, low, rows = self.place(k)
        return ref.at[(b, *lead, pl.ds(low, rows))]

    def a_y(self, k):
        return self.copy(
            self.side(self.own, k, 1 - self.p.y, slice(None)), self.side(self.ry, k, slice(None)), 0, 1, k, self.p.to_y
        )

    def a_x(self, k):
        return self.copy(
            self.side(self.own, k, self.p.y, 1 - self.p.x), self.side(self.rx, k), 1, 2, k, self.p.to_x
        )

    def b_x(self, k):
        return self.copy(
            self.side(self.own, k, slice(None), 1 - self.p.x), self.side(self.ry, k, slice(None)), 0, 1, k, self.p.to_x
        )

    def b_y(self, k):
        return self.copy(
            self.side(self.own, k, 1 - self.p.y, self.p.x), self.side(self.rx, k), 1, 2, k, self.p.to_y
        )

    def half(self, k):
        return self.side(self.own, k, self.p.y, self.p.x)

    def l_in(self, k):
        return self.copy(self.half(k), self.side(self.r1, k), 2, 3, k, self.p.to_mate)

    def l_mid(self, k):
        return self.copy(self.half(k), self.side(self.r2, k), 3, 4, k, self.p.to_far)

    def l_out(self, k):
        return self.copy(self.side(self.r2, k), self.side(self.r1, k), 2, 3, k, self.p.to_mate)

    def l_leave(self, k, inner):
        src = self.side(self.r2 if inner else self.r1, k)
        dst = self.side(self.tot, k, self.p.x)
        self.last(src, dst, 4, 5, self.p.to_x).start()
        self.keep(src, dst).start()

    def q_pair(self, k):
        return self.copy(
            self.side(self.own, k, slice(None), 1 - self.p.h),
            self.side(self.ry, k, slice(None)),
            0,
            1,
            k,
            self.p.to_mate,
        )

    def q_y(self, k):
        return self.copy(
            self.side(self.own, k, 1 - self.p.y, self.p.h), self.side(self.rx, k), 1, 2, k, self.p.to_y
        )

    def q_own(self, k, far):
        return self.own.at[self.place(k)[0], self.p.y, self.p.h, self.part(k, far)]

    def q_in(self, k, second):
        b, low, rows = self.place(k)
        return self.r1.at[b, pl.ds(low + second * (rows // 2), rows // 2)]

    def q_x(self, k):
        return self.copy(self.q_own(k, True), self.q_in(k, 0), 6, 3, k, self.p.to_x)

    def q_far(self, k):
        return self.copy(self.q_own(k, False), self.q_in(k, 1), 7, 4, k, self.p.to_far)

    def q_gather(self, k):
        both = self.r2.at[self.place(k)[0], self.part(k, False)]
        return self.copy(both, both, 8, 5, k, self.p.to_x)

    def q_leave(self, k):
        src, dst = self.side(self.r2, k), self.side(self.tot, k, self.p.h)
        self.last(src, dst, 9, 10, self.p.to_mate).start()
        self.keep(src, dst).start()

    def keep(self, src, dst):
        return pltpu.make_async_copy(src, dst, self.send.at[11])

    def split(self, k, a, b, c):
        {"a": a, "b": b, "c": c}[WAYS[k]](k)

    def seat(self, k):
        return k % SLOT_COUNT if isinstance(k, int) else lax.rem(k, SLOT_COUNT)

    def slot(self, k):
        if isinstance(k, int):
            self.c_core(k - SLOT_COUNT).wait_send()
        else:
            pl.when(k >= SLOT_COUNT)(lambda: self.c_core(k - SLOT_COUNT).wait_send())

    def put_wide(self, k, side, grad):
        slot = self.seat(k)
        for yy in range(2):
            for i in range(2):
                rows = slice(i * CR, (i + 1) * CR)
                cols = slice(i * 128, (i + 1) * 128)
                self.own[k, yy, side, rows] = grad[yy * CR : (yy + 1) * CR, cols]
                self.nbr[slot, yy, side, rows] = grad[(2 + yy) * CR : (3 + yy) * CR, cols]

    def put_small(self, k, grad):
        slot = self.seat(k)
        b, low, rows = self.place(k)
        for yy in range(2):
            for i in range(2):
                cols = slice(i * 128, (i + 1) * 128)
                self.own[b, yy, i, low : low + rows] = grad[yy * CR : (yy + 1) * CR, cols]
                self.nbr[slot, yy, i, 0:rows] = grad[(2 + yy) * CR : (3 + yy) * CR, cols]

    def put_tall(self, k, grad):
        slot = self.seat(k)
        for yy in range(2):
            for i in range(6):
                rows = slice(i % 3 * 128, (i % 3 + 1) * 128)
                cols = slice(i * 128, (i + 1) * 128)
                self.own[k, yy, i // 3, rows] = grad[yy * 128 : (yy + 1) * 128, cols]
                self.nbr[slot, yy, i // 3, rows] = grad[(2 + yy) * 128 : (3 + yy) * 128, cols]

    def add(self, to, more):
        to[...] = to[...] + more[...]

    def stage_1(self, k):
        self.c_core(k).wait_recv()
        both = (slice(None), slice(None))
        self.add(self.side(self.own, k, *both), self.side(self.rc, k, *both))
        self.split(
            k,
            lambda k: self.a_y(k).start(),
            lambda k: self.b_x(k).start(),
            lambda k: self.q_pair(k).start(),
        )

    def stage_2(self, k):
        self.a_y(k).wait_recv()
        came = self.side(self.ry, k, slice(None))

        def a(k):
            self.add(self.side(self.own, k, self.p.y, slice(None)), came)
            self.a_x(k).start()

        def b(k):
            self.add(self.side(self.own, k, slice(None), self.p.x), came)
            self.b_y(k).start()

        def c(k):
            self.add(self.side(self.own, k, slice(None), self.p.h), came)
            self.q_y(k).start()

        self.split(k, a, b, c)

    def stage_3(self, k):
        self.a_x(k).wait_recv()
        came = self.side(self.rx, k)

        def line(k):
            self.add(self.half(k), came)
            pl.when(self.p.outer)(lambda: self.l_in(k).start())

        def c(k):
            self.add(self.side(self.own, k, self.p.y, self.p.h), came)
            self.q_x(k).start()

        self.split(k, line, line, c)

    def stage_4(self, k):
        def line(k):
            @pl.when(self.p.inner)
            def _():
                self.l_in(k).wait_recv()
                self.add(self.half(k), self.side(self.r1, k))
                self.l_mid(k).start()

        def c(k):
            self.q_x(k).wait_recv()
            self.add(self.q_own(k, False), self.q_in(k, 0))
            self.q_far(k).start()

        self.split(k, line, line, c)

    def stage_5(self, k):
        def line(k):
            @pl.when(self.p.inner)
            def _():
                self.l_mid(k).wait_recv()
                self.add(self.side(self.r2, k), self.half(k))
                self.l_out(k).start()
                self.l_leave(k, True)

        def c(k):
            self.q_far(k).wait_recv()
            total = self.q_own(k, False)[...] + self.q_in(k, 1)[...]
            self.r2[self.place(k)[0], self.part(k, False)] = total
            self.q_gather(k).start()

        self.split(k, line, line, c)

    def stage_6(self, k):
        def line(k):
            @pl.when(self.p.outer)
            def _():
                self.l_in(k).wait_recv()
                self.l_leave(k, False)

        def c(k):
            self.q_gather(k).wait_recv()
            self.q_leave(k)

        self.split(k, line, line, c)

    def close(self):
        rest = WAYS[:LAST_BIG].count("c") + WAYS[LAST_BIG:].count("c") // 2
        line = BUFFERS - rest
        peer = self.p.to_x

        def whole(ref, count, kind):
            span = ref.at[pl.ds(0, count)]
            return remote(span, span, self.send.at[kind], self.send.at[kind], peer)

        def parts(kind):
            span = self.r1.at[pl.ds(0, rest), pl.ds(0, CR)]
            return remote(span, span, self.send.at[kind], self.send.at[kind], peer)

        for k in range(K - SLOT_COUNT, K):
            self.c_core(k).wait_send()
        whole(self.ry, BUFFERS, 0).wait_send()
        whole(self.rx, BUFFERS, 1).wait_send()
        whole(self.r1, line, 2).wait_send()
        pl.when(self.p.inner)(lambda: whole(self.r1, line, 3).wait_send())
        whole(self.r1, line, 4).wait_send()
        whole(self.r1, line, 5).wait_recv()
        parts(6).wait_send()
        parts(7).wait_send()
        parts(8).wait_send()
        whole(self.r1, rest, 9).wait_send()
        whole(self.r1, rest, 10).wait_recv()
        pltpu.make_async_copy(self.r1, self.r2, self.send.at[11]).wait()

    def run(self, steps):
        stages = (self.stage_1, self.stage_2, self.stage_3, self.stage_4, self.stage_5, self.stage_6)
        for step in steps:
            stages[step // 100 - 1](step % 100)

    def run_at(self, index, table):
        for i, steps in enumerate(table):
            if steps:
                pl.when(index == i)(lambda steps=steps: self.run(steps))


def norm_parts(values):
    mean = jnp.mean(values, axis=-1, keepdims=True)
    centred = values - mean
    spread = jnp.mean(centred * centred, axis=-1, keepdims=True)
    scale = lax.rsqrt(spread + epsilon)
    return centred * scale, scale


def norm_back(hat, scale, gain, grad):
    lifted = grad * gain
    level = jnp.mean(lifted, axis=-1, keepdims=True)
    slope = jnp.mean(lifted * hat, axis=-1, keepdims=True)
    return scale * (lifted - level - hat * slope)


def three_parts(values):
    high = values.astype(BF).astype(F32)
    rest = values - high
    middle = rest.astype(BF).astype(F32)
    return high, middle, rest - middle


def layer_kernel(
    tok_ref, cot_ref, cnt_ref, fg_ref, fb_ref, ib_ref, ob_ref, sg_ref, sb_ref, eb_ref, rb_ref,
    wi_ref, wo_ref, we_ref, wr_ref,
    tot_ref, vs, lo_ref, gto_ref, gtr_ref,
    own, nbr, rc, ry, rx, r1, r2, vec,
    tokx, dyx, w1, wo, wr, qkv, kvr, rowb, kaug, qaug, att, mid, low2, turned, g_t, du_t, y_sum, h_sum,
    d_out, dp, dq_sum, dkv_own, dkv_far, dkv_send, dkv_recv, lo, gts, vr,
    csend, send, recv, lsem, xsend, xrecv, ksend, krecv, vsend, vrecv,
):
    p = Place()
    loads = [
        pltpu.make_async_copy(tok_ref.at[p.y, 0], tokx.at[pl.ds(0, PART)], lsem.at[0]),
        pltpu.make_async_copy(wi_ref, w1.at[:, pl.ds(0, 2304)], lsem.at[1]),
        pltpu.make_async_copy(cot_ref.at[p.y, 0], dyx.at[pl.ds(0, PART)], lsem.at[2]),
        pltpu.make_async_copy(wo_ref, wo, lsem.at[3]),
        pltpu.make_async_copy(wr_ref, wr, lsem.at[4]),
    ]
    for one in loads:
        one.start()
    enter(p)
    red = Reduce(p, (own, nbr, rc, ry, rx, r1, r2), tot_ref, csend, send, recv)

    def swap(index, src, dst, peer):
        return remote(src, dst, xsend.at[index], xrecv.at[index], peer)

    c_tok = [
        swap(8 * i, tok_ref.at[1 - p.y, 0, pl.ds(i * 128, 128)], tokx.at[pl.ds(PART + i * 128, 128)], p.to_y)
        for i in range(2)
    ]
    c_cot = swap(1, cot_ref.at[1 - p.y, 0], dyx.at[pl.ds(PART, PART)], p.to_y)
    c_row = swap(2, rowb.at[2], rowb.at[1], p.to_y)
    c_aug = swap(3, kaug.at[pl.ds(0, ROWS)], kaug.at[pl.ds(ROWS, ROWS)], p.to_core)
    pieces = ((0, PART), (PART, 128), (PART + 128, 128))
    c_kv = [
        swap(index, qkv.at[pl.ds(first, rows), pl.ds(768, 1536)], kvr.at[pl.ds(first, rows)], p.to_core)
        for index, (first, rows) in zip((4, 5, 9), pieces)
    ]

    lane = lax.broadcasted_iota(jnp.int32, (16, PART), 1)

    def bias_row(m):
        frame = lane // SLOTS
        kept = jnp.zeros_like(lane)
        for j in range(FRAME_DEV):
            kept = jnp.where(frame == j, cnt_ref[m, 0, j], kept)
        return jnp.where(lane - frame * SLOTS < kept, 0.0, LOW).astype(BF)

    rowb[2] = bias_row(1 - p.y)
    c_row.start()
    for one in c_tok:
        one.start()
    rowb[0] = bias_row(p.y)
    for row, ref in ((0, fg_ref), (1, fb_ref), (4, ob_ref), (5, sg_ref), (6, sb_ref), (7, rb_ref)):
        vec[row : row + 1] = ref[...].astype(F32).reshape(1, D)
    vec[2:4] = ib_ref[...].astype(F32)
    for f in range(4):
        vec[8 + f : 9 + f] = eb_ref[f * D : (f + 1) * D].astype(F32).reshape(1, D)
    pick = jnp.where(
        jnp.logical_and(
            lax.broadcasted_iota(jnp.int32, (16, 128), 0) == 0,
            lax.broadcasted_iota(jnp.int32, (16, 128), 1) == 0,
        ),
        1.0,
        0.0,
    ).astype(BF)
    kaug[pl.ds(0, PART)] = dot_tn(rowb[0], pick).astype(BF)
    lane_q = lax.broadcasted_iota(jnp.int32, (PART, 128), 1)
    lane_row = lax.broadcasted_iota(jnp.int32, (1, 128), 1)
    head_mask = [
        jnp.where((lane_row < 64) == (h == 0), 1.0, 0.0).astype(BF) for h in range(2)
    ]
    qaug[...] = jnp.where(lax.broadcasted_iota(jnp.int32, (ROWS, 128), 1) == 0, 1.0, 0.0)
    vs[...] = jnp.zeros_like(vs)

    def project(r):
        rows = pl.ds(*pieces[r])
        hat, _ = norm_parts(tokx[rows].astype(F32))
        low2[rows] = (hat * vec[0:1] + vec[1:2]).astype(BF)

        def column(j):
            col = pl.multiple_of(j * 256, 256)
            part = lax.rem(j, 3) * 256
            shift = jnp.where(
                j < 3, vec[2:3, at256(part)], jnp.where(j >= 6, vec[3:4, at256(part)], 0.0)
            )
            value = dot_nn(low2[rows], w1[:, pl.ds(col, 256)]) + shift
            qkv[rows, pl.ds(col, 256)] = (value * jnp.where(j < 3, 0.125, 1.0)).astype(BF)

        loop(3, 9, column)
        c_kv[r].start()
        loop(0, 3, column)

    loads[0].wait()
    loads[1].wait()
    project(0)
    c_row.wait_recv()
    kaug[pl.ds(PART, PART)] = dot_tn(rowb[1], pick).astype(BF)
    c_aug.start()
    c_tok[0].wait_recv()
    project(1)
    c_tok[1].wait_recv()
    c_cot.start()
    project(2)
    load_we = pltpu.make_async_copy(we_ref, w1, lsem.at[5])
    load_we.start()
    c_aug.wait_recv()
    for one in c_kv:
        one.wait_recv()

    def attend(pair):
        col = pl.multiple_of(pair * 128, 128)
        ones = jnp.ones((ROWS, 128), BF)
        first = jnp.where(lane_q == 0, 1.0, 0.0).astype(BF)
        k_here = jnp.concatenate([qkv[:, at128(768 + col)], kaug[pl.ds(0, ROWS)]], axis=1)
        k_there = jnp.concatenate([kvr[:, at128(col)], kaug[pl.ds(ROWS, ROWS)]], axis=1)
        v_here = jnp.concatenate([qkv[:, at128(1536 + col)], ones], axis=1)
        v_there = jnp.concatenate([kvr[:, at128(768 + col)], ones], axis=1)
        def scores(unit):
            block, h = unit // 2, unit % 2
            query = qkv[pl.ds(block * PART, PART), at128(col)]
            lifted = jnp.concatenate([query * head_mask[h], first], axis=1)
            return dot_nt(lifted, k_here), dot_nt(lifted, k_there)

        ready = scores(0)
        for unit in range(4):
            block, h = unit // 2, unit % 2
            rows = pl.ds(block * PART, PART)
            s_here, s_there = ready
            if unit < 3:
                ready = scores(unit + 1)
            top = jnp.maximum(
                jnp.max(s_here, axis=-1, keepdims=True), jnp.max(s_there, axis=-1, keepdims=True)
            )
            e_here = jnp.exp(s_here - top).astype(BF)
            e_there = jnp.exp(s_there - top).astype(BF)
            both = dot_nn(e_here, v_here) + dot_nn(e_there, v_there)
            total = both[:, 128:]
            out = both[:, :128] / total
            parts = three_parts(top + jnp.log(total))
            base = 1 + 3 * (2 * pair + h)
            extra = qaug[rows] if h == 0 else extra
            for i in range(3):
                extra = jnp.where(lane_q == base + i, -parts[i], extra)
            if h == 0:
                held = out
            else:
                qaug[rows] = extra
                att[rows, at128(col)] = jnp.where(lane_q < 64, held, out).astype(BF)

    loop(0, 6, attend)

    def turn(rows, block):
        flipped = block.T
        for quarter in range(4):
            seat = pl.multiple_of(p.seat(quarter) * CR, CR)
            turned[pl.ds(seat, CR), rows] = flipped[quarter * CR : (quarter + 1) * CR]

    loads[3].wait()

    def middle(i):
        rows = at256(i * PART)
        value = tokx[rows].astype(F32) + dot_nn(att[rows], wo[...]) + vec[4:5]
        mid[rows] = value
        hat, _ = norm_parts(value)
        block = (hat * vec[5:6] + vec[6:7]).astype(BF)
        low2[rows] = block
        turn(rows, block)

    loop(0, 2, middle)
    loads[2].wait()
    loads[4].wait()
    load_we.wait()
    c_cot.wait_recv()
    y_sum[...] = jnp.zeros_like(y_sum)
    h_sum[...] = jnp.zeros_like(h_sum)

    def feed(t):
        starts = []
        for side in range(2):
            cc = p.core if side == 0 else 1 - p.core
            for yy in range(2):
                starts.append((yy * 2 + cc) * 768 + t * 128)
        w_up = jnp.concatenate([w1[:, at128(s)] for s in starts], axis=1)
        shifts = vec[8:12, at128(t * 128)]
        zeroth = p.core == 0
        shift = jnp.concatenate(
            [
                jnp.where(zeroth, shifts[yy * 2 + s : yy * 2 + s + 1], shifts[yy * 2 + 1 - s : yy * 2 + 2 - s])
                for s in range(2)
                for yy in range(2)
            ],
            axis=1,
        )
        before = dot_nn(low2[...], w_up) + shift
        half = 0.5 + 0.5 * lax.erf(before * 0.7071067811865476)
        active = (before * half).astype(BF)
        slope = half + before * (jnp.exp(before * before * -0.5) * 0.3989422804014327)
        g_t[...] = active
        w_down = jnp.concatenate([wr[at128(s), :] for s in starts], axis=0)
        du_t[...] = (dot_nt(dyx[...], w_down) * slope).astype(BF)
        tall = dot_nn(g_t[...].T, dyx[...]).astype(BF)
        red.slot(2 * t)
        red.put_tall(2 * t, tall)
        red.c_core(2 * t).start()
        red.slot(2 * t + 1)
        for e in range(2):
            seats = [e + 2 * (p.core if cc == 0 else 1 - p.core) for cc in range(2)]
            right = jnp.concatenate([du_t[:, at128(s * 128)] for s in seats], axis=1)
            red.put_wide(2 * t + 1, e, dot_nn(turned[...], right).astype(BF))
        red.c_core(2 * t + 1).start()
        sums = jnp.sum(du_t[...].astype(F32), axis=0, keepdims=True)
        seat = [sums[:, i * 128 : (i + 1) * 128] for i in range(4)]
        vs[8:12, at128(t * 128)] = jnp.concatenate(
            [
                jnp.where(zeroth, seat[yy + 2 * cc], seat[yy + 2 - 2 * cc])
                for yy in range(2)
                for cc in range(2)
            ],
            axis=0,
        )
        red.run_at(t, FEED_STEPS[0])
        y_sum[...] += dot_nn(g_t[...], w_down)
        h_sum[...] += dot_nt(du_t[...], w_up)
        red.run_at(t, FEED_STEPS[1])

    loop(0, 6, feed)
    reload_wi = pltpu.make_async_copy(wi_ref, w1.at[:, pl.ds(0, 2304)], lsem.at[6])
    reload_wi.start()

    def second(i):
        rows = at256(i * PART)
        value = mid[rows]
        lo[rows] = (value + y_sum[rows] + vec[7:8]).astype(BF)
        hat, scale = norm_parts(value)
        grad = h_sum[rows]
        upstream = dyx[rows].astype(F32)
        vs[5:6] += jnp.sum(grad * hat, axis=0, keepdims=True)
        vs[6:7] += jnp.sum(grad, axis=0, keepdims=True)
        vs[7:8] += jnp.sum(upstream, axis=0, keepdims=True)
        total = upstream + norm_back(hat, scale, vec[5:6], grad)
        mid[rows] = total
        block = total.astype(BF)
        low2[rows] = block
        vs[4:5] += jnp.sum(block.astype(F32), axis=0, keepdims=True)
        d_out[rows] = dot_nt(block, wo[...]).astype(BF)
        turn(rows, att[rows])
        red.run_at(i, NORM_STEPS)

    loop(0, 2, second)
    c_lo = swap(6, lo.at[pl.ds(PART, PART)], lo_ref.at[p.y], p.to_y)
    keep_lo = pltpu.make_async_copy(lo.at[pl.ds(0, PART)], lo_ref.at[p.y], lsem.at[7])
    keep_lo.start()

    red.slot(12)
    red.slot(13)
    for k, side, first in ((12, 0, 0), (12, 1, 256), (13, 0, 512)):
        red.put_wide(k, side, dot_nn(turned[...], low2[:, first : first + 256]).astype(BF))
    red.c_core(12).start()
    red.run(OUT_STEPS)

    def turn_first(i):
        rows = at256(i * PART)
        hat, _ = norm_parts(tokx[rows].astype(F32))
        turn(rows, (hat * vec[0:1] + vec[1:2]).astype(BF))

    loop(0, 2, turn_first)

    def in_grad(first):
        return dot_nn(turned[...], dp[:, at256(first)]).astype(BF)

    def put_side(at):
        k, side = 13 + at // 2, lax.rem(at, 2)
        pl.when(side == 0)(lambda: red.slot(k))
        red.put_wide(k, side, in_grad(lax.rem(at - 1, 3) * 768 + (at - 1) // 3 * 256))
        pl.when(side == 1)(lambda: red.c_core(k).start())

    def put_last(k):
        red.slot(k)
        red.put_small(k, in_grad((k + 1) % 3 * 768 + (k - 11) // 3 * 256))
        red.c_core(k).start()

    def in_grads(pair):
        pl.when(pair == 2)(lambda: loop(1, 4, put_side))

        @pl.when(pair == 4)
        def _():
            loop(4, 6, put_side)
            put_last(16)

    def c_dkv(pair):
        return remote(
            dkv_send.at[lax.rem(pair, 2)], dkv_recv.at[pair], ksend.at[pair], krecv.at[pair], p.to_core
        )

    def settle(pair):
        c_dkv(pair).wait_recv()
        slot = lax.rem(pair, 2)
        for i in range(2):
            total = dkv_own[slot, i] + dkv_recv[pair, i].astype(F32)
            dp[:, at128(768 * (i + 1) + pair * 128)] = total.astype(BF)

    lane_k = lax.broadcasted_iota(jnp.int32, (ROWS, 128), 1)

    def attend_back(pair):
        col = pl.multiple_of(pair * 128, 128)
        slot = lax.rem(pair, 2)
        query = qkv[:, at128(col)]
        extra_q = qaug[...].astype(BF)
        grads = d_out[:, at128(col)]
        outs = att[:, at128(col)].astype(F32)
        three = jnp.where(lane_k < 3, 1.0, 0.0).astype(BF)

        @pl.when(pair >= 1)
        def _():
            settle(pair - 1)

        def products(unit):
            h, side = unit // 2, unit % 2
            q_h = query * head_mask[h]
            g_h = grads * head_mask[h]
            parts = three_parts(jnp.sum(g_h.astype(F32) * outs, axis=-1, keepdims=True))
            extra_g = jnp.zeros((ROWS, 128), F32)
            for i in range(3):
                extra_g = jnp.where(lane_k == i, -parts[i], extra_g)
            q_wide = jnp.concatenate([q_h, extra_q], axis=1)
            g_wide = jnp.concatenate([g_h, extra_g.astype(BF)], axis=1)
            base = 1 + 3 * (2 * pair + h)
            mark = jnp.where(
                jnp.logical_and(lane_k >= base, lane_k < base + 3), 1.0, 0.0
            ).astype(BF)
            if side == 0:
                key, value = qkv[:, at128(768 + col)], qkv[:, at128(1536 + col)]
            else:
                key, value = kvr[:, at128(col)], kvr[:, at128(768 + col)]
            k_wide = jnp.concatenate([key, kaug[pl.ds(side * ROWS, ROWS)] + mark], axis=1)
            v_wide = jnp.concatenate([value, three], axis=1)
            return dot_nt(k_wide, q_wide), dot_nt(v_wide, g_wide), q_h, g_h, (key * head_mask[h]).T

        ready = products(0)
        for unit in range(4):
            h, side = unit // 2, unit % 2
            score, slope, q_h, g_h, key_t = ready
            if unit < 3 and unit not in CUTS:
                ready = products(unit + 1)
            weight = jnp.exp(score)
            slope = (weight * slope).astype(BF)
            add_k, add_v = dot_nn(slope, q_h), dot_nn(weight.astype(BF), g_h)
            add_q = dot_nn(key_t, slope)
            if unit == 0:
                dq_sum[...] = add_q
            else:
                dq_sum[...] += add_q
            sums = dkv_own.at[slot] if side == 0 else dkv_far
            if h == 0:
                sums[0] = add_k
                sums[1] = add_v
            else:
                sums[0] += add_k
                sums[1] += add_v
            if unit in CUTS:
                red.run_at(pair, ATTEND_STEPS[CUTS.index(unit)])
                if unit < 3:
                    ready = products(unit + 1)
        dp[:, at128(col)] = (dq_sum[...].T.astype(BF).astype(F32) * 0.125).astype(BF)

        @pl.when(pair >= 2)
        def _():
            c_dkv(pair - 2).wait_send()

        dkv_send[slot] = dkv_far[...].astype(BF)
        c_dkv(pair).start()
        in_grads(pair)
        pl.when(pair == 1)(lambda: c_lo.start())

    loop(0, 6, attend_back)
    settle(5)
    c_dkv(4).wait_send()
    c_dkv(5).wait_send()

    for k in range(17, 20):
        put_last(k)
    red.run(PROJECT_STEPS)
    vs[2:3] = jnp.sum(dp[:, 0:768].astype(F32), axis=0, keepdims=True)
    vs[3:4] = jnp.sum(dp[:, 1536:2304].astype(F32), axis=0, keepdims=True)
    reload_wi.wait()

    def first_back(i):
        rows = at256(i * PART)
        grad = dot_nt(dp[rows], w1[:, pl.ds(0, 2304)])
        hat, scale = norm_parts(tokx[rows].astype(F32))
        vs[0:1] += jnp.sum(grad * hat, axis=0, keepdims=True)
        vs[1:2] += jnp.sum(grad, axis=0, keepdims=True)
        y_sum[rows] = mid[rows] + norm_back(hat, scale, vec[0:1], grad)
        red.run_at(i, LAST_STEPS)

    loop(0, 2, first_back)
    gts[...] = y_sum[pl.ds(PART, PART)].astype(BF)
    c_gt = swap(7, gts, gtr_ref, p.to_y)
    keep_gt = pltpu.make_async_copy(y_sum.at[pl.ds(0, PART)], gto_ref, lsem.at[8])
    c_gt.start()
    keep_gt.start()

    def c_vec(stage, peer):
        return remote(vr.at[2 * stage], vr.at[2 * stage + 1], vsend.at[stage], vrecv.at[stage], peer)

    def vec_pair(stage, peer):
        vr[2 * stage] = vs[...]
        c_vec(stage, peer).start()

    def vec_take(stage, peer):
        c_vec(stage, peer).wait()
        vs[...] += vr[2 * stage + 1]

    def vec_0():
        vec_take(0, p.to_core)
        vec_pair(1, p.to_y)

    def vec_1():
        vec_take(1, p.to_y)
        vec_pair(2, p.to_x)

    def vec_2():
        vec_take(2, p.to_x)

        @pl.when(p.outer)
        def _():
            vec_pair(3, p.to_mate)

    def vec_3():
        @pl.when(p.inner)
        def _():
            c_vec(3, p.to_mate).wait_recv()
            vs[...] += vr[7]
            vec_pair(4, p.to_far)

    def vec_4():
        @pl.when(p.inner)
        def _():
            vec_take(4, p.to_far)
            vec_pair(3, p.to_mate)

    def vec_5():
        @pl.when(p.outer)
        def _():
            c_vec(3, p.to_mate).wait_recv()
            vs[...] = vr[7]

        c_vec(3, p.to_mate).wait_send()

    vec_pair(0, p.to_core)
    vec_steps = (vec_0, vec_1, vec_2, vec_3, vec_4, vec_5)
    for step in DRAIN_STEPS:
        if step < 100:
            vec_steps[step]()
        else:
            red.run((step,))
    red.close()
    for one in c_tok + c_kv:
        one.wait_send()
    c_row.wait_send()
    c_cot.wait_send()
    c_aug.wait_send()
    c_lo.wait()
    c_gt.wait()
    keep_lo.wait()
    keep_gt.wait()


def finish_kernel(
    tot_ref, vs, lo_in, gto, gtr_ref,
    lo_out, gt, g0, g1, wi_out, g2, wo_out, g4, g5, g6, we_out, g8, wr_out, g7,
    tot, gtr, gt_s, lo_s, wi, wo, we, wr, in_sem, out_sem,
):
    y = lax.axis_index("frame") // 2
    frame = lax.axis_index("frame")
    spans = [(2 * t, 2) for t in range(6)] + [(12, 2), (14, 2), (16, 2)]
    loads = [
        pltpu.make_async_copy(tot_ref.at[pl.ds(k, n)], tot.at[pl.ds(k, n)], in_sem.at[i])
        for i, (k, n) in enumerate(spans)
    ]
    loads += [
        pltpu.make_async_copy(gtr_ref, gtr, in_sem.at[9]),
        pltpu.make_async_copy(gto, gt_s.at[0], in_sem.at[10]),
        pltpu.make_async_copy(lo_in, lo_s, in_sem.at[11]),
    ]
    for one in loads:
        one.start()
    outs = []

    def leave(src, dst):
        one = pltpu.make_async_copy(src, dst, out_sem.at[len(outs)])
        one.start()
        outs.append(one)

    for t in range(6):
        loads[t].wait()
        rows = pl.ds(t * 128, 128)
        for i in range(6):
            block = slice(i % 3 * 128, (i % 3 + 1) * 128)
            wr[rows, i * 128 : (i + 1) * 128] = tot[2 * t, i // 3, block].astype(F32)
        leave(wr.at[rows], wr_out.at[rows])
        for j in range(4):
            cols = pl.ds(j * 768 + t * 128, 128)
            block = slice(j % 2 * CR, (j % 2 + 1) * CR)
            we[:, cols] = tot[2 * t + 1, j // 2, block].astype(F32)
    leave(we, we_out)
    for n, col in enumerate(COLUMNS):
        if n % 8 == 0:
            loads[6 + n // 8].wait()
        block = slice(n % 2 * CR, (n % 2 + 1) * CR)
        value = tot[12 + n // 4, n % 4 // 2, block].astype(F32)
        if n < 6:
            wo[:, col * 128 : (col + 1) * 128] = value
        else:
            wi[:, col * 128 : (col + 1) * 128] = value
        if n == 5:
            leave(wo, wo_out)
    leave(wi, wi_out)
    loads[9].wait()
    gt_s[1] = gtr[...].astype(F32)
    leave(gt_s.at[1], gt.at[1 - y, 0])
    loads[10].wait()
    leave(gt_s.at[0], gt.at[y, 0])
    loads[11].wait()
    leave(lo_s.at[0], lo_out.at[0, 0])
    leave(lo_s.at[1], lo_out.at[1, 0])
    mine = vs[0:8, 0:CR]
    row = vs[8:9]
    for f in range(1, 4):
        mine = jnp.where(frame == f, vs[0:8, f * CR : (f + 1) * CR], mine)
        row = jnp.where(frame == f, vs[8 + f : 9 + f], row)
    g0[...] = mine[0]
    g1[...] = mine[1]
    g2[...] = mine[2:4]
    g4[...] = mine[4]
    g5[...] = mine[5]
    g6[...] = mine[6]
    g7[...] = mine[7]
    g8[...] = row[0]
    for one in outs:
        one.wait()


def local_slice(
    tokens,
    counts,
    first_gain,
    first_bias,
    input_weight,
    input_bias,
    output_weight,
    output_bias,
    second_gain,
    second_bias,
    expand_weight,
    expand_bias,
    reduce_weight,
    reduce_bias,
    cotangent,
):
    anywhere = pl.BlockSpec(memory_space=pl.ANY)
    vmem = pl.BlockSpec(memory_space=pltpu.VMEM)
    smem = pl.BlockSpec(memory_space=pltpu.SMEM)
    shape = jax.ShapeDtypeStruct
    dma = pltpu.SemaphoreType.DMA
    tot, vs, lo, gto, gtr = pl.pallas_call(
        layer_kernel,
        out_shape=(
            shape((BUFFERS, 2, HR, 128), BF),
            shape((16, D), F32),
            shape((2, PART, D), BF),
            shape((PART, D), F32),
            shape((PART, D), BF),
        ),
        in_specs=[anywhere, anywhere, smem] + [vmem] * 8 + [anywhere] * 4,
        out_specs=(anywhere, vmem, anywhere, anywhere, anywhere),
        scratch_shapes=[
            pltpu.VMEM((BUFFERS, 2, 2, HR, 128), BF),
            pltpu.VMEM((SLOT_COUNT, 2, 2, HR, 128), BF),
            pltpu.VMEM((BUFFERS, 2, 2, HR, 128), BF),
            pltpu.VMEM((BUFFERS, 2, HR, 128), BF),
            pltpu.VMEM((BUFFERS, HR, 128), BF),
            pltpu.VMEM((BUFFERS, HR, 128), BF),
            pltpu.VMEM((BUFFERS, HR, 128), BF),
            pltpu.VMEM((12, D), F32),
            pltpu.VMEM((ROWS, D), BF),
            pltpu.VMEM((ROWS, D), BF),
            pltpu.VMEM((D, FF), BF),
            pltpu.VMEM((D, D), BF),
            pltpu.VMEM((FF, D), BF),
            pltpu.VMEM((ROWS, 3 * D), BF),
            pltpu.VMEM((ROWS, 2 * D), BF),
            pltpu.VMEM((3, 16, PART), BF),
            pltpu.VMEM((2 * ROWS, 128), BF),
            pltpu.VMEM((ROWS, 128), F32),
            pltpu.VMEM((ROWS, D), BF),
            pltpu.VMEM((ROWS, D), F32),
            pltpu.VMEM((ROWS, D), BF),
            pltpu.VMEM((D, ROWS), BF),
            pltpu.VMEM((ROWS, ROWS), BF),
            pltpu.VMEM((ROWS, ROWS), BF),
            pltpu.VMEM((ROWS, D), F32),
            pltpu.VMEM((ROWS, D), F32),
            pltpu.VMEM((ROWS, D), BF),
            pltpu.VMEM((ROWS, 3 * D), BF),
            pltpu.VMEM((128, ROWS), F32),
            pltpu.VMEM((2, 2, ROWS, 128), F32),
            pltpu.VMEM((2, ROWS, 128), F32),
            pltpu.VMEM((2, 2, ROWS, 128), BF),
            pltpu.VMEM((6, 2, ROWS, 128), BF),
            pltpu.VMEM((ROWS, D), BF),
            pltpu.VMEM((PART, D), BF),
            pltpu.VMEM((10, 16, D), F32),
            dma((SLOT_COUNT,)),
            dma((12,)),
            dma((6, K)),
            dma((9,)),
            dma((10,)),
            dma((10,)),
            dma((6,)),
            dma((6,)),
            dma((5,)),
            dma((5,)),
        ],
        compiler_params=pltpu.CompilerParams(
            collective_id=0, has_side_effects=True, vmem_limit_bytes=62 << 20
        ),
    )(
        tokens,
        cotangent,
        counts,
        first_gain,
        first_bias,
        input_bias,
        output_bias,
        second_gain,
        second_bias,
        expand_bias,
        reduce_bias,
        input_weight,
        output_weight,
        expand_weight,
        reduce_weight,
    )
    return pl.pallas_call(
        finish_kernel,
        out_shape=(
            shape((MICRO, 1, PART, D), BF),
            shape((MICRO, 1, PART, D), F32),
            shape((CR,), F32),
            shape((CR,), F32),
            shape((CR, 3 * D), F32),
            shape((2, CR), F32),
            shape((CR, D), F32),
            shape((CR,), F32),
            shape((CR,), F32),
            shape((CR,), F32),
            shape((CR, FF), F32),
            shape((D,), F32),
            shape((D, D), F32),
            shape((CR,), F32),
        ),
        in_specs=[anywhere, vmem, anywhere, anywhere, anywhere],
        out_specs=tuple(anywhere if i in (0, 1, 4, 6, 10, 12) else vmem for i in range(14)),
        scratch_shapes=[
            pltpu.VMEM((BUFFERS, 2, HR, 128), BF),
            pltpu.VMEM((PART, D), BF),
            pltpu.VMEM((2, PART, D), F32),
            pltpu.VMEM((2, PART, D), BF),
            pltpu.VMEM((CR, 3 * D), F32),
            pltpu.VMEM((CR, D), F32),
            pltpu.VMEM((CR, FF), F32),
            pltpu.VMEM((D, D), F32),
            dma((12,)),
            dma((16,)),
        ],
        compiler_params=pltpu.CompilerParams(vmem_limit_bytes=62 << 20),
    )(tot, vs, lo, gto, gtr)


def solution(mesh):
    fits = mesh.shape["clip"] == 8 and mesh.shape["frame"] == 4
    return jax.shard_map(
        local_slice if fits else local,
        mesh=mesh,
        in_specs=(
            P(None, "clip", "frame", None),
            P(None, "clip", "frame"),
            P(),
            P(),
            P(),
            P(),
            P(),
            P(),
            P(),
            P(),
            P(),
            P(),
            P(),
            P(),
            P(None, "clip", "frame", None),
        ),
        out_specs=(
            P(None, "clip", "frame", None),
            P(None, "clip", "frame", None),
            P("frame"),
            P("frame"),
            P("frame", None),
            P(None, "frame"),
            P("frame", None),
            P("frame"),
            P("frame"),
            P("frame"),
            P("frame", None),
            P("frame"),
            P("frame", None),
            P("frame"),
        ),
        check_vma=False,
    )
```

```python
import jax
import jax.numpy as jnp
from jax import lax
from jax.experimental import pallas as pl
from jax.experimental.pallas import tpu as pltpu
from jax.sharding import PartitionSpec as P

D = 768
H = 12
HD = 64
MICRO = 2
FRAME_DEV = 4
SLOTS = 64
BLOCK = 256


epsilon = 1e-06


def from_behind(block, axis, distance):
    devices = range(lax.axis_size(axis))
    route = [((i - distance) % len(devices), i) for i in devices]
    return lax.ppermute(block, axis, route)


def norm_rows(values, gain, shift):
    mean = jnp.mean(values, axis=-1, keepdims=True)
    centred = values - mean
    spread = jnp.mean(centred * centred, axis=-1, keepdims=True)
    return centred * lax.rsqrt(spread + epsilon) * gain + shift


def gelu_exact(values):
    return jax.nn.gelu(values, approximate=False)


def key_valid(every_count, source):
    frame_counts = lax.dynamic_slice_in_dim(every_count, source * FRAME_DEV, FRAME_DEV, 1)
    slot_index = jnp.arange(SLOTS, dtype=jnp.int32)
    return (slot_index[None, None, :] < frame_counts[:, :, None]).reshape(MICRO, BLOCK)


def scores_of(query, keys, valid):
    key_heads = keys.reshape(MICRO, BLOCK, H, HD)
    scores = jnp.einsum("mqhd,mkhd->mhqk", query, key_heads, preferred_element_type=jnp.float32)
    return jnp.where(valid[:, None, None, :], scores, -1e30)


def absorb(state, query, keys, values, valid):
    top, total, summed = state
    scores = scores_of(query, keys, valid)
    new_top = jnp.maximum(top, jnp.max(scores, axis=-1, keepdims=True))
    factor = jnp.exp(top - new_top)
    lifted = jnp.exp(scores - new_top)
    total = total * factor + jnp.sum(lifted, axis=-1, keepdims=True)
    value_heads = values.reshape(MICRO, BLOCK, H, HD)
    summed = summed * factor + jnp.einsum(
        "mhqk,mkhd->mhqd",
        lifted.astype(jnp.bfloat16),
        value_heads,
        preferred_element_type=jnp.float32,
    )
    return (new_top, total, summed)


def block_back(query, keys, values, valid, log_total, delta, grad_heads):
    scores = scores_of(query, keys, valid)
    weights = jnp.exp(scores - log_total)
    key_heads = keys.reshape(MICRO, BLOCK, H, HD)
    value_heads = values.reshape(MICRO, BLOCK, H, HD)
    grad_weights = jnp.einsum(
        "mqhd,mkhd->mhqk", grad_heads, value_heads, preferred_element_type=jnp.float32
    )
    grad_scores = (weights * (grad_weights - delta)).astype(jnp.bfloat16)
    grad_query = jnp.einsum(
        "mhqk,mkhd->mqhd", grad_scores, key_heads, preferred_element_type=jnp.float32
    )
    grad_keys = jnp.einsum(
        "mhqk,mqhd->mkhd", grad_scores, query, preferred_element_type=jnp.float32
    )
    grad_values = jnp.einsum(
        "mhqk,mqhd->mkhd",
        weights.astype(jnp.bfloat16),
        grad_heads,
        preferred_element_type=jnp.float32,
    )
    return (grad_query, grad_keys.reshape(MICRO, BLOCK, D), grad_values.reshape(MICRO, BLOCK, D))


def local(
    tokens,
    counts,
    first_gain,
    first_bias,
    input_weight,
    input_bias,
    output_weight,
    output_bias,
    second_gain,
    second_bias,
    expand_weight,
    expand_bias,
    reduce_weight,
    reduce_bias,
    cotangent,
):
    members = lax.axis_size("frame")
    myself = lax.axis_index("frame")
    total_rows = MICRO * BLOCK
    seq_in = tokens.reshape(total_rows, D).astype(jnp.float32)
    every_count = lax.all_gather(counts.reshape(MICRO, FRAME_DEV), "frame", axis=1, tiled=True)
    gain_one = first_gain.astype(jnp.float32)
    shift_one = first_bias.astype(jnp.float32)
    gain_two = second_gain.astype(jnp.float32)
    shift_two = second_bias.astype(jnp.float32)
    qv_bias = input_bias.astype(jnp.float32)
    first_low = norm_rows(seq_in, gain_one, shift_one).astype(jnp.bfloat16)
    projected = jnp.dot(first_low, input_weight, preferred_element_type=jnp.float32)
    query = (
        ((projected[:, :D] + qv_bias[0]) * 0.125).astype(jnp.bfloat16).reshape(MICRO, BLOCK, H, HD)
    )
    keys = projected[:, D : 2 * D].astype(jnp.bfloat16).reshape(MICRO, BLOCK, D)
    values = (projected[:, 2 * D :] + qv_bias[1]).astype(jnp.bfloat16).reshape(MICRO, BLOCK, D)
    start = (
        jnp.full((MICRO, H, BLOCK, 1), -1e30, jnp.float32),
        jnp.zeros((MICRO, H, BLOCK, 1), jnp.float32),
        jnp.zeros((MICRO, H, BLOCK, HD), jnp.float32),
    )
    state = absorb(start, query, keys, values, key_valid(every_count, myself))
    stored = ()

    def forward_hop(step, carry):
        state_now, moving, kept = carry
        moving = from_behind((moving[0], moving[1]), "frame", 1)
        source = (myself - step) % members
        state_now = absorb(state_now, query, moving[0], moving[1], key_valid(every_count, source))
        return (state_now, moving, kept)

    state, _, stored = lax.fori_loop(1, members, forward_hop, (state, (keys, values), stored))
    top, total, summed = state
    log_total = top + jnp.log(total)
    attend_full = jnp.transpose(summed / total, (0, 2, 1, 3))
    attend_low = attend_full.reshape(total_rows, D).astype(jnp.bfloat16)
    middle = (
        seq_in
        + jnp.dot(attend_low, output_weight, preferred_element_type=jnp.float32)
        + output_bias.astype(jnp.float32)
    )
    second_low = norm_rows(middle, gain_two, shift_two).astype(jnp.bfloat16)
    before = jnp.dot(
        second_low, expand_weight, preferred_element_type=jnp.float32
    ) + expand_bias.astype(jnp.float32)
    active_low = gelu_exact(before).astype(jnp.bfloat16)
    result = (
        middle
        + jnp.dot(active_low, reduce_weight, preferred_element_type=jnp.float32)
        + reduce_bias.astype(jnp.float32)
    )
    layer_out = result.astype(jnp.bfloat16).reshape(MICRO, 1, BLOCK, D)
    upstream_low = cotangent.reshape(total_rows, D)
    upstream = upstream_low.astype(jnp.float32)
    grad_reduce_weight = jnp.dot(active_low.T, upstream_low, preferred_element_type=jnp.float32)
    grad_reduce_bias = jnp.sum(upstream, axis=0)
    grad_active = jnp.dot(upstream_low, reduce_weight.T, preferred_element_type=jnp.float32)
    _, gelu_back = jax.vjp(gelu_exact, before)
    grad_before = gelu_back(grad_active)[0].astype(jnp.bfloat16)
    grad_expand_weight = jnp.dot(second_low.T, grad_before, preferred_element_type=jnp.float32)
    grad_expand_bias = jnp.sum(grad_before.astype(jnp.float32), axis=0)
    grad_second = jnp.dot(grad_before, expand_weight.T, preferred_element_type=jnp.float32)
    _, second_back = jax.vjp(norm_rows, middle, gain_two, shift_two)
    middle_part, grad_second_gain, grad_second_bias = second_back(grad_second)
    grad_middle = upstream + middle_part
    grad_branch = grad_middle.astype(jnp.bfloat16)
    grad_output_weight = jnp.dot(attend_low.T, grad_branch, preferred_element_type=jnp.float32)
    grad_output_bias = jnp.sum(grad_branch.astype(jnp.float32), axis=0)
    grad_attend = jnp.dot(grad_branch, output_weight.T, preferred_element_type=jnp.float32).astype(
        jnp.bfloat16
    )
    grad_heads = grad_attend.reshape(MICRO, BLOCK, H, HD)
    delta = jnp.transpose(
        jnp.sum(grad_heads.astype(jnp.float32) * attend_full, axis=-1), (0, 2, 1)
    )[..., None]
    first_terms = block_back(
        query, keys, values, key_valid(every_count, myself), log_total, delta, grad_heads
    )

    def backward_hop(step, carry):
        grad_query, running, moving = carry
        running = (
            from_behind(running[0].astype(jnp.bfloat16), "frame", 1).astype(jnp.float32),
            from_behind(running[1].astype(jnp.bfloat16), "frame", 1).astype(jnp.float32),
        )
        current = from_behind((moving[0], moving[1]), "frame", 1)
        source = (myself - step) % members
        add_query, add_keys, add_values = block_back(
            query,
            current[0],
            current[1],
            key_valid(every_count, source),
            log_total,
            delta,
            grad_heads,
        )
        return (grad_query + add_query, (running[0] + add_keys, running[1] + add_values), current)

    grad_query, running, _ = lax.fori_loop(
        1, members, backward_hop, (first_terms[0], (first_terms[1], first_terms[2]), (keys, values))
    )
    finished = (
        from_behind(running[0].astype(jnp.bfloat16), "frame", 1).astype(jnp.float32),
        from_behind(running[1].astype(jnp.bfloat16), "frame", 1).astype(jnp.float32),
    )
    query_low = grad_query.astype(jnp.bfloat16).reshape(total_rows, D) * 0.125
    keys_low = finished[0].astype(jnp.bfloat16).reshape(total_rows, D)
    values_low = finished[1].astype(jnp.bfloat16).reshape(total_rows, D)
    grad_projected = jnp.concatenate([query_low, keys_low, values_low], axis=1)
    grad_input_weight = jnp.dot(first_low.T, grad_projected, preferred_element_type=jnp.float32)
    grad_input_bias = jnp.stack(
        [
            jnp.sum(query_low.astype(jnp.float32), axis=0),
            jnp.sum(values_low.astype(jnp.float32), axis=0),
        ]
    )
    grad_first = jnp.dot(grad_projected, input_weight.T, preferred_element_type=jnp.float32)
    _, first_back = jax.vjp(norm_rows, seq_in, gain_one, shift_one)
    input_part, grad_first_gain, grad_first_bias = first_back(grad_first)
    grad_tokens = (grad_middle + input_part).reshape(MICRO, 1, BLOCK, D)
    shares = (
        lax.psum_scatter(
            grad_first_gain.astype(jnp.bfloat16), "frame", scatter_dimension=0, tiled=True
        ).astype(jnp.float32),
        lax.psum_scatter(
            grad_first_bias.astype(jnp.bfloat16), "frame", scatter_dimension=0, tiled=True
        ).astype(jnp.float32),
        lax.psum_scatter(
            grad_input_weight.astype(jnp.bfloat16), "frame", scatter_dimension=0, tiled=True
        ).astype(jnp.float32),
        lax.psum_scatter(
            grad_input_bias.astype(jnp.bfloat16), "frame", scatter_dimension=1, tiled=True
        ).astype(jnp.float32),
        lax.psum_scatter(
            grad_output_weight.astype(jnp.bfloat16), "frame", scatter_dimension=0, tiled=True
        ).astype(jnp.float32),
        lax.psum_scatter(
            grad_output_bias.astype(jnp.bfloat16), "frame", scatter_dimension=0, tiled=True
        ).astype(jnp.float32),
        lax.psum_scatter(
            grad_second_gain.astype(jnp.bfloat16), "frame", scatter_dimension=0, tiled=True
        ).astype(jnp.float32),
        lax.psum_scatter(
            grad_second_bias.astype(jnp.bfloat16), "frame", scatter_dimension=0, tiled=True
        ).astype(jnp.float32),
        lax.psum_scatter(
            grad_expand_weight.astype(jnp.bfloat16), "frame", scatter_dimension=0, tiled=True
        ).astype(jnp.float32),
        lax.psum_scatter(
            grad_expand_bias.astype(jnp.bfloat16), "frame", scatter_dimension=0, tiled=True
        ).astype(jnp.float32),
        lax.psum_scatter(
            grad_reduce_weight.astype(jnp.bfloat16), "frame", scatter_dimension=0, tiled=True
        ).astype(jnp.float32),
        lax.psum_scatter(
            grad_reduce_bias.astype(jnp.bfloat16), "frame", scatter_dimension=0, tiled=True
        ).astype(jnp.float32),
    )
    totals = (
        lax.psum(shares[0].astype(jnp.bfloat16), "clip").astype(jnp.float32),
        lax.psum(shares[1].astype(jnp.bfloat16), "clip").astype(jnp.float32),
        lax.psum(shares[2].astype(jnp.bfloat16), "clip").astype(jnp.float32),
        lax.psum(shares[3].astype(jnp.bfloat16), "clip").astype(jnp.float32),
        lax.psum(shares[4].astype(jnp.bfloat16), "clip").astype(jnp.float32),
        lax.psum(shares[5].astype(jnp.bfloat16), "clip").astype(jnp.float32),
        lax.psum(shares[6].astype(jnp.bfloat16), "clip").astype(jnp.float32),
        lax.psum(shares[7].astype(jnp.bfloat16), "clip").astype(jnp.float32),
        lax.psum(shares[8].astype(jnp.bfloat16), "clip").astype(jnp.float32),
        lax.psum(shares[9].astype(jnp.bfloat16), "clip").astype(jnp.float32),
        lax.psum(shares[10].astype(jnp.bfloat16), "clip").astype(jnp.float32),
        lax.psum(shares[11].astype(jnp.bfloat16), "clip").astype(jnp.float32),
    )
    return (
        layer_out,
        grad_tokens,
        totals[0],
        totals[1],
        totals[2],
        totals[3],
        totals[4],
        totals[5],
        totals[6],
        totals[7],
        totals[8],
        totals[9],
        totals[10],
        totals[11],
    )


MESH = pl.DeviceIdType.MESH
BF = jnp.bfloat16
F32 = jnp.float32
K = 20
BUFFERS = 18
QR = 768
HR = 384
CR = 192
SLOT_COUNT = 4
ROWS = 512
PART = 256
FF = 3072
LOW = -1e30
COLUMNS = (0, 1, 2, 3, 4, 5, 0, 1, 6, 7, 12, 13, 2, 3, 8, 9, 14, 4, 15, 5, 10, 16, 11, 17)
LAST_BIG = 16
WAYS = "acabcbbccbabcabaaaab"
CUTS = (0, 1, 2, 3)
FEED_STEPS = (((), (), (101, 102), (104,), (200, 106), (203, 202, 108, 109)), ((), (100,), (103,), (105,), (201, 107), (204,)))
NORM_STEPS = ((301, 205, 110), (111,))
OUT_STEPS = (303, 300, 207)
ATTEND_STEPS = (((304,), (302,), (401,), (405, 211, 309, 404, 603, 402), (504, 601), (311, 506, 214)), ((), (403,), (503, 306), (501, 310, 113, 600, 407, 114), (), (508, 604, 602, 115)), ((112, 305, 206), (210,), (212,), (406, 408, 505), (502, 410), (412, 116, 213, 607)), ((208,), (400, 307, 209), (308, 500), (409,), (312, 507, 605), (509, 411, 606, 314)))
PROJECT_STEPS = (510, 608, 512)
LAST_STEPS = ((215, 117, 511, 313, 118, 119, 216, 414, 609), (612, 610))
DRAIN_STEPS = (217, 315, 413, 514, 0, 218, 219, 611, 316, 1, 513, 415, 2, 416, 614, 3, 317, 515, 613, 318, 516, 4, 319, 417, 418, 615, 5, 616, 419, 517, 518, 519, 617, 618, 619)


def dot_nn(a, b):
    return lax.dot_general(a, b, (((1,), (0,)), ((), ())), preferred_element_type=F32)


def dot_nt(a, b):
    return lax.dot_general(a, b, (((1,), (1,)), ((), ())), preferred_element_type=F32)


def dot_tn(a, b):
    return lax.dot_general(a, b, (((0,), (0,)), ((), ())), preferred_element_type=F32)


def at128(index):
    return pl.ds(pl.multiple_of(index, 128), 128)


def at256(index):
    return pl.ds(pl.multiple_of(index, 256), 256)


def loop(low, high, body):
    def step(i, carry):
        body(i)
        return carry

    lax.fori_loop(low, high, step, 0)


class Place:
    def __init__(self):
        self.clip = lax.axis_index("clip")
        self.frame = lax.axis_index("frame")
        self.x = lax.rem(self.clip, 2)
        self.z = self.clip // 2
        self.core = lax.rem(self.frame, 2)
        self.y = self.frame // 2
        self.outer = jnp.logical_or(self.z == 0, self.z == 3)
        self.inner = jnp.logical_not(self.outer)
        self.to_core = (self.clip, self.y * 2 + (1 - self.core))
        self.to_y = (self.clip, (1 - self.y) * 2 + self.core)
        self.to_x = (self.z * 2 + (1 - self.x), self.frame)
        mate = self.z + 1 - 2 * lax.rem(self.z, 2)
        self.to_mate = (mate * 2 + self.x, self.frame)
        self.to_far = ((3 - self.z) * 2 + self.x, self.frame)
        self.h = jnp.where(self.inner, 1, 0)

    def seat(self, quarter):
        yy, cc = quarter // 2, quarter % 2
        return yy + 2 * (self.core if cc == 0 else 1 - self.core)


def enter(place):
    barrier = pltpu.get_barrier_semaphore()
    for peer in (place.to_core, place.to_y, place.to_x, place.to_mate, place.to_far):
        pl.semaphore_signal(barrier, inc=1, device_id=peer, device_id_type=MESH)
    pl.semaphore_wait(barrier, 5)


def remote(src, dst, send, recv, peer):
    return pltpu.make_async_remote_copy(
        src_ref=src, dst_ref=dst, send_sem=send, recv_sem=recv, device_id=peer, device_id_type=MESH
    )


class Reduce:
    def __init__(self, place, bufs, tot, csend, send, recv):
        self.p = place
        self.own, self.nbr, self.rc, self.ry, self.rx, self.r1, self.r2 = bufs
        self.tot, self.csend, self.send, self.recv = tot, csend, send, recv

    def copy(self, src, dst, kind, stage, k, peer):
        return remote(src, dst, self.send.at[kind], self.recv.at[stage, k], peer)

    def last(self, src, dst, kind, end, peer):
        return remote(src, dst, self.send.at[kind], self.send.at[end], peer)

    def place(self, k):
        if k < LAST_BIG:
            return k, 0, HR
        return LAST_BIG + (k - LAST_BIG) // 2, (k - LAST_BIG) % 2 * CR, CR

    def part(self, k, far):
        _, low, rows = self.place(k)
        side = 1 - self.p.x if far else self.p.x
        return pl.ds(pl.multiple_of(low + side * (rows // 2), 32), rows // 2)

    def c_core(self, k):
        slot = self.seat(k)
        src, dst = self.nbr.at[slot], self.rc.at[k] if not isinstance(k, int) or k < LAST_BIG else None
        if dst is None:
            b, low, rows = self.place(k)
            src, dst = self.nbr.at[slot, :, :, pl.ds(0, rows)], self.rc.at[b, :, :, pl.ds(low, rows)]
        return remote(src, dst, self.csend.at[slot], self.recv.at[0, k], self.p.to_core)

    def side(self, ref, k, *lead):
        b, low, rows = self.place(k)
        return ref.at[(b, *lead, pl.ds(low, rows))]

    def a_y(self, k):
        return self.copy(
            self.side(self.own, k, 1 - self.p.y, slice(None)), self.side(self.ry, k, slice(None)), 0, 1, k, self.p.to_y
        )

    def a_x(self, k):
        return self.copy(
            self.side(self.own, k, self.p.y, 1 - self.p.x), self.side(self.rx, k), 1, 2, k, self.p.to_x
        )

    def b_x(self, k):
        return self.copy(
            self.side(self.own, k, slice(None), 1 - self.p.x), self.side(self.ry, k, slice(None)), 0, 1, k, self.p.to_x
        )

    def b_y(self, k):
        return self.copy(
            self.side(self.own, k, 1 - self.p.y, self.p.x), self.side(self.rx, k), 1, 2, k, self.p.to_y
        )

    def half(self, k):
        return self.side(self.own, k, self.p.y, self.p.x)

    def l_in(self, k):
        return self.copy(self.half(k), self.side(self.r1, k), 2, 3, k, self.p.to_mate)

    def l_mid(self, k):
        return self.copy(self.half(k), self.side(self.r2, k), 3, 4, k, self.p.to_far)

    def l_out(self, k):
        return self.copy(self.side(self.r2, k), self.side(self.r1, k), 2, 3, k, self.p.to_mate)

    def l_leave(self, k, inner):
        src = self.side(self.r2 if inner else self.r1, k)
        dst = self.side(self.tot, k, self.p.x)
        self.last(src, dst, 4, 5, self.p.to_x).start()
        self.keep(src, dst).start()

    def q_pair(self, k):
        return self.copy(
            self.side(self.own, k, slice(None), 1 - self.p.h),
            self.side(self.ry, k, slice(None)),
            0,
            1,
            k,
            self.p.to_mate,
        )

    def q_y(self, k):
        return self.copy(
            self.side(self.own, k, 1 - self.p.y, self.p.h), self.side(self.rx, k), 1, 2, k, self.p.to_y
        )

    def q_own(self, k, far):
        return self.own.at[self.place(k)[0], self.p.y, self.p.h, self.part(k, far)]

    def q_in(self, k, second):
        b, low, rows = self.place(k)
        return self.r1.at[b, pl.ds(low + second * (rows // 2), rows // 2)]

    def q_x(self, k):
        return self.copy(self.q_own(k, True), self.q_in(k, 0), 6, 3, k, self.p.to_x)

    def q_far(self, k):
        return self.copy(self.q_own(k, False), self.q_in(k, 1), 7, 4, k, self.p.to_far)

    def q_gather(self, k):
        both = self.r2.at[self.place(k)[0], self.part(k, False)]
        return self.copy(both, both, 8, 5, k, self.p.to_x)

    def q_leave(self, k):
        src, dst = self.side(self.r2, k), self.side(self.tot, k, self.p.h)
        self.last(src, dst, 9, 10, self.p.to_mate).start()
        self.keep(src, dst).start()

    def keep(self, src, dst):
        return pltpu.make_async_copy(src, dst, self.send.at[11])

    def split(self, k, a, b, c):
        {"a": a, "b": b, "c": c}[WAYS[k]](k)

    def seat(self, k):
        return k % SLOT_COUNT if isinstance(k, int) else lax.rem(k, SLOT_COUNT)

    def slot(self, k):
        if isinstance(k, int):
            self.c_core(k - SLOT_COUNT).wait_send()
        else:
            pl.when(k >= SLOT_COUNT)(lambda: self.c_core(k - SLOT_COUNT).wait_send())

    def put_wide(self, k, side, grad):
        slot = self.seat(k)
        for yy in range(2):
            for i in range(2):
                rows = slice(i * CR, (i + 1) * CR)
                cols = slice(i * 128, (i + 1) * 128)
                self.own[k, yy, side, rows] = grad[yy * CR : (yy + 1) * CR, cols]
                self.nbr[slot, yy, side, rows] = grad[(2 + yy) * CR : (3 + yy) * CR, cols]

    def put_small(self, k, grad):
        slot = self.seat(k)
        b, low, rows = self.place(k)
        for yy in range(2):
            for i in range(2):
                cols = slice(i * 128, (i + 1) * 128)
                self.own[b, yy, i, low : low + rows] = grad[yy * CR : (yy + 1) * CR, cols]
                self.nbr[slot, yy, i, 0:rows] = grad[(2 + yy) * CR : (3 + yy) * CR, cols]

    def put_tall(self, k, grad):
        slot = self.seat(k)
        for yy in range(2):
            for i in range(6):
                rows = slice(i % 3 * 128, (i % 3 + 1) * 128)
                cols = slice(i * 128, (i + 1) * 128)
                self.own[k, yy, i // 3, rows] = grad[yy * 128 : (yy + 1) * 128, cols]
                self.nbr[slot, yy, i // 3, rows] = grad[(2 + yy) * 128 : (3 + yy) * 128, cols]

    def add(self, to, more):
        to[...] = to[...] + more[...]

    def stage_1(self, k):
        self.c_core(k).wait_recv()
        both = (slice(None), slice(None))
        self.add(self.side(self.own, k, *both), self.side(self.rc, k, *both))
        self.split(
            k,
            lambda k: self.a_y(k).start(),
            lambda k: self.b_x(k).start(),
            lambda k: self.q_pair(k).start(),
        )

    def stage_2(self, k):
        self.a_y(k).wait_recv()
        came = self.side(self.ry, k, slice(None))

        def a(k):
            self.add(self.side(self.own, k, self.p.y, slice(None)), came)
            self.a_x(k).start()

        def b(k):
            self.add(self.side(self.own, k, slice(None), self.p.x), came)
            self.b_y(k).start()

        def c(k):
            self.add(self.side(self.own, k, slice(None), self.p.h), came)
            self.q_y(k).start()

        self.split(k, a, b, c)

    def stage_3(self, k):
        self.a_x(k).wait_recv()
        came = self.side(self.rx, k)

        def line(k):
            self.add(self.half(k), came)
            pl.when(self.p.outer)(lambda: self.l_in(k).start())

        def c(k):
            self.add(self.side(self.own, k, self.p.y, self.p.h), came)
            self.q_x(k).start()

        self.split(k, line, line, c)

    def stage_4(self, k):
        def line(k):
            @pl.when(self.p.inner)
            def _():
                self.l_in(k).wait_recv()
                self.add(self.half(k), self.side(self.r1, k))
                self.l_mid(k).start()

        def c(k):
            self.q_x(k).wait_recv()
            self.add(self.q_own(k, False), self.q_in(k, 0))
            self.q_far(k).start()

        self.split(k, line, line, c)

    def stage_5(self, k):
        def line(k):
            @pl.when(self.p.inner)
            def _():
                self.l_mid(k).wait_recv()
                self.add(self.side(self.r2, k), self.half(k))
                self.l_out(k).start()
                self.l_leave(k, True)

        def c(k):
            self.q_far(k).wait_recv()
            total = self.q_own(k, False)[...] + self.q_in(k, 1)[...]
            self.r2[self.place(k)[0], self.part(k, False)] = total
            self.q_gather(k).start()

        self.split(k, line, line, c)

    def stage_6(self, k):
        def line(k):
            @pl.when(self.p.outer)
            def _():
                self.l_in(k).wait_recv()
                self.l_leave(k, False)

        def c(k):
            self.q_gather(k).wait_recv()
            self.q_leave(k)

        self.split(k, line, line, c)

    def close(self):
        rest = WAYS[:LAST_BIG].count("c") + WAYS[LAST_BIG:].count("c") // 2
        line = BUFFERS - rest
        peer = self.p.to_x

        def whole(ref, count, kind):
            span = ref.at[pl.ds(0, count)]
            return remote(span, span, self.send.at[kind], self.send.at[kind], peer)

        def parts(kind):
            span = self.r1.at[pl.ds(0, rest), pl.ds(0, CR)]
            return remote(span, span, self.send.at[kind], self.send.at[kind], peer)

        for k in range(K - SLOT_COUNT, K):
            self.c_core(k).wait_send()
        whole(self.ry, BUFFERS, 0).wait_send()
        whole(self.rx, BUFFERS, 1).wait_send()
        whole(self.r1, line, 2).wait_send()
        pl.when(self.p.inner)(lambda: whole(self.r1, line, 3).wait_send())
        whole(self.r1, line, 4).wait_send()
        whole(self.r1, line, 5).wait_recv()
        parts(6).wait_send()
        parts(7).wait_send()
        parts(8).wait_send()
        whole(self.r1, rest, 9).wait_send()
        whole(self.r1, rest, 10).wait_recv()
        pltpu.make_async_copy(self.r1, self.r2, self.send.at[11]).wait()

    def run(self, steps):
        stages = (self.stage_1, self.stage_2, self.stage_3, self.stage_4, self.stage_5, self.stage_6)
        for step in steps:
            stages[step // 100 - 1](step % 100)

    def run_at(self, index, table):
        for i, steps in enumerate(table):
            if steps:
                pl.when(index == i)(lambda steps=steps: self.run(steps))


def norm_parts(values):
    mean = jnp.mean(values, axis=-1, keepdims=True)
    centred = values - mean
    spread = jnp.mean(centred * centred, axis=-1, keepdims=True)
    scale = lax.rsqrt(spread + epsilon)
    return centred * scale, scale


def norm_back(hat, scale, gain, grad):
    lifted = grad * gain
    level = jnp.mean(lifted, axis=-1, keepdims=True)
    slope = jnp.mean(lifted * hat, axis=-1, keepdims=True)
    return scale * (lifted - level - hat * slope)


def three_parts(values):
    high = values.astype(BF).astype(F32)
    rest = values - high
    middle = rest.astype(BF).astype(F32)
    return high, middle, rest - middle


def layer_kernel(
    tok_ref, cot_ref, cnt_ref, fg_ref, fb_ref, ib_ref, ob_ref, sg_ref, sb_ref, eb_ref, rb_ref,
    wi_ref, wo_ref, we_ref, wr_ref,
    tot_ref, vs, lo_ref, gto_ref, gtr_ref,
    own, nbr, rc, ry, rx, r1, r2, vec,
    tokx, dyx, w1, wo, wr, qkv, kvr, rowb, kaug, qaug, att, mid, low2, turned, g_t, du_t, y_sum, h_sum,
    d_out, dp, dq_sum, dkv_own, dkv_far, dkv_send, dkv_recv, lo, gts, vr,
    csend, send, recv, lsem, xsend, xrecv, ksend, krecv, vsend, vrecv,
):
    p = Place()
    loads = [
        pltpu.make_async_copy(tok_ref.at[p.y, 0], tokx.at[pl.ds(0, PART)], lsem.at[0]),
        pltpu.make_async_copy(wi_ref, w1.at[:, pl.ds(0, 2304)], lsem.at[1]),
        pltpu.make_async_copy(cot_ref.at[p.y, 0], dyx.at[pl.ds(0, PART)], lsem.at[2]),
        pltpu.make_async_copy(wo_ref, wo, lsem.at[3]),
        pltpu.make_async_copy(wr_ref, wr, lsem.at[4]),
    ]
    for one in loads:
        one.start()
    enter(p)
    red = Reduce(p, (own, nbr, rc, ry, rx, r1, r2), tot_ref, csend, send, recv)

    def swap(index, src, dst, peer):
        return remote(src, dst, xsend.at[index], xrecv.at[index], peer)

    c_tok = [
        swap(8 * i, tok_ref.at[1 - p.y, 0, pl.ds(i * 128, 128)], tokx.at[pl.ds(PART + i * 128, 128)], p.to_y)
        for i in range(2)
    ]
    c_cot = swap(1, cot_ref.at[1 - p.y, 0], dyx.at[pl.ds(PART, PART)], p.to_y)
    c_row = swap(2, rowb.at[2], rowb.at[1], p.to_y)
    c_aug = swap(3, kaug.at[pl.ds(0, ROWS)], kaug.at[pl.ds(ROWS, ROWS)], p.to_core)
    pieces = ((0, PART), (PART, 128), (PART + 128, 128))
    c_kv = [
        swap(index, qkv.at[pl.ds(first, rows), pl.ds(768, 1536)], kvr.at[pl.ds(first, rows)], p.to_core)
        for index, (first, rows) in zip((4, 5, 9), pieces)
    ]

    lane = lax.broadcasted_iota(jnp.int32, (16, PART), 1)

    def bias_row(m):
        frame = lane // SLOTS
        kept = jnp.zeros_like(lane)
        for j in range(FRAME_DEV):
            kept = jnp.where(frame == j, cnt_ref[m, 0, j], kept)
        return jnp.where(lane - frame * SLOTS < kept, 0.0, LOW).astype(BF)

    rowb[2] = bias_row(1 - p.y)
    c_row.start()
    for one in c_tok:
        one.start()
    rowb[0] = bias_row(p.y)
    for row, ref in ((0, fg_ref), (1, fb_ref), (4, ob_ref), (5, sg_ref), (6, sb_ref), (7, rb_ref)):
        vec[row : row + 1] = ref[...].astype(F32).reshape(1, D)
    vec[2:4] = ib_ref[...].astype(F32)
    for f in range(4):
        vec[8 + f : 9 + f] = eb_ref[f * D : (f + 1) * D].astype(F32).reshape(1, D)
    pick = jnp.where(
        jnp.logical_and(
            lax.broadcasted_iota(jnp.int32, (16, 128), 0) == 0,
            lax.broadcasted_iota(jnp.int32, (16, 128), 1) == 0,
        ),
        1.0,
        0.0,
    ).astype(BF)
    kaug[pl.ds(0, PART)] = dot_tn(rowb[0], pick).astype(BF)
    lane_q = lax.broadcasted_iota(jnp.int32, (PART, 128), 1)
    lane_row = lax.broadcasted_iota(jnp.int32, (1, 128), 1)
    head_mask = [
        jnp.where((lane_row < 64) == (h == 0), 1.0, 0.0).astype(BF) for h in range(2)
    ]
    qaug[...] = jnp.where(lax.broadcasted_iota(jnp.int32, (ROWS, 128), 1) == 0, 1.0, 0.0)
    vs[...] = jnp.zeros_like(vs)

    def project(r):
        rows = pl.ds(*pieces[r])
        hat, _ = norm_parts(tokx[rows].astype(F32))
        low2[rows] = (hat * vec[0:1] + vec[1:2]).astype(BF)

        def column(j):
            col = pl.multiple_of(j * 256, 256)
            part = lax.rem(j, 3) * 256
            shift = jnp.where(
                j < 3, vec[2:3, at256(part)], jnp.where(j >= 6, vec[3:4, at256(part)], 0.0)
            )
            value = dot_nn(low2[rows], w1[:, pl.ds(col, 256)]) + shift
            qkv[rows, pl.ds(col, 256)] = (value * jnp.where(j < 3, 0.125, 1.0)).astype(BF)

        loop(3, 9, column)
        c_kv[r].start()
        loop(0, 3, column)

    loads[0].wait()
    loads[1].wait()
    project(0)
    c_row.wait_recv()
    kaug[pl.ds(PART, PART)] = dot_tn(rowb[1], pick).astype(BF)
    c_aug.start()
    c_tok[0].wait_recv()
    project(1)
    c_tok[1].wait_recv()
    c_cot.start()
    project(2)
    load_we = pltpu.make_async_copy(we_ref, w1, lsem.at[5])
    load_we.start()
    c_aug.wait_recv()
    for one in c_kv:
        one.wait_recv()

    def attend(group):
        cols = [pl.multiple_of(group * 256 + i * 128, 128) for i in range(2)]
        ones = jnp.ones((ROWS, 128), BF)
        first = jnp.where(lane_q == 0, 1.0, 0.0).astype(BF)
        k_here = [jnp.concatenate([qkv[:, at128(768 + c)], kaug[pl.ds(0, ROWS)]], axis=1) for c in cols]
        k_there = [jnp.concatenate([kvr[:, at128(c)], kaug[pl.ds(ROWS, ROWS)]], axis=1) for c in cols]
        v_here = [jnp.concatenate([qkv[:, at128(1536 + c)], ones], axis=1) for c in cols]
        v_there = [jnp.concatenate([kvr[:, at128(768 + c)], ones], axis=1) for c in cols]

        def scores(unit):
            i, block, h = unit // 4, unit // 2 % 2, unit % 2
            query = qkv[pl.ds(block * PART, PART), at128(cols[i])]
            lifted = jnp.concatenate([query * head_mask[h], first], axis=1)
            return dot_nt(lifted, k_here[i]), dot_nt(lifted, k_there[i])

        ready = scores(0)
        for unit in range(8):
            one, block, h = unit // 4, unit // 2 % 2, unit % 2
            rows = pl.ds(block * PART, PART)
            s_here, s_there = ready
            if unit < 7:
                ready = scores(unit + 1)
            top = jnp.maximum(
                jnp.max(s_here, axis=-1, keepdims=True), jnp.max(s_there, axis=-1, keepdims=True)
            )
            e_here = jnp.exp(s_here - top).astype(BF)
            e_there = jnp.exp(s_there - top).astype(BF)
            both = dot_nn(e_here, v_here[one]) + dot_nn(e_there, v_there[one])
            total = both[:, 128:]
            out = both[:, :128] / total
            parts = three_parts(top + jnp.log(total))
            base = 1 + 3 * (2 * (2 * group + one) + h)
            extra = qaug[rows] if h == 0 else extra
            for i in range(3):
                extra = jnp.where(lane_q == base + i, -parts[i], extra)
            if h == 0:
                held = out
            else:
                qaug[rows] = extra
                att[rows, at128(cols[one])] = jnp.where(lane_q < 64, held, out).astype(BF)

    loop(0, 3, attend)

    def turn(rows, block):
        flipped = block.T
        for quarter in range(4):
            seat = pl.multiple_of(p.seat(quarter) * CR, CR)
            turned[pl.ds(seat, CR), rows] = flipped[quarter * CR : (quarter + 1) * CR]

    loads[3].wait()

    def middle(i):
        rows = at256(i * PART)
        value = tokx[rows].astype(F32) + dot_nn(att[rows], wo[...]) + vec[4:5]
        mid[rows] = value
        hat, _ = norm_parts(value)
        block = (hat * vec[5:6] + vec[6:7]).astype(BF)
        low2[rows] = block
        turn(rows, block)

    loop(0, 2, middle)
    loads[2].wait()
    loads[4].wait()
    load_we.wait()
    c_cot.wait_recv()
    y_sum[...] = jnp.zeros_like(y_sum)
    h_sum[...] = jnp.zeros_like(h_sum)

    def feed(t):
        starts = []
        for side in range(2):
            cc = p.core if side == 0 else 1 - p.core
            for yy in range(2):
                starts.append((yy * 2 + cc) * 768 + t * 128)
        w_up = jnp.concatenate([w1[:, at128(s)] for s in starts], axis=1)
        shifts = vec[8:12, at128(t * 128)]
        zeroth = p.core == 0
        shift = jnp.concatenate(
            [
                jnp.where(zeroth, shifts[yy * 2 + s : yy * 2 + s + 1], shifts[yy * 2 + 1 - s : yy * 2 + 2 - s])
                for s in range(2)
                for yy in range(2)
            ],
            axis=1,
        )
        before = dot_nn(low2[...], w_up) + shift
        half = 0.5 + 0.5 * lax.erf(before * 0.7071067811865476)
        active = (before * half).astype(BF)
        slope = half + before * (jnp.exp(before * before * -0.5) * 0.3989422804014327)
        g_t[...] = active
        w_down = jnp.concatenate([wr[at128(s), :] for s in starts], axis=0)
        du_t[...] = (dot_nt(dyx[...], w_down) * slope).astype(BF)
        tall = dot_nn(g_t[...].T, dyx[...]).astype(BF)
        red.slot(2 * t)
        red.put_tall(2 * t, tall)
        red.c_core(2 * t).start()
        red.slot(2 * t + 1)
        for e in range(2):
            seats = [e + 2 * (p.core if cc == 0 else 1 - p.core) for cc in range(2)]
            right = jnp.concatenate([du_t[:, at128(s * 128)] for s in seats], axis=1)
            red.put_wide(2 * t + 1, e, dot_nn(turned[...], right).astype(BF))
        red.c_core(2 * t + 1).start()
        sums = jnp.sum(du_t[...].astype(F32), axis=0, keepdims=True)
        seat = [sums[:, i * 128 : (i + 1) * 128] for i in range(4)]
        vs[8:12, at128(t * 128)] = jnp.concatenate(
            [
                jnp.where(zeroth, seat[yy + 2 * cc], seat[yy + 2 - 2 * cc])
                for yy in range(2)
                for cc in range(2)
            ],
            axis=0,
        )
        red.run_at(t, FEED_STEPS[0])
        y_sum[...] += dot_nn(g_t[...], w_down)
        h_sum[...] += dot_nt(du_t[...], w_up)
        red.run_at(t, FEED_STEPS[1])

    loop(0, 6, feed)
    reload_wi = pltpu.make_async_copy(wi_ref, w1.at[:, pl.ds(0, 2304)], lsem.at[6])
    reload_wi.start()

    def second(i):
        rows = at256(i * PART)
        value = mid[rows]
        lo[rows] = (value + y_sum[rows] + vec[7:8]).astype(BF)
        hat, scale = norm_parts(value)
        grad = h_sum[rows]
        upstream = dyx[rows].astype(F32)
        vs[5:6] += jnp.sum(grad * hat, axis=0, keepdims=True)
        vs[6:7] += jnp.sum(grad, axis=0, keepdims=True)
        vs[7:8] += jnp.sum(upstream, axis=0, keepdims=True)
        total = upstream + norm_back(hat, scale, vec[5:6], grad)
        mid[rows] = total
        block = total.astype(BF)
        low2[rows] = block
        vs[4:5] += jnp.sum(block.astype(F32), axis=0, keepdims=True)
        d_out[rows] = dot_nt(block, wo[...]).astype(BF)
        turn(rows, att[rows])
        red.run_at(i, NORM_STEPS)

    loop(0, 2, second)
    c_lo = swap(6, lo.at[pl.ds(PART, PART)], lo_ref.at[p.y], p.to_y)
    keep_lo = pltpu.make_async_copy(lo.at[pl.ds(0, PART)], lo_ref.at[p.y], lsem.at[7])
    keep_lo.start()

    red.slot(12)
    red.slot(13)
    for k, side, first in ((12, 0, 0), (12, 1, 256), (13, 0, 512)):
        red.put_wide(k, side, dot_nn(turned[...], low2[:, first : first + 256]).astype(BF))
    red.c_core(12).start()
    red.run(OUT_STEPS)

    def turn_first(i):
        rows = at256(i * PART)
        hat, _ = norm_parts(tokx[rows].astype(F32))
        turn(rows, (hat * vec[0:1] + vec[1:2]).astype(BF))

    loop(0, 2, turn_first)

    def in_grad(first):
        return dot_nn(turned[...], dp[:, at256(first)]).astype(BF)

    def put_side(at):
        k, side = 13 + at // 2, lax.rem(at, 2)
        pl.when(side == 0)(lambda: red.slot(k))
        red.put_wide(k, side, in_grad(lax.rem(at - 1, 3) * 768 + (at - 1) // 3 * 256))
        pl.when(side == 1)(lambda: red.c_core(k).start())

    def put_last(k):
        red.slot(k)
        red.put_small(k, in_grad((k + 1) % 3 * 768 + (k - 11) // 3 * 256))
        red.c_core(k).start()

    def in_grads(pair):
        pl.when(pair == 2)(lambda: loop(1, 4, put_side))

        @pl.when(pair == 4)
        def _():
            loop(4, 6, put_side)
            put_last(16)

    def c_dkv(pair):
        return remote(
            dkv_send.at[lax.rem(pair, 2)], dkv_recv.at[pair], ksend.at[pair], krecv.at[pair], p.to_core
        )

    def settle(pair):
        c_dkv(pair).wait_recv()
        slot = lax.rem(pair, 2)
        for i in range(2):
            total = dkv_own[slot, i] + dkv_recv[pair, i].astype(F32)
            dp[:, at128(768 * (i + 1) + pair * 128)] = total.astype(BF)

    lane_k = lax.broadcasted_iota(jnp.int32, (ROWS, 128), 1)

    def attend_back(pair):
        col = pl.multiple_of(pair * 128, 128)
        slot = lax.rem(pair, 2)
        query = qkv[:, at128(col)]
        extra_q = qaug[...].astype(BF)
        grads = d_out[:, at128(col)]
        outs = att[:, at128(col)].astype(F32)
        three = jnp.where(lane_k < 3, 1.0, 0.0).astype(BF)

        @pl.when(pair >= 1)
        def _():
            settle(pair - 1)

        def products(unit):
            h, side = unit // 2, unit % 2
            q_h = query * head_mask[h]
            g_h = grads * head_mask[h]
            parts = three_parts(jnp.sum(g_h.astype(F32) * outs, axis=-1, keepdims=True))
            extra_g = jnp.zeros((ROWS, 128), F32)
            for i in range(3):
                extra_g = jnp.where(lane_k == i, -parts[i], extra_g)
            q_wide = jnp.concatenate([q_h, extra_q], axis=1)
            g_wide = jnp.concatenate([g_h, extra_g.astype(BF)], axis=1)
            base = 1 + 3 * (2 * pair + h)
            mark = jnp.where(
                jnp.logical_and(lane_k >= base, lane_k < base + 3), 1.0, 0.0
            ).astype(BF)
            if side == 0:
                key, value = qkv[:, at128(768 + col)], qkv[:, at128(1536 + col)]
            else:
                key, value = kvr[:, at128(col)], kvr[:, at128(768 + col)]
            k_wide = jnp.concatenate([key, kaug[pl.ds(side * ROWS, ROWS)] + mark], axis=1)
            v_wide = jnp.concatenate([value, three], axis=1)
            return dot_nt(k_wide, q_wide), dot_nt(v_wide, g_wide), q_h, g_h, (key * head_mask[h]).T

        ready = products(0)
        for unit in range(4):
            h, side = unit // 2, unit % 2
            score, slope, q_h, g_h, key_t = ready
            if unit < 3 and unit not in CUTS:
                ready = products(unit + 1)
            weight = jnp.exp(score)
            slope = (weight * slope).astype(BF)
            add_k, add_v = dot_nn(slope, q_h), dot_nn(weight.astype(BF), g_h)
            add_q = dot_nn(key_t, slope)
            if unit == 0:
                dq_sum[...] = add_q
            else:
                dq_sum[...] += add_q
            sums = dkv_own.at[slot] if side == 0 else dkv_far
            if h == 0:
                sums[0] = add_k
                sums[1] = add_v
            else:
                sums[0] += add_k
                sums[1] += add_v
            if unit in CUTS:
                red.run_at(pair, ATTEND_STEPS[CUTS.index(unit)])
                if unit < 3:
                    ready = products(unit + 1)
        dp[:, at128(col)] = (dq_sum[...].T.astype(BF).astype(F32) * 0.125).astype(BF)

        @pl.when(pair >= 2)
        def _():
            c_dkv(pair - 2).wait_send()

        dkv_send[slot] = dkv_far[...].astype(BF)
        c_dkv(pair).start()
        in_grads(pair)
        pl.when(pair == 1)(lambda: c_lo.start())

    loop(0, 6, attend_back)
    settle(5)
    c_dkv(4).wait_send()
    c_dkv(5).wait_send()

    for k in range(17, 20):
        put_last(k)
    red.run(PROJECT_STEPS)
    vs[2:3] = jnp.sum(dp[:, 0:768].astype(F32), axis=0, keepdims=True)
    vs[3:4] = jnp.sum(dp[:, 1536:2304].astype(F32), axis=0, keepdims=True)
    reload_wi.wait()

    def first_back(i):
        rows = at256(i * PART)
        grad = dot_nt(dp[rows], w1[:, pl.ds(0, 2304)])
        hat, scale = norm_parts(tokx[rows].astype(F32))
        vs[0:1] += jnp.sum(grad * hat, axis=0, keepdims=True)
        vs[1:2] += jnp.sum(grad, axis=0, keepdims=True)
        y_sum[rows] = mid[rows] + norm_back(hat, scale, vec[0:1], grad)
        red.run_at(i, LAST_STEPS)

    loop(0, 2, first_back)
    gts[...] = y_sum[pl.ds(PART, PART)].astype(BF)
    c_gt = swap(7, gts, gtr_ref, p.to_y)
    keep_gt = pltpu.make_async_copy(y_sum.at[pl.ds(0, PART)], gto_ref, lsem.at[8])
    c_gt.start()
    keep_gt.start()

    def c_vec(stage, peer):
        return remote(vr.at[2 * stage], vr.at[2 * stage + 1], vsend.at[stage], vrecv.at[stage], peer)

    def vec_pair(stage, peer):
        vr[2 * stage] = vs[...]
        c_vec(stage, peer).start()

    def vec_take(stage, peer):
        c_vec(stage, peer).wait()
        vs[...] += vr[2 * stage + 1]

    def vec_0():
        vec_take(0, p.to_core)
        vec_pair(1, p.to_y)

    def vec_1():
        vec_take(1, p.to_y)
        vec_pair(2, p.to_x)

    def vec_2():
        vec_take(2, p.to_x)

        @pl.when(p.outer)
        def _():
            vec_pair(3, p.to_mate)

    def vec_3():
        @pl.when(p.inner)
        def _():
            c_vec(3, p.to_mate).wait_recv()
            vs[...] += vr[7]
            vec_pair(4, p.to_far)

    def vec_4():
        @pl.when(p.inner)
        def _():
            vec_take(4, p.to_far)
            vec_pair(3, p.to_mate)

    def vec_5():
        @pl.when(p.outer)
        def _():
            c_vec(3, p.to_mate).wait_recv()
            vs[...] = vr[7]

        c_vec(3, p.to_mate).wait_send()

    vec_pair(0, p.to_core)
    vec_steps = (vec_0, vec_1, vec_2, vec_3, vec_4, vec_5)
    for step in DRAIN_STEPS:
        if step < 100:
            vec_steps[step]()
        else:
            red.run((step,))
    red.close()
    for one in c_tok + c_kv:
        one.wait_send()
    c_row.wait_send()
    c_cot.wait_send()
    c_aug.wait_send()
    c_lo.wait()
    c_gt.wait()
    keep_lo.wait()
    keep_gt.wait()


def finish_kernel(
    tot_ref, vs, lo_in, gto, gtr_ref,
    lo_out, gt, g0, g1, wi_out, g2, wo_out, g4, g5, g6, we_out, g8, wr_out, g7,
    tot, gtr, gt_s, lo_s, wi, wo, we, wr, in_sem, out_sem,
):
    y = lax.axis_index("frame") // 2
    frame = lax.axis_index("frame")
    spans = [(2 * t, 2) for t in range(6)] + [(12, 2), (14, 2), (16, 2)]
    loads = [
        pltpu.make_async_copy(tot_ref.at[pl.ds(k, n)], tot.at[pl.ds(k, n)], in_sem.at[i])
        for i, (k, n) in enumerate(spans)
    ]
    loads += [
        pltpu.make_async_copy(gtr_ref, gtr, in_sem.at[9]),
        pltpu.make_async_copy(gto, gt_s.at[0], in_sem.at[10]),
        pltpu.make_async_copy(lo_in, lo_s, in_sem.at[11]),
    ]
    for one in loads:
        one.start()
    outs = []

    def leave(src, dst):
        one = pltpu.make_async_copy(src, dst, out_sem.at[len(outs)])
        one.start()
        outs.append(one)

    for t in range(6):
        loads[t].wait()
        rows = pl.ds(t * 128, 128)
        for i in range(6):
            block = slice(i % 3 * 128, (i % 3 + 1) * 128)
            wr[rows, i * 128 : (i + 1) * 128] = tot[2 * t, i // 3, block].astype(F32)
        leave(wr.at[rows], wr_out.at[rows])
        for j in range(4):
            cols = pl.ds(j * 768 + t * 128, 128)
            block = slice(j % 2 * CR, (j % 2 + 1) * CR)
            we[:, cols] = tot[2 * t + 1, j // 2, block].astype(F32)
    leave(we, we_out)
    for n, col in enumerate(COLUMNS):
        if n % 8 == 0:
            loads[6 + n // 8].wait()
        block = slice(n % 2 * CR, (n % 2 + 1) * CR)
        value = tot[12 + n // 4, n % 4 // 2, block].astype(F32)
        if n < 6:
            wo[:, col * 128 : (col + 1) * 128] = value
        else:
            wi[:, col * 128 : (col + 1) * 128] = value
        if n == 5:
            leave(wo, wo_out)
    leave(wi, wi_out)
    loads[9].wait()
    gt_s[1] = gtr[...].astype(F32)
    leave(gt_s.at[1], gt.at[1 - y, 0])
    loads[10].wait()
    leave(gt_s.at[0], gt.at[y, 0])
    loads[11].wait()
    leave(lo_s.at[0], lo_out.at[0, 0])
    leave(lo_s.at[1], lo_out.at[1, 0])
    mine = vs[0:8, 0:CR]
    row = vs[8:9]
    for f in range(1, 4):
        mine = jnp.where(frame == f, vs[0:8, f * CR : (f + 1) * CR], mine)
        row = jnp.where(frame == f, vs[8 + f : 9 + f], row)
    g0[...] = mine[0]
    g1[...] = mine[1]
    g2[...] = mine[2:4]
    g4[...] = mine[4]
    g5[...] = mine[5]
    g6[...] = mine[6]
    g7[...] = mine[7]
    g8[...] = row[0]
    for one in outs:
        one.wait()


def local_slice(
    tokens,
    counts,
    first_gain,
    first_bias,
    input_weight,
    input_bias,
    output_weight,
    output_bias,
    second_gain,
    second_bias,
    expand_weight,
    expand_bias,
    reduce_weight,
    reduce_bias,
    cotangent,
):
    anywhere = pl.BlockSpec(memory_space=pl.ANY)
    vmem = pl.BlockSpec(memory_space=pltpu.VMEM)
    smem = pl.BlockSpec(memory_space=pltpu.SMEM)
    shape = jax.ShapeDtypeStruct
    dma = pltpu.SemaphoreType.DMA
    tot, vs, lo, gto, gtr = pl.pallas_call(
        layer_kernel,
        out_shape=(
            shape((BUFFERS, 2, HR, 128), BF),
            shape((16, D), F32),
            shape((2, PART, D), BF),
            shape((PART, D), F32),
            shape((PART, D), BF),
        ),
        in_specs=[anywhere, anywhere, smem] + [vmem] * 8 + [anywhere] * 4,
        out_specs=(anywhere, vmem, anywhere, anywhere, anywhere),
        scratch_shapes=[
            pltpu.VMEM((BUFFERS, 2, 2, HR, 128), BF),
            pltpu.VMEM((SLOT_COUNT, 2, 2, HR, 128), BF),
            pltpu.VMEM((BUFFERS, 2, 2, HR, 128), BF),
            pltpu.VMEM((BUFFERS, 2, HR, 128), BF),
            pltpu.VMEM((BUFFERS, HR, 128), BF),
            pltpu.VMEM((BUFFERS, HR, 128), BF),
            pltpu.VMEM((BUFFERS, HR, 128), BF),
            pltpu.VMEM((12, D), F32),
            pltpu.VMEM((ROWS, D), BF),
            pltpu.VMEM((ROWS, D), BF),
            pltpu.VMEM((D, FF), BF),
            pltpu.VMEM((D, D), BF),
            pltpu.VMEM((FF, D), BF),
            pltpu.VMEM((ROWS, 3 * D), BF),
            pltpu.VMEM((ROWS, 2 * D), BF),
            pltpu.VMEM((3, 16, PART), BF),
            pltpu.VMEM((2 * ROWS, 128), BF),
            pltpu.VMEM((ROWS, 128), F32),
            pltpu.VMEM((ROWS, D), BF),
            pltpu.VMEM((ROWS, D), F32),
            pltpu.VMEM((ROWS, D), BF),
            pltpu.VMEM((D, ROWS), BF),
            pltpu.VMEM((ROWS, ROWS), BF),
            pltpu.VMEM((ROWS, ROWS), BF),
            pltpu.VMEM((ROWS, D), F32),
            pltpu.VMEM((ROWS, D), F32),
            pltpu.VMEM((ROWS, D), BF),
            pltpu.VMEM((ROWS, 3 * D), BF),
            pltpu.VMEM((128, ROWS), F32),
            pltpu.VMEM((2, 2, ROWS, 128), F32),
            pltpu.VMEM((2, ROWS, 128), F32),
            pltpu.VMEM((2, 2, ROWS, 128), BF),
            pltpu.VMEM((6, 2, ROWS, 128), BF),
            pltpu.VMEM((ROWS, D), BF),
            pltpu.VMEM((PART, D), BF),
            pltpu.VMEM((10, 16, D), F32),
            dma((SLOT_COUNT,)),
            dma((12,)),
            dma((6, K)),
            dma((9,)),
            dma((10,)),
            dma((10,)),
            dma((6,)),
            dma((6,)),
            dma((5,)),
            dma((5,)),
        ],
        compiler_params=pltpu.CompilerParams(
            collective_id=0, has_side_effects=True, vmem_limit_bytes=62 << 20
        ),
    )(
        tokens,
        cotangent,
        counts,
        first_gain,
        first_bias,
        input_bias,
        output_bias,
        second_gain,
        second_bias,
        expand_bias,
        reduce_bias,
        input_weight,
        output_weight,
        expand_weight,
        reduce_weight,
    )
    return pl.pallas_call(
        finish_kernel,
        out_shape=(
            shape((MICRO, 1, PART, D), BF),
            shape((MICRO, 1, PART, D), F32),
            shape((CR,), F32),
            shape((CR,), F32),
            shape((CR, 3 * D), F32),
            shape((2, CR), F32),
            shape((CR, D), F32),
            shape((CR,), F32),
            shape((CR,), F32),
            shape((CR,), F32),
            shape((CR, FF), F32),
            shape((D,), F32),
            shape((D, D), F32),
            shape((CR,), F32),
        ),
        in_specs=[anywhere, vmem, anywhere, anywhere, anywhere],
        out_specs=tuple(anywhere if i in (0, 1, 4, 6, 10, 12) else vmem for i in range(14)),
        scratch_shapes=[
            pltpu.VMEM((BUFFERS, 2, HR, 128), BF),
            pltpu.VMEM((PART, D), BF),
            pltpu.VMEM((2, PART, D), F32),
            pltpu.VMEM((2, PART, D), BF),
            pltpu.VMEM((CR, 3 * D), F32),
            pltpu.VMEM((CR, D), F32),
            pltpu.VMEM((CR, FF), F32),
            pltpu.VMEM((D, D), F32),
            dma((12,)),
            dma((16,)),
        ],
        compiler_params=pltpu.CompilerParams(vmem_limit_bytes=62 << 20),
    )(tot, vs, lo, gto, gtr)


def solution(mesh):
    fits = mesh.shape["clip"] == 8 and mesh.shape["frame"] == 4
    return jax.shard_map(
        local_slice if fits else local,
        mesh=mesh,
        in_specs=(
            P(None, "clip", "frame", None),
            P(None, "clip", "frame"),
            P(),
            P(),
            P(),
            P(),
            P(),
            P(),
            P(),
            P(),
            P(),
            P(),
            P(),
            P(),
            P(None, "clip", "frame", None),
        ),
        out_specs=(
            P(None, "clip", "frame", None),
            P(None, "clip", "frame", None),
            P("frame"),
            P("frame"),
            P("frame", None),
            P(None, "frame"),
            P("frame", None),
            P("frame"),
            P("frame"),
            P("frame"),
            P("frame", None),
            P("frame"),
            P("frame", None),
            P("frame"),
        ),
        check_vma=False,
    )
```
